512 devices in a mesh: seq: 32 (over z_hi, y), vocab: 16 (over x, z_lo, core).
Axes of the slice: x: 4, y: 8, z: 8 (z_hi: 4, z_lo: 2; z = z_hi * 2 + z_lo), core: 2. Of those that a mesh axis runs over, the one named last changes fastest.
Arguments:
- hidden: bfloat16 [2048, 5120], P('seq'), may hold values from -6 to 6
- norm_gain: float32 [5120], replicated, may hold values from 0.25 to 1.75
- head_weight: bfloat16 [4096, 5120], P('vocab'), may hold values from -1 to 1
- targets: int32 [2048], P('seq'), may hold values from 0 to 4095
- out_proj: bfloat16 [12288, 5120], P('seq', 'vocab'), may hold values from -0.078125 to 0.078125
- query: bfloat16 [2048, 12288], P(('seq', 'vocab')), may hold values from -6 to 6
- saved_key_value: bfloat16 [2, 2048, 1024], P(None, ('seq', 'vocab')), may hold values from -6 to 6
- offset: int32 [1], replicated, may hold values from 1 to 2047
Outputs:
- token_loss: float32 [2048], P('seq')
- hidden_grad: bfloat16 [2048, 5120], P('seq', 'vocab')
- query_grad: bfloat16 [2048, 12288], P(('seq', 'vocab'))
- key_value_gradient: bfloat16 [2, 2048, 1024], P(None, ('seq', 'vocab'))
The draws below stay inside these ranges and needn't reach their ends.
All inputs are finite; a program needn't handle non-finite values.
Results may differ from the reference program's by a relative error of at most 0.039.
Values may be sent and summed in bfloat16 or wider, within the bound.
A program may use at most 64 MiB of HBM per device.

```python
import math
import jax
import jax.numpy as jnp
import numpy as np
from jax import lax

D = 5120
QUERY_HEAD_COUNT = 96
KEY_VALUE_HEADS = 8
HEAD_SIZE = 128
WINDOW_TOKENS = 2048
VOCAB = 4096
N_VOCAB = 16


def draw_hidden(key, part):
    own_share = jax.random.fold_in(key, 11)
    base_offset = jnp.clip(jax.random.normal(own_share, (WINDOW_TOKENS, D), jnp.float32), -6.0, 6.0)
    return base_offset.astype(jnp.bfloat16)


def draw_head_weight(key, part):
    own_share = jax.random.fold_in(key, 12)
    spread = 1.0 / math.sqrt(D // 9)
    base_offset = jnp.clip(jax.random.normal(own_share, (VOCAB, D), jnp.float32), -6.0, 6.0) * spread
    return jnp.clip(base_offset, -1.0, 1.0).astype(jnp.bfloat16)


def draw_query(key, part):
    own_share = jax.random.fold_in(key, 13)
    base_offset = jnp.clip(jax.random.normal(own_share, (WINDOW_TOKENS, QUERY_HEAD_COUNT * HEAD_SIZE), jnp.float32), -6.0, 6.0)
    return base_offset.astype(jnp.bfloat16)


def draw_saved_key_value(key, part):
    own_share = jax.random.fold_in(key, 14)
    base_offset = jnp.clip(jax.random.normal(own_share, (2, WINDOW_TOKENS, KEY_VALUE_HEADS * HEAD_SIZE), jnp.float32), -6.0, 6.0)
    return base_offset.astype(jnp.bfloat16)


def touch_ends(values, own_key, least, largest):
    spot = [jax.random.randint(jax.random.fold_in(own_key, axis), (), 0, length) for axis, length in enumerate(values.shape)]
    longest = values.shape.index(max(values.shape))
    beside = spot[:longest] + [(spot[longest] + 1) % values.shape[longest]] + spot[longest + 1:]
    return values.at[tuple(spot)].set(least).at[tuple(beside)].set(largest)


def block_levels(rng, dims, cuts, smallest, high):
    factor_of, own = 1.0, jax.random.fold_in(rng, 6)
    for position, blocks in cuts:
        steps = jnp.exp(jax.random.uniform(jax.random.fold_in(own, position), (blocks,), jnp.float32, smallest / len(cuts), high / len(cuts)))
        factor_of = factor_of * jnp.repeat(steps, dims[position] // blocks).reshape([-1 if axis == position else 1 for axis in range(len(dims))])
    return factor_of


def cumulative_ranks(number_of, skew):
    loads = [(1 << 20) // math.isqrt(rank ** skew) + 1 for rank in range(1, number_of + 1)]
    scale = 1 + sum(loads) // (1 << 30)
    return np.cumsum(np.array([max(1, weight // scale) for weight in loads]))


def skewed_ids(stream_key, extent, number_of, slope):
    listing = cumulative_ranks(number_of, slope)
    ticket = jax.random.randint(jax.random.fold_in(stream_key, 1), extent, 0, int(listing[number_of - 1]))
    rank = jnp.searchsorted(jnp.asarray(listing, jnp.int32), ticket, side="right")
    return jax.random.permutation(jax.random.fold_in(stream_key, 2), number_of)[rank].astype(jnp.int32)


def bell_draw(stream_key, extent, deviation, limit, cuts=(), kind=jnp.bfloat16):
    drawn = jax.random.normal(stream_key, extent, jnp.float32) * deviation
    if len(cuts) > 0:
        drawn = block_levels(stream_key, extent, cuts, -0.22, 0.18) * drawn
    return jnp.clip(drawn, min=-limit, max=limit).astype(kind)


def setup_inputs(seed: int = 0) -> dict:
    arg_keys = jax.random.split(jax.random.key(seed), 9)
    return {
        "hidden": draw_hidden(jax.random.fold_in(arg_keys[8], 71), 0),
        "norm_gain": jnp.clip(1.0 + 0.15 * jax.random.normal(arg_keys[1], (D,), jnp.float32), 0.25, 1.75),
        "head_weight": draw_head_weight(jax.random.fold_in(arg_keys[8], 71), 0),
        "targets": touch_ends(skewed_ids(arg_keys[3], (WINDOW_TOKENS,), VOCAB, 2), jax.random.fold_in(arg_keys[3], 3), 0, VOCAB - 1).astype(jnp.int32),
        "out_proj": bell_draw(arg_keys[4], (QUERY_HEAD_COUNT * HEAD_SIZE, D), D ** -0.5, 0.078125, ((0, 32), (1, 16))),
        "query": draw_query(jax.random.fold_in(arg_keys[8], 71), 0),
        "saved_key_value": draw_saved_key_value(jax.random.fold_in(arg_keys[8], 71), 0),
        "offset": jax.random.randint(arg_keys[7], (1,), 1, WINDOW_TOKENS).astype(jnp.int32),
    }


epsilon = 1e-05
loss_scaling = 32.0
masked_score = -1e+30

def head_backward(q_rows, key_rows, value_rows, out_grad, q_position, k_position, doc_start):
    score_scale = q_rows.shape[-1] ** (-0.5)
    scores = lax.dot_general(q_rows, key_rows, (((1,), (1,)), ((), ())), preferred_element_type=jnp.float32) * score_scale
    visible = (k_position[None, :] <= q_position[:, None]) & ((k_position[None, :] >= doc_start) | (q_position[:, None] < doc_start))
    scores = jnp.where(visible, scores, masked_score)
    peak_score = lax.optimization_barrier(jnp.max(scores, axis=-1, keepdims=True))
    raised = jnp.exp(scores - peak_score)
    probs = raised / lax.optimization_barrier(jnp.sum(raised, axis=-1, keepdims=True))
    probs_low = probs.astype(jnp.bfloat16)
    attended = jnp.dot(probs_low, value_rows, preferred_element_type=jnp.float32)
    row_delta = lax.optimization_barrier(jnp.sum(out_grad.astype(jnp.float32) * attended, axis=-1, keepdims=True))
    prob_grad = lax.dot_general(out_grad, value_rows, (((1,), (1,)), ((), ())), preferred_element_type=jnp.float32)
    score_grad = (probs * (prob_grad - row_delta)).astype(jnp.bfloat16)
    query_part = (jnp.dot(score_grad, key_rows, preferred_element_type=jnp.float32) * score_scale).astype(jnp.bfloat16)
    key_part = lax.dot_general(score_grad, q_rows, (((0,), (0,)), ((), ())), preferred_element_type=jnp.float32) * score_scale
    value_part = lax.dot_general(probs_low, out_grad, (((0,), (0,)), ((), ())), preferred_element_type=jnp.float32)
    return (query_part, key_part, value_part)

def reference(hidden, norm_gain, head_weight, targets, out_proj, query, saved_key_value, offset):
    wide_hidden = hidden.astype(jnp.float32)
    inv_rms = lax.rsqrt(lax.optimization_barrier(jnp.mean(wide_hidden * wide_hidden, axis=-1, keepdims=True)) + epsilon)
    normed = (wide_hidden * inv_rms * norm_gain).astype(jnp.bfloat16)
    logits = lax.dot_general(normed, head_weight, (((1,), (1,)), ((), ())), preferred_element_type=jnp.float32)
    row_peak = lax.optimization_barrier(jnp.max(logits, axis=-1, keepdims=True))
    raised = jnp.exp(logits - row_peak)
    row_total = lax.optimization_barrier(jnp.sum(raised, axis=-1, keepdims=True))
    columns = jnp.arange(VOCAB, dtype=jnp.int32)
    target_hit = targets[:, None] == columns[None, :]
    target_logit = lax.optimization_barrier(jnp.sum(jnp.where(target_hit, logits, jnp.float32(0.0)), axis=-1))
    token_loss = jnp.log(row_total[:, 0]) + row_peak[:, 0] - target_logit
    logit_grad = (loss_scaling * (raised / row_total - target_hit.astype(jnp.float32))).astype(jnp.bfloat16)
    normed_grad = jnp.dot(logit_grad, head_weight, preferred_element_type=jnp.float32)
    gain_grad = normed_grad * norm_gain
    inner = lax.optimization_barrier(jnp.sum(wide_hidden * gain_grad, axis=-1, keepdims=True))
    hidden_grad = (inv_rms * gain_grad - wide_hidden * inv_rms ** 3 * inner / D).astype(jnp.bfloat16)
    width = D // N_VOCAB

    def add_block(total, block):
        rows_part = lax.dynamic_slice_in_dim(hidden_grad, block * width, width, 1)
        proj_part = lax.dynamic_slice_in_dim(out_proj, block * width, width, 1)
        partial_sum = lax.dot_general(rows_part, proj_part, (((1,), (1,)), ((), ())), preferred_element_type=jnp.float32)
        rounded = lax.optimization_barrier(partial_sum.astype(jnp.bfloat16)).astype(jnp.float32)
        return (total + rounded, None)
    summed, ignored = lax.scan(add_block, jnp.zeros((WINDOW_TOKENS, QUERY_HEAD_COUNT * HEAD_SIZE), jnp.float32), jnp.arange(N_VOCAB, dtype=jnp.int32))
    head_out_grad = summed.astype(jnp.bfloat16)
    q_heads = query.reshape(WINDOW_TOKENS, QUERY_HEAD_COUNT, HEAD_SIZE).transpose(1, 0, 2)
    grad_heads = head_out_grad.reshape(WINDOW_TOKENS, QUERY_HEAD_COUNT, HEAD_SIZE).transpose(1, 0, 2)
    paired_heads = saved_key_value.reshape(2, WINDOW_TOKENS, KEY_VALUE_HEADS, HEAD_SIZE).transpose(2, 0, 1, 3)
    positions = jnp.arange(WINDOW_TOKENS, dtype=jnp.int32)
    doc_start = offset[0]
    group_index = QUERY_HEAD_COUNT // KEY_VALUE_HEADS

    def one_head(carry, inputs):
        q_rows, out_grad, head = inputs
        pair = paired_heads[head // group_index]
        parts = head_backward(q_rows, pair[0], pair[1], out_grad, positions, positions, doc_start)
        return (carry, parts)
    final_carry, stacked = lax.scan(one_head, jnp.zeros((), jnp.int32), (q_heads, grad_heads, jnp.arange(QUERY_HEAD_COUNT, dtype=jnp.int32)))
    query_parts, key_pieces_list, value_pieces_list = stacked
    query_grad = query_parts.transpose(1, 0, 2).reshape(WINDOW_TOKENS, QUERY_HEAD_COUNT * HEAD_SIZE)
    key_total = key_pieces_list.reshape(KEY_VALUE_HEADS, group_index, WINDOW_TOKENS, HEAD_SIZE).sum(axis=1)
    value_total = value_pieces_list.reshape(KEY_VALUE_HEADS, group_index, WINDOW_TOKENS, HEAD_SIZE).sum(axis=1)
    key_value_gradient = jnp.stack([key_total, value_total]).transpose(0, 2, 1, 3).reshape(2, WINDOW_TOKENS, KEY_VALUE_HEADS * HEAD_SIZE).astype(jnp.bfloat16)
    return (token_loss, hidden_grad, query_grad, key_value_gradient)
```

```python
import jax
import jax.numpy as jnp
from jax import lax
from jax.experimental import pallas as pl
from jax.experimental.pallas import tpu as pltpu
from jax.sharding import PartitionSpec as P

D = 5120
HEAD = 128
SEQ = 32
VOC = 16
TOK = 64
GROUP_HEADS = 3
ROWS = 128
STACK = GROUP_HEADS * ROWS
KEYS = 2048
EPS = 1e-05
LOSS_SCALE = 32.0
MASKED = -1e30
SCALE = HEAD ** (-0.5)
MESH = pl.DeviceIdType.MESH
F32 = jnp.float32
BF16 = jnp.bfloat16


def remote(src, dst, send_sem, recv_sem, **device):
    return pltpu.make_async_remote_copy(
        src_ref=src,
        dst_ref=dst,
        send_sem=send_sem,
        recv_sem=recv_sem,
        device_id=device,
        device_id_type=MESH,
    )


def low_rows(shape):
    return lax.broadcasted_iota(jnp.int32, shape, len(shape) - 2) < 4


def turn(x):
    return pltpu.roll(x, 4, len(x.shape) - 2)


def first_halves(a, b):
    return jnp.where(low_rows(a.shape), a, turn(b))


def second_halves(a, b):
    return jnp.where(low_rows(a.shape), turn(a), b)


def dot_nt(a, b):
    return lax.dot_general(a, b, (((1,), (1,)), ((), ())), preferred_element_type=F32)


def dot_tn(a, b):
    return lax.dot_general(a, b, (((0,), (0,)), ((), ())), preferred_element_type=F32)


def body(
    hidden, gain, weight, targets, out_proj, query, key_value, offset,
    loss_out, hidden_out, query_out, kv_out,
    logits_t, stat_send, stat_recv, part_send, part_recv, gain_chunk, hidden_chunk, grad_pad,
    slice_recv, slice_tiles, blocks, acts, proj_pad, proj_half, proj,
    query_wide, query_send, query_recv, query_rows, kv_send, kv_recv, kv,
    scores, probs_low, prob_grad, score_grad, og,
    dq_send, dq_recv, dkv_send, dkv_recv, fold_send, fold_recv,
    stat_s, stat_r, part_s, part_r, slice_s, slice_r, z_s, z_r, ring_s, ring_r,
    half_s, half_r, proj_s, proj_r, pfwd_s, pfwd_r, q_s, q_r, kv1_s, kv1_r, kv2_s, kv2_r,
    kfwd_s, kfwd_r, dq_s, dq_r, dkv_s, dkv_r, fold_s, fold_r,
):
    s = lax.axis_index("seq")
    v = lax.axis_index("vocab")
    h, y = s // 8, lax.rem(s, 8)
    slot = y * 4 + h
    chip, core = v // 2, lax.rem(v, 2)
    mate = v + 1 - 2 * core

    barrier = pltpu.get_barrier_semaphore()

    @pl.loop(1, VOC)
    def _(d):
        pl.semaphore_signal(
            barrier, inc=1, device_id={"vocab": lax.rem(v + d, VOC)}, device_id_type=MESH
        )

    @pl.loop(1, SEQ)
    def _(d):
        pl.semaphore_signal(
            barrier, inc=1, device_id={"seq": lax.rem(s + d, SEQ)}, device_id_type=MESH
        )

    def square(j, acc):
        x = hidden[:, pl.ds(pl.multiple_of(j * 512, 512), 512)].astype(F32)
        x = x * x
        return acc + (x[:, :128] + x[:, 128:256]) + (x[:, 256:384] + x[:, 384:])

    squares = lax.fori_loop(0, 10, square, jnp.zeros((TOK, 128), F32))
    inv_rms = lax.rsqrt(jnp.sum(squares, axis=1, keepdims=True) / D + EPS)

    def logit_step(j, acc):
        cols = pl.ds(pl.multiple_of(j * 512, 512), 512)
        normed = (hidden[:, cols].astype(F32) * inv_rms * gain[:, cols]).astype(BF16)
        return acc + dot_nt(weight[:, cols], normed)

    logits = lax.fori_loop(0, 10, logit_step, jnp.zeros((256, TOK), F32))
    logits_t[...] = logits
    hit = (v * 256 + lax.broadcasted_iota(jnp.int32, (256, TOK), 0)) == targets[...]
    peak = jnp.max(logits, axis=0, keepdims=True)
    raised = jnp.exp(logits - peak)
    stat_send[...] = jnp.zeros((8, 128), F32)
    stat_send[0:1, 0:TOK] = peak
    stat_send[1:2, 0:TOK] = jnp.sum(raised, axis=0, keepdims=True)
    stat_send[2:3, 0:TOK] = jnp.sum(raised * (logits - peak), axis=0, keepdims=True)
    stat_send[3:4, 0:TOK] = jnp.sum(jnp.where(hit, logits, 0.0), axis=0, keepdims=True)
    stat_recv[v] = stat_send[...]

    query_wide[...] = jnp.zeros(query_wide.shape, F32)
    for t in range(SEQ):
        for j in range(GROUP_HEADS):
            lane = (GROUP_HEADS * t + j) * HEAD
            query_wide[t, 4 * j : 4 * j + 4, :] = query[:, lane : lane + HEAD].astype(F32)
    query_send[...] = query_wide[...].astype(BF16)
    for k in range(8):
        kv_send[k, 0:4, :] = key_value[0, :, k * HEAD : k * HEAD + HEAD].astype(F32)
        kv_send[k, 4:8, :] = key_value[1, :, k * HEAD : k * HEAD + HEAD].astype(F32)
    proj_pad[...] = jnp.zeros(proj_pad.shape, BF16)
    proj_pad[:, 0:320] = out_proj[...]

    pl.semaphore_wait(barrier, VOC - 1 + SEQ - 1)

    def stat_copy(p, q):
        return remote(stat_send, stat_recv.at[q], stat_s.at[p], stat_r.at[q], vocab=p)

    @pl.loop(1, VOC)
    def _(d):
        stat_copy(lax.rem(v + d, VOC), v).start()

    half_copy = remote(
        proj_pad.at[pl.ds(pl.multiple_of(192 * (1 - core), 192), 192)],
        proj_half, half_s, half_r, vocab=mate,
    )
    half_copy.start()

    def kv1_copy(p, where):
        return remote(kv_send.at[p // 4], kv_recv.at[where], kv1_s.at[p], kv1_r.at[where], seq=p)

    def q_copy(p, where):
        return remote(query_send.at[p], query_recv.at[where], q_s.at[p], q_r.at[where], seq=p)

    @pl.loop(1, SEQ)
    def _(d):
        kv1_copy(lax.rem(s + d, SEQ), slot).start()

    @pl.loop(1, SEQ)
    def _(d):
        q_copy(lax.rem(s + d, SEQ), slot).start()

    kv_recv[slot] = kv_send[s // 4]
    query_recv[slot] = query_send[s]

    wide = hidden[pl.ds(pl.multiple_of(16 * (v // 4), 16), 16), :].astype(F32)
    wide = jnp.where(lax.rem(v // 2, 2) == 0, wide[0:8], wide[8:16])
    wide = jnp.where(core == 0, wide, turn(wide))
    gains = jnp.broadcast_to(gain[...], (8, D))

    def own_rows(x):
        x = jnp.broadcast_to(x, (TOK, 128)).reshape(8, 8, 128)
        at = lax.broadcasted_iota(jnp.int32, x.shape, 0) == v // 2
        x = jnp.sum(jnp.where(at, x, 0.0), axis=0)
        x = jnp.where(core == 0, x, turn(x))
        return first_halves(x, x)

    own_inv = own_rows(inv_rms)
    for b in range(20):
        left, right = slice(256 * b, 256 * b + 128), slice(256 * b + 128, 256 * b + 256)
        hidden_chunk[8 * b : 8 * b + 8, :] = first_halves(wide[:, left], wide[:, right])
        gain_chunk[8 * b : 8 * b + 8, :] = own_inv * first_halves(gains[:, left], gains[:, right])

    @pl.loop(1, VOC)
    def _(d):
        stat_copy(v, lax.rem(v + d, VOC)).wait_recv()

    stats = stat_recv[...]
    peaks = stats[:, 0, 0:TOK]
    row_peak = jnp.max(peaks, axis=0, keepdims=True)
    factor = jnp.exp(peaks - row_peak)
    row_total = jnp.sum(stats[:, 1, 0:TOK] * factor, axis=0, keepdims=True)
    weighted = jnp.sum(
        factor * (stats[:, 2, 0:TOK] + stats[:, 1, 0:TOK] * (peaks - row_peak)),
        axis=0, keepdims=True,
    )
    target_logit = jnp.sum(stats[:, 3, 0:TOK], axis=0, keepdims=True)
    loss_out[...] = jnp.log(row_total) + row_peak - target_logit
    tilt = weighted / row_total + (row_peak - target_logit)
    eye = lax.broadcasted_iota(jnp.int32, (TOK, TOK), 0) == lax.broadcasted_iota(
        jnp.int32, (TOK, TOK), 1
    )
    tilt = jnp.sum(jnp.where(eye, jnp.broadcast_to(tilt, (TOK, TOK)), 0.0), axis=1, keepdims=True)
    own_tilt = own_rows(inv_rms * inv_rms * tilt * (LOSS_SCALE / D))

    logits = logits_t[...]
    logit_grad = (
        LOSS_SCALE * (jnp.exp(logits - row_peak) / row_total - hit.astype(F32))
    ).astype(BF16)

    def part_step(j, carry):
        cols = pl.ds(pl.multiple_of(j * 512, 512), 512)
        rows = pl.ds(pl.multiple_of(j * 16, 16), 16)
        out = dot_tn(logit_grad, weight[:, cols])
        t = [out[:, 128 * i : 128 * i + 128].reshape(8, 8, 128) for i in range(4)]
        part_send[:, 0, rows, :] = jnp.concatenate(
            [first_halves(t[0], t[1]), first_halves(t[2], t[3])], axis=1
        ).astype(BF16)
        part_send[:, 1, rows, :] = jnp.concatenate(
            [second_halves(t[0], t[1]), second_halves(t[2], t[3])], axis=1
        ).astype(BF16)
        return carry

    lax.fori_loop(0, 10, part_step, 0)

    def part_copy(p, q):
        return remote(
            part_send.at[p // 2, lax.rem(p, 2)], part_recv.at[q], part_s.at[p], part_r.at[q], vocab=p
        )

    @pl.loop(1, VOC)
    def _(d):
        part_copy(lax.rem(v + d, VOC), v).start()

    part_recv[v] = part_send[chip, core]

    @pl.loop(1, SEQ)
    def _(d):
        o = lax.rem(s + d, SEQ)
        kv1_copy(s, lax.rem(o, 8) * 4 + o // 8).wait_recv()

    pairs = kv_recv[...].reshape(16, 2, 8, 128)
    own_keys = pl.ds(pl.multiple_of(v * ROWS, ROWS), ROWS)
    kv[0, own_keys, :] = first_halves(pairs[:, 0], pairs[:, 1]).reshape(ROWS, 128).astype(BF16)
    kv[1, own_keys, :] = second_halves(pairs[:, 0], pairs[:, 1]).reshape(ROWS, 128).astype(BF16)

    def kv2_copy(c, origin):
        at = kv.at[:, pl.ds(pl.multiple_of((2 * origin + core) * ROWS, ROWS), ROWS), :]
        return remote(at, at, kv2_s.at[c], kv2_r.at[origin], vocab=2 * c + core)

    def kfwd_copy(origin, side):
        at = kv.at[:, pl.ds(pl.multiple_of((2 * origin + side) * ROWS, ROWS), ROWS), :]
        return remote(at, at, kfwd_s.at[origin], kfwd_r.at[origin], vocab=mate)

    @pl.loop(1, 8)
    def _(d):
        kv2_copy(lax.rem(chip + d, 8), chip).start()

    kfwd_copy(chip, core).start()

    half_copy.wait_recv()
    lanes = lax.broadcasted_iota(jnp.int32, (192, 128), 1) < 64
    mine = pl.ds(pl.multiple_of(192 * core, 192), 192)
    lefts, rights = [], []
    for i in range(3):
        a = proj_pad[mine, 128 * i : 128 * i + 128].astype(F32)
        b = proj_half[:, 128 * i : 128 * i + 128].astype(F32)
        lefts.append(jnp.where(core == 0, a, b))
        rights.append(pltpu.roll(jnp.where(core == 0, b, a), 64, 1))
    tiles = [
        lefts[0], lefts[1],
        jnp.where(lanes, lefts[2], rights[0]),
        jnp.where(lanes, rights[0], rights[1]),
        jnp.where(lanes, rights[1], rights[2]),
    ]
    for i in range(5):
        proj[core, :, pl.ds(pl.multiple_of(640 * chip + 128 * i, 128), 128)] = tiles[i].astype(BF16)

    def proj_copy(c, origin):
        at = proj.at[core, :, pl.ds(pl.multiple_of(640 * origin, 640), 640)]
        return remote(at, at, proj_s.at[c], proj_r.at[origin], vocab=2 * c + core)

    def pfwd_copy(origin, side):
        at = proj.at[side, :, pl.ds(pl.multiple_of(640 * origin, 640), 640)]
        return remote(at, at, pfwd_s.at[origin], pfwd_r.at[origin], vocab=mate)

    @pl.loop(1, 8)
    def _(d):
        proj_copy(lax.rem(chip + d, 8), chip).start()

    pfwd_copy(chip, core).start()

    @pl.loop(1, SEQ)
    def _(d):
        o = lax.rem(s + d, SEQ)
        q_copy(s, lax.rem(o, 8) * 4 + o // 8).wait_recv()

    pairs = query_recv[...].astype(F32).reshape(16, 2, 16, 128)
    even, odd = pairs[:, 0], pairs[:, 1]
    query_rows[0:128, :] = first_halves(even[:, 0:8], odd[:, 0:8]).reshape(128, 128).astype(BF16)
    query_rows[128:256, :] = second_halves(even[:, 0:8], odd[:, 0:8]).reshape(128, 128).astype(BF16)
    query_rows[256:384, :] = first_halves(even[:, 8:16], odd[:, 8:16]).reshape(128, 128).astype(BF16)

    @pl.loop(1, VOC)
    def _(d):
        part_copy(v, lax.rem(v + d, VOC)).wait_recv()

    def grad_step(j, carry):
        rows = pl.ds(pl.multiple_of(j * 16, 16), 16)
        total = jnp.sum(part_recv[:, rows, :].astype(F32), axis=0)
        tilt16 = jnp.concatenate([own_tilt, own_tilt], axis=0)
        out = (gain_chunk[rows, :] * total - hidden_chunk[rows, :] * tilt16).astype(BF16)
        grad_pad[rows, :] = out
        blocks[y, h, rows, :] = out
        return carry

    lax.fori_loop(0, 10, grad_step, 0)
    grad_pad[160:176, :] = jnp.zeros((16, 128), BF16)

    def z_copy(d, target, origin):
        return remote(
            blocks.at[y, origin], blocks.at[y, origin], z_s.at[d], z_r.at[d], seq=target * 8 + y
        )

    for d in (1, 3, 2):
        z_copy(d, lax.rem(h + d, 4), h).start()

    def ring_copy(way, k, e, block):
        to = lax.rem(y + 1 + 6 * way, 8)
        at = blocks.at[block, lax.rem(h + e, 4)]
        return remote(at, at, ring_s.at[way, k, e], ring_r.at[way, k, e], seq=h * 8 + to)

    def sent(way, k):
        return lax.rem(y + (8 - k if way == 0 else k), 8)

    def got(way, k):
        return lax.rem(y + (7 - k if way == 0 else k + 1), 8)

    def goes(way, k, e):
        return k < 3 or (e < 2) == (way == 0)

    def first_rows(p):
        return pl.multiple_of((4 * ((5 * p) // 2)) // 16 * 16, 16)

    def slice_copy(p, q):
        return remote(
            grad_pad.at[pl.ds(first_rows(p), 32)], slice_recv.at[q], slice_s.at[p], slice_r.at[q], vocab=p
        )

    for way in range(2):
        ring_copy(way, 0, 0, y).start()

    @pl.loop(1, VOC)
    def _(d):
        slice_copy(lax.rem(v + d, VOC), v).start()

    slice_recv[v] = grad_pad[pl.ds(first_rows(v), 32), :]

    for e in (1, 3, 2):
        z_copy(4 - e, h, lax.rem(h + e, 4)).wait_recv()
        for way in range(2):
            ring_copy(way, 0, e, y).start()

    def ring_step(k):
        for e in (0, 1, 3, 2):
            for way in range(2):
                ring_copy(way, k - 1, e, got(way, k - 1)).wait_recv()
                if goes(way, k, e):
                    ring_copy(way, k, e, sent(way, k)).start()

    @pl.loop(1, 8)
    def _(d):
        o = lax.rem(chip + d, 8)
        kv2_copy(chip, o).wait_recv()
        kfwd_copy(o, core).start()

    @pl.loop(0, 8)
    def _(o):
        kfwd_copy(o, 1 - core).wait_recv()

    ring_step(1)

    start = offset[0]
    r = lax.rem(lax.broadcasted_iota(jnp.int32, (1, STACK), 1), ROWS)
    q_place = (lax.rem(r // 4, 4) * 8 + r // 16) * TOK + 4 * v + lax.rem(r, 4)
    r = lax.broadcasted_iota(jnp.int32, (ROWS, 1), 0)
    k_base = (lax.rem(r // 4, 4) * 8 + r // 16) * TOK + lax.rem(r, 4)
    q_before = q_place < start

    def score_step(c, top):
        keys = pl.ds(pl.multiple_of(c * ROWS, ROWS), ROWS)
        k_place = k_base + 4 * c
        seen = (k_place <= q_place) & ((k_place >= start) | q_before)
        x = jnp.where(seen, dot_nt(kv[0, keys, :], query_rows[...]) * SCALE, MASKED)
        scores[keys, :] = x
        return jnp.maximum(top, jnp.max(x, axis=0, keepdims=True))

    top = lax.fori_loop(0, 16, score_step, jnp.full((1, STACK), MASKED, F32))

    def exp_step(c, total):
        keys = pl.ds(pl.multiple_of(c * ROWS, ROWS), ROWS)
        x = jnp.exp(scores[keys, :] - top)
        scores[keys, :] = x
        return total + jnp.sum(x, axis=0, keepdims=True)

    total = lax.fori_loop(0, 16, exp_step, jnp.zeros((1, STACK), F32))
    share = 1.0 / total

    ring_step(2)

    def prob_step(c, carry):
        keys = pl.ds(pl.multiple_of(c * ROWS, ROWS), ROWS)
        x = scores[keys, :] * share
        scores[keys, :] = x
        probs_low[keys, :] = x.astype(BF16)
        return carry

    lax.fori_loop(0, 16, prob_step, 0)

    ring_step(3)

    @pl.loop(1, 8)
    def _(d):
        o = lax.rem(chip + d, 8)
        proj_copy(chip, o).wait_recv()
        pfwd_copy(o, core).start()

    @pl.loop(1, VOC)
    def _(d):
        slice_copy(v, lax.rem(v + d, VOC)).wait_recv()

    pairs = slice_recv[...].astype(F32).reshape(8, 2, 32, 128)
    for b in range(4):
        even, odd = pairs[:, 0, 8 * b : 8 * b + 8], pairs[:, 1, 8 * b : 8 * b + 8]
        slice_tiles[2 * b] = first_halves(even, odd).reshape(TOK, 128)
        slice_tiles[2 * b + 1] = second_halves(even, odd).reshape(TOK, 128)
    skip = (5 * v) // 2 - first_rows(v) // 4
    lanes = lax.broadcasted_iota(jnp.int32, (TOK, 128), 1) < 64
    t = [slice_tiles[skip + i] for i in range(3)]
    turned = [pltpu.roll(x, 64, 1) for x in t]
    hidden_out[:, 0:128] = jnp.where(
        core == 0, t[0], jnp.where(lanes, turned[0], turned[1])
    ).astype(BF16)
    hidden_out[:, 128:256] = jnp.where(
        core == 0, t[1], jnp.where(lanes, turned[1], turned[2])
    ).astype(BF16)
    hidden_out[:, 256:320] = jnp.where(core == 0, t[2], turned[2])[:, 0:64].astype(BF16)

    for e in range(4):
        way = 0 if e < 2 else 1
        ring_copy(way, 3, e, got(way, 3)).wait_recv()

    def act_step(i, carry):
        b, j = i // 10, lax.rem(i, 10)
        x = blocks[b, :, pl.ds(pl.multiple_of(j * 16, 16), 16), :].astype(F32)
        rows = pl.ds(pl.multiple_of(b * 16, 16), 16)
        for n in range(4):
            part = x[:, 8 * (n // 2) : 8 * (n // 2) + 8]
            join = first_halves if n % 2 == 0 else second_halves
            cols = pl.ds(pl.multiple_of(j * 512 + 128 * n, 128), 128)
            acts[rows, cols] = jnp.concatenate(
                [join(part[0], part[1]), join(part[2], part[3])], axis=0
            ).astype(BF16)
        return carry

    lax.fori_loop(0, 80, act_step, 0)

    @pl.loop(0, 8)
    def _(o):
        pfwd_copy(o, 1 - core).wait_recv()

    for side in range(2):
        out = jnp.zeros((ROWS, 192), F32)

        def og_step(j, acc):
            cols = pl.ds(pl.multiple_of(j * 512, 512), 512)
            return acc + dot_nt(acts[:, cols], proj[side, :, cols])

        og[side] = lax.fori_loop(0, 10, og_step, out).astype(BF16)
    out_grad = jnp.concatenate(
        [
            og[0, :, 0:128],
            jnp.concatenate([og[0, :, 128:192], og[1, :, 0:64]], axis=1),
            og[1, :, 64:192],
        ],
        axis=0,
    )

    def grad_pass(c, delta):
        keys = pl.ds(pl.multiple_of(c * ROWS, ROWS), ROWS)
        x = dot_nt(kv[1, keys, :], out_grad)
        prob_grad[keys, :] = x
        return delta + jnp.sum(probs_low[keys, :].astype(F32) * x, axis=0, keepdims=True)

    delta = lax.fori_loop(0, 16, grad_pass, jnp.zeros((1, STACK), F32))

    def dkv_copy(p, q):
        return remote(dkv_send.at[p], dkv_recv.at[q], dkv_s.at[p], dkv_r.at[q], vocab=p)

    def key_pass(d, carry):
        c = lax.rem(v + d, VOC)
        keys = pl.ds(pl.multiple_of(c * ROWS, ROWS), ROWS)
        ds_low = (scores[keys, :] * (prob_grad[keys, :] - delta)).astype(BF16)
        score_grad[keys, :] = ds_low
        key_part = jnp.dot(ds_low, query_rows[...], preferred_element_type=F32) * SCALE
        value_part = jnp.dot(probs_low[keys, :], out_grad, preferred_element_type=F32)
        dkv_send[c, 0] = key_part.astype(BF16)
        dkv_send[c, 1] = value_part.astype(BF16)

        @pl.when(d < VOC)
        def _():
            dkv_copy(c, v).start()

        return carry

    lax.fori_loop(1, VOC + 1, key_pass, 0)
    dkv_recv[v] = dkv_send[v]

    dq = dot_tn(score_grad[...], kv[0]) * SCALE
    t0, t1, t2 = [dq[128 * j : 128 * j + 128].reshape(16, 8, 128) for j in range(3)]
    dq_send[:, 0] = jnp.concatenate([first_halves(t0, t1), t2], axis=1).astype(BF16)
    dq_send[:, 1] = jnp.concatenate([second_halves(t0, t1), turn(t2)], axis=1).astype(BF16)

    def dq_copy(p, q):
        at = lax.rem(p, 8) * 4 + p // 8
        return remote(
            dq_send.at[at // 2, lax.rem(at, 2)], dq_recv.at[q], dq_s.at[p], dq_r.at[q], seq=p
        )

    @pl.loop(1, SEQ)
    def _(d):
        dq_copy(lax.rem(s + d, SEQ), s).start()

    dq_recv[s] = dq_send[slot // 2, lax.rem(slot, 2)]

    @pl.loop(1, VOC)
    def _(d):
        dkv_copy(v, lax.rem(v + d, VOC)).wait_recv()

    keys_sum = jnp.sum(dkv_recv[:, 0].astype(F32), axis=0).reshape(16, 8, 128)
    values_sum = jnp.sum(dkv_recv[:, 1].astype(F32), axis=0).reshape(16, 8, 128)
    fold_send[:, 0] = first_halves(keys_sum, values_sum)
    fold_send[:, 1] = second_halves(keys_sum, values_sum)

    def fold_copy(p, q):
        at = lax.rem(p, 8) * 4 + p // 8
        return remote(
            fold_send.at[at // 2, lax.rem(at, 2)], fold_recv.at[q], fold_s.at[p], fold_r.at[q], seq=p
        )

    @pl.loop(1, SEQ)
    def _(d):
        fold_copy(lax.rem(s + d, SEQ), s).start()

    fold_recv[s] = fold_send[slot // 2, lax.rem(slot, 2)]

    @pl.loop(1, SEQ)
    def _(d):
        dq_copy(s, lax.rem(s + d, SEQ)).wait_recv()

    for t in range(SEQ):
        x = dq_recv[t].astype(F32)
        for j in range(GROUP_HEADS):
            lane = (GROUP_HEADS * t + j) * HEAD
            query_out[:, lane : lane + HEAD] = x[4 * j : 4 * j + 4].astype(BF16)

    @pl.loop(1, SEQ)
    def _(d):
        fold_copy(s, lax.rem(s + d, SEQ)).wait_recv()

    for k in range(8):
        x = jnp.sum(fold_recv[4 * k : 4 * k + 4], axis=0)
        kv_out[0, :, k * HEAD : k * HEAD + HEAD] = x[0:4].astype(BF16)
        kv_out[1, :, k * HEAD : k * HEAD + HEAD] = x[4:8].astype(BF16)

    half_copy.wait_send()

    @pl.loop(1, VOC)
    def _(d):
        p = lax.rem(v + d, VOC)
        stat_copy(p, v).wait_send()
        part_copy(p, v).wait_send()
        slice_copy(p, v).wait_send()
        dkv_copy(p, v).wait_send()

    @pl.loop(1, SEQ)
    def _(d):
        p = lax.rem(s + d, SEQ)
        kv1_copy(p, slot).wait_send()
        q_copy(p, slot).wait_send()
        dq_copy(p, s).wait_send()
        fold_copy(p, s).wait_send()

    @pl.loop(1, 8)
    def _(d):
        c = lax.rem(chip + d, 8)
        kv2_copy(c, chip).wait_send()
        proj_copy(c, chip).wait_send()

    @pl.loop(0, 8)
    def _(o):
        kfwd_copy(o, core).wait_send()
        pfwd_copy(o, core).wait_send()

    for d in (1, 3, 2):
        z_copy(d, lax.rem(h + d, 4), h).wait_send()
    for k in range(4):
        for e in range(4):
            for way in range(2):
                if goes(way, k, e):
                    ring_copy(way, k, e, sent(way, k)).wait_send()


def scratch():
    v = pltpu.VMEM
    dma = pltpu.SemaphoreType.DMA
    buffers = [
        v((256, TOK), F32), v((8, 128), F32), v((VOC, 8, 128), F32),
        v((8, 2, 160, 128), BF16), v((VOC, 160, 128), BF16),
        v((160, 128), F32), v((160, 128), F32), v((176, 128), BF16),
        v((VOC, 32, 128), BF16), v((8, TOK, 128), F32),
        v((8, 4, 160, 128), BF16), v((ROWS, D), BF16),
        v((384, 384), BF16), v((192, 384), BF16), v((2, 192, D), BF16),
        v((SEQ, 16, 128), F32), v((SEQ, 16, 128), BF16), v((SEQ, 16, 128), BF16), v((STACK, 128), BF16),
        v((8, 8, 128), F32), v((SEQ, 8, 128), F32), v((2, KEYS, 128), BF16),
        v((KEYS, STACK), F32), v((KEYS, STACK), BF16), v((KEYS, STACK), F32), v((KEYS, STACK), BF16),
        v((2, ROWS, 192), BF16),
        v((16, 2, 16, 128), BF16), v((SEQ, 16, 128), BF16),
        v((VOC, 2, ROWS, 128), BF16), v((VOC, 2, ROWS, 128), BF16),
        v((16, 2, 8, 128), F32), v((SEQ, 8, 128), F32),
    ]
    sizes = [
        (VOC,), (VOC,), (VOC,), (VOC,), (VOC,), (VOC,), (4,), (4,), (2, 4, 4), (2, 4, 4),
        None, None, (8,), (8,), (8,), (8,), (SEQ,), (SEQ,), (SEQ,), (SEQ,), (8,), (8,),
        (8,), (8,), (SEQ,), (SEQ,), (VOC,), (VOC,), (SEQ,), (SEQ,),
    ]
    return buffers + [dma if n is None else dma(n) for n in sizes]


def shards(hidden, norm_gain, head_weight, targets, out_proj, query, saved_key_value, offset):
    vmem = pl.BlockSpec(memory_space=pltpu.VMEM)
    loss, hidden_grad, query_grad, kv_grad = pl.pallas_call(
        body,
        out_shape=(
            jax.ShapeDtypeStruct((1, TOK), F32),
            jax.ShapeDtypeStruct((TOK, 320), BF16),
            jax.ShapeDtypeStruct(query.shape, BF16),
            jax.ShapeDtypeStruct(saved_key_value.shape, BF16),
        ),
        in_specs=[vmem] * 7 + [pl.BlockSpec(memory_space=pltpu.SMEM)],
        out_specs=(vmem,) * 4,
        scratch_shapes=scratch(),
        compiler_params=pltpu.CompilerParams(
            collective_id=0, has_side_effects=True, vmem_limit_bytes=56 * 2**20
        ),
    )(
        hidden, norm_gain.reshape(1, D), head_weight, targets.reshape(1, TOK), out_proj, query,
        saved_key_value, offset,
    )
    return loss.reshape(TOK), hidden_grad, query_grad, kv_grad


def solution(mesh):
    in_specs = (
        P("seq", None),
        P(),
        P("vocab", None),
        P("seq"),
        P("seq", "vocab"),
        P(("seq", "vocab"), None),
        P(None, ("seq", "vocab"), None),
        P(),
    )
    out_specs = (
        P("seq"),
        P("seq", "vocab"),
        P(("seq", "vocab"), None),
        P(None, ("seq", "vocab"), None),
    )
    return jax.shard_map(shards, mesh=mesh, in_specs=in_specs, out_specs=out_specs, check_vma=False)
```

```python
import jax
import jax.numpy as jnp
from jax import lax
from jax.experimental import pallas as pl
from jax.experimental.pallas import tpu as pltpu
from jax.sharding import PartitionSpec as P

D = 5120
HEAD = 128
SEQ = 32
VOC = 16
TOK = 64
GROUP_HEADS = 3
ROWS = 128
STACK = GROUP_HEADS * ROWS
KEYS = 2048
EPS = 1e-05
LOSS_SCALE = 32.0
MASKED = -1e30
VMEM_BYTES = 62 * 2**20
SCALE = HEAD ** (-0.5)
MESH = pl.DeviceIdType.MESH
F32 = jnp.float32
BF16 = jnp.bfloat16


def remote(src, dst, send_sem, recv_sem, **device):
    return pltpu.make_async_remote_copy(
        src_ref=src,
        dst_ref=dst,
        send_sem=send_sem,
        recv_sem=recv_sem,
        device_id=device,
        device_id_type=MESH,
    )


def low_rows(shape):
    return lax.broadcasted_iota(jnp.int32, shape, len(shape) - 2) < 4


def turn(x):
    return pltpu.roll(x, 4, len(x.shape) - 2)


def first_halves(a, b):
    return jnp.where(low_rows(a.shape), a, turn(b))


def second_halves(a, b):
    return jnp.where(low_rows(a.shape), turn(a), b)


def dot_nt(a, b):
    return lax.dot_general(a, b, (((1,), (1,)), ((), ())), preferred_element_type=F32)


def dot_tn(a, b):
    return lax.dot_general(a, b, (((0,), (0,)), ((), ())), preferred_element_type=F32)


def body(
    hidden_in, gain_in, weight_in, targets_in, proj_in, query_in, key_value_in, offset,
    loss_res, hidden_res, query_res, kv_res,
    hidden, gain, weight, targets, query, key_value, loss_out, hidden_out, query_out, kv_out,
    logits_t, stat_send, stat_recv, part_send, part_mate, part_sum, part_recv,
    gain_chunk, hidden_chunk, grad_pad, slice_recv, slice_tiles, blocks, acts, proj,
    query_wide, query_send, query_recv, query_rows, kv_send, kv_recv, kv,
    scores, probs_low, prob_grad, score_grad,
    dq_send, dq_recv, dkv_own, dkv_give, dkv_mate, dkv_sum, dkv_recv, fold_send, fold_recv,
    in_s, out_s, stat_s, stat_r, mate_s, mate_r, part_s, part_r, slice_s, slice_r, z_s, z_r, ring_s, ring_r,
    proj_s, proj_z, proj_x, proj_xx, proj_m, q_s, q_r, kv1_s, kv1_r, kv_s, kv_z, kv_x, kv_xx, kvm_s, kvm_r,
    dq_s, dq_r, dkvm_s, dkvm_r, dkv_s, dkv_r, fold_s, fold_r,
):
    s = lax.axis_index("seq")
    v = lax.axis_index("vocab")
    h, y = s // 8, lax.rem(s, 8)
    slot = y * 4 + h
    chip, core = v // 2, lax.rem(v, 2)
    mate = v + 1 - 2 * core
    beside = v + 2 - 4 * lax.rem(chip, 2)

    def around(block, steps):
        return lax.rem(block + 4 * steps, VOC)

    def wait_recv(ref, sem):
        remote(ref, ref, sem, sem, vocab=mate).wait_recv()

    def wait_send(ref, sem):
        remote(ref, ref, sem, sem, vocab=mate).wait_send()

    def proj_rows(block, first=0, count=320):
        return proj.at[pl.ds(pl.multiple_of(320 * block + first, 16), count)]

    loads = [
        pltpu.make_async_copy(src, dst, in_s.at[i])
        for i, (src, dst) in enumerate(
            [
                (hidden_in, hidden), (gain_in, gain), (targets_in, targets),
                (weight_in.at[:, 0:2560], weight.at[:, 0:2560]),
                (weight_in.at[:, 2560:5120], weight.at[:, 2560:5120]),
                (query_in, query), (key_value_in, key_value), (proj_in, proj_rows(v)),
            ]
        )
    ]
    for load in loads:
        load.start()
    barrier = pltpu.get_barrier_semaphore()

    @pl.loop(1, VOC)
    def _(d):
        pl.semaphore_signal(
            barrier, inc=1, device_id={"vocab": lax.rem(v + d, VOC)}, device_id_type=MESH
        )

    @pl.loop(1, SEQ)
    def _(d):
        pl.semaphore_signal(
            barrier, inc=1, device_id={"seq": lax.rem(s + d, SEQ)}, device_id_type=MESH
        )

    stores = [
        pltpu.make_async_copy(src, dst, out_s.at[i])
        for i, (src, dst) in enumerate(
            [(loss_out, loss_res), (hidden_out, hidden_res), (query_out, query_res), (kv_out, kv_res)]
        )
    ]

    def square(j, acc):
        x = hidden[:, pl.ds(pl.multiple_of(j * 512, 512), 512)].astype(F32)
        x = x * x
        return acc + (x[:, :128] + x[:, 128:256]) + (x[:, 256:384] + x[:, 384:])

    loads[0].wait()
    squares = lax.fori_loop(0, 10, square, jnp.zeros((TOK, 128), F32))
    inv_rms = lax.rsqrt(jnp.sum(squares, axis=1, keepdims=True) / D + EPS)
    loads[1].wait()
    loads[3].wait()

    def logit_step(j, acc):
        cols = pl.ds(pl.multiple_of(j * 512, 512), 512)
        normed = (hidden[:, cols].astype(F32) * inv_rms * gain[:, cols]).astype(BF16)
        return acc + dot_nt(weight[:, cols], normed)

    logits = lax.fori_loop(0, 5, logit_step, jnp.zeros((256, TOK), F32))
    loads[4].wait()
    logits = lax.fori_loop(5, 10, logit_step, logits)
    logits_t[...] = logits
    loads[2].wait()
    hit = (v * 256 + lax.broadcasted_iota(jnp.int32, (256, TOK), 0)) == targets[...]
    peak = jnp.max(logits, axis=0, keepdims=True)
    raised = jnp.exp(logits - peak)
    stat_send[...] = jnp.zeros((8, 128), F32)
    stat_send[0:1, 0:TOK] = peak
    stat_send[1:2, 0:TOK] = jnp.sum(raised, axis=0, keepdims=True)
    stat_send[2:3, 0:TOK] = jnp.sum(raised * (logits - peak), axis=0, keepdims=True)
    stat_send[3:4, 0:TOK] = jnp.sum(jnp.where(hit, logits, 0.0), axis=0, keepdims=True)
    stat_recv[v] = stat_send[...]

    for load in loads[5:]:
        load.wait()
    query_wide[...] = jnp.zeros(query_wide.shape, F32)
    for t in range(SEQ):
        for j in range(GROUP_HEADS):
            lane = (GROUP_HEADS * t + j) * HEAD
            query_wide[t, 4 * j : 4 * j + 4, :] = query[:, lane : lane + HEAD].astype(F32)
    query_send[...] = query_wide[...].astype(BF16)
    for k in range(8):
        kv_send[k, 0:4, :] = key_value[0, :, k * HEAD : k * HEAD + HEAD].astype(F32)
        kv_send[k, 4:8, :] = key_value[1, :, k * HEAD : k * HEAD + HEAD].astype(F32)

    pl.semaphore_wait(barrier, VOC - 1 + SEQ - 1)

    @pl.loop(1, VOC)
    def _(d):
        remote(stat_send, stat_recv.at[v], stat_s, stat_r, vocab=lax.rem(v + d, VOC)).start()

    @pl.loop(1, SEQ)
    def _(d):
        p = lax.rem(s + d, SEQ)
        remote(kv_send.at[p // 4], kv_recv.at[slot], kv1_s, kv1_r, seq=p).start()

    def proj_copy(at, sem, to):
        return remote(at, at, proj_s, sem, vocab=to)

    kv_recv[slot] = kv_send[s // 4]
    query_recv[slot] = query_send[s]

    wide = hidden[pl.ds(pl.multiple_of(16 * (v // 4), 16), 16), :].astype(F32)
    wide = jnp.where(lax.rem(v // 2, 2) == 0, wide[0:8], wide[8:16])
    wide = jnp.where(core == 0, wide, turn(wide))
    gains = jnp.broadcast_to(gain[...], (8, D))

    def own_rows(x):
        x = jnp.broadcast_to(x, (TOK, 128)).reshape(8, 8, 128)
        at = lax.broadcasted_iota(jnp.int32, x.shape, 0) == v // 2
        x = jnp.sum(jnp.where(at, x, 0.0), axis=0)
        x = jnp.where(core == 0, x, turn(x))
        return first_halves(x, x)

    own_inv = own_rows(inv_rms)
    for b in range(20):
        left, right = slice(256 * b, 256 * b + 128), slice(256 * b + 128, 256 * b + 256)
        hidden_chunk[8 * b : 8 * b + 8, :] = first_halves(wide[:, left], wide[:, right])
        gain_chunk[8 * b : 8 * b + 8, :] = own_inv * first_halves(gains[:, left], gains[:, right])

    wait_recv(stat_recv.at[pl.ds(0, VOC - 1)], stat_r)
    stats = stat_recv[...]
    peaks = stats[:, 0, 0:TOK]
    row_peak = jnp.max(peaks, axis=0, keepdims=True)
    factor = jnp.exp(peaks - row_peak)
    row_total = jnp.sum(stats[:, 1, 0:TOK] * factor, axis=0, keepdims=True)
    weighted = jnp.sum(
        factor * (stats[:, 2, 0:TOK] + stats[:, 1, 0:TOK] * (peaks - row_peak)),
        axis=0, keepdims=True,
    )
    target_logit = jnp.sum(stats[:, 3, 0:TOK], axis=0, keepdims=True)
    loss_out[...] = jnp.log(row_total) + row_peak - target_logit
    stores[0].start()
    tilt = weighted / row_total + (row_peak - target_logit)
    eye = lax.broadcasted_iota(jnp.int32, (TOK, TOK), 0) == lax.broadcasted_iota(
        jnp.int32, (TOK, TOK), 1
    )
    tilt = jnp.sum(jnp.where(eye, jnp.broadcast_to(tilt, (TOK, TOK)), 0.0), axis=1, keepdims=True)
    own_tilt = own_rows(inv_rms * inv_rms * tilt * (LOSS_SCALE / D))

    logits = logits_t[...]
    logit_grad = (
        LOSS_SCALE * (jnp.exp(logits - row_peak) / row_total - hit.astype(F32))
    ).astype(BF16)

    def part_step(j, carry):
        cols = pl.ds(pl.multiple_of(j * 512, 512), 512)
        rows = pl.ds(pl.multiple_of(j * 16, 16), 16)
        out = dot_tn(logit_grad, weight[:, cols])
        t = [out[:, 128 * i : 128 * i + 128].reshape(8, 8, 128) for i in range(4)]
        part_send[0, :, rows, :] = jnp.concatenate(
            [first_halves(t[0], t[1]), first_halves(t[2], t[3])], axis=1
        ).astype(BF16)
        part_send[1, :, rows, :] = jnp.concatenate(
            [second_halves(t[0], t[1]), second_halves(t[2], t[3])], axis=1
        ).astype(BF16)
        return carry

    halves = [pl.ds(0, 80), pl.ds(80, 80)]

    def mate_copy(i):
        return remote(
            part_send.at[1 - core, :, halves[i]], part_mate.at[:, halves[i]],
            mate_s.at[i], mate_r.at[i], vocab=mate,
        )

    for i in range(2):
        lax.fori_loop(5 * i, 5 * i + 5, part_step, 0)
        mate_copy(i).start()

    for i in range(2):
        mate_copy(i).wait_recv()
        for b in range(5):
            rows = pl.ds(80 * i + 16 * b, 16)
            part_sum[:, rows, :] = (
                part_send[core, :, rows, :].astype(F32) + part_mate[:, rows, :].astype(F32)
            ).astype(BF16)

        @pl.loop(1, 8)
        def _(d):
            m = lax.rem(chip + d, 8)
            remote(
                part_sum.at[m, halves[i]], part_recv.at[chip, halves[i]], part_s, part_r.at[i],
                vocab=2 * m + core,
            ).start()

    @pl.loop(1, SEQ)
    def _(d):
        p = lax.rem(s + d, SEQ)
        remote(query_send.at[p], query_recv.at[slot], q_s, q_r, seq=p).start()

    part_recv[chip] = part_sum[chip]

    wait_recv(kv_recv.at[pl.ds(0, SEQ - 1)], kv1_r)
    pairs = kv_recv[...].reshape(16, 2, 8, 128)
    kv[0, chip, core] = first_halves(pairs[:, 0], pairs[:, 1]).reshape(ROWS, 128).astype(BF16)
    kv[1, chip, core] = second_halves(pairs[:, 0], pairs[:, 1]).reshape(ROWS, 128).astype(BF16)

    def kv_copy(block, sem, to, kinds=slice(0, 2)):
        at = kv.at[kinds, block // 2, lax.rem(block, 2)]
        return remote(at, at, kv_s, sem, vocab=to)

    kv_copy(v, kv_z, beside).start()
    for way in range(2):
        kv_copy(v, kv_x.at[way, 0], around(v, 1 + 2 * way)).start()

    def grad_step(j, carry):
        rows = pl.ds(pl.multiple_of(j * 16, 16), 16)
        total = jnp.sum(part_recv[:, rows, :].astype(F32), axis=0)
        tilt16 = jnp.concatenate([own_tilt, own_tilt], axis=0)
        out = (gain_chunk[rows, :] * total - hidden_chunk[rows, :] * tilt16).astype(BF16)
        grad_pad[rows, :] = out
        blocks[y, h, rows, :] = out
        return carry

    for i in range(2):
        wait_recv(part_recv.at[pl.ds(0, 7), halves[i]], part_r.at[i])
        lax.fori_loop(5 * i, 5 * i + 5, grad_step, 0)
    grad_pad[160:176, :] = jnp.zeros((16, 128), BF16)

    def z_copy(d, target, origin):
        at = blocks.at[y, origin]
        return remote(at, at, z_s, z_r.at[d], seq=target * 8 + y)

    for d in (1, 3, 2):
        z_copy(d, lax.rem(h + d, 4), h).start()

    def ring_copy(way, k, e, block):
        to = lax.rem(y + 1 + 6 * way, 8)
        at = blocks.at[block, lax.rem(h + e, 4)]
        return remote(at, at, ring_s, ring_r.at[way, k, e], seq=h * 8 + to)

    def sent(way, k):
        return lax.rem(y + (8 - k if way == 0 else k), 8)

    def got(way, k):
        return lax.rem(y + (7 - k if way == 0 else k + 1), 8)

    def goes(way, k, e):
        return k < 3 or (e < 2) == (way == 0)

    def first_rows(p):
        return pl.multiple_of((4 * ((5 * p) // 2)) // 16 * 16, 16)

    for way in range(2):
        ring_copy(way, 0, 0, y).start()
    proj_copy(proj_rows(v), proj_z, beside).start()
    for way in range(2):
        proj_copy(proj_rows(v), proj_x.at[way, 0], around(v, 1 + 2 * way)).start()
    proj_copy(proj_rows(v), proj_m, mate).start()

    def proj_next(kind):
        block = v if kind == 0 else beside
        for way in range(2):
            here = around(block, 3 - 2 * way)
            proj_copy(proj_rows(here), proj_x.at[way, kind], mate).wait_recv()
            proj_copy(
                proj_rows(here, 160 * way, 160), proj_xx.at[way, kind], around(v, 1 + 2 * way)
            ).start()
            proj_copy(proj_rows(here), proj_m, mate).start()

    def kv_next(kind):
        block = v if kind == 0 else beside
        for way in range(2):
            here = around(block, 3 - 2 * way)
            kv_copy(here, kv_x.at[way, kind], mate).wait_recv()
            kv_copy(here, kv_xx.at[way, kind], around(v, 1 + 2 * way), slice(way, way + 1)).start()

    def ring_start(e):
        z_copy(4 - e, h, lax.rem(h + e, 4)).wait_recv()
        for way in range(2):
            ring_copy(way, 0, e, y).start()

    def ring_next(k, e):
        for way in range(2):
            if goes(way, k - 1, e):
                ring_copy(way, k - 1, e, got(way, k - 1)).wait_recv()
            if k < 4 and goes(way, k, e):
                ring_copy(way, k, e, sent(way, k)).start()

    kv_copy(beside, kv_z, mate).wait_recv()
    for way in range(2):
        kv_copy(beside, kv_x.at[way, 1], around(v, 1 + 2 * way)).start()
    kv_next(0)
    ring_start(1)
    ring_next(1, 0)
    kv_next(1)
    ring_start(3)
    ring_next(1, 1)
    proj_copy(proj_rows(beside), proj_z, mate).wait_recv()
    for way in range(2):
        proj_copy(proj_rows(beside), proj_x.at[way, 1], around(v, 1 + 2 * way)).start()
    proj_copy(proj_rows(beside), proj_m, mate).start()

    for kind in range(2):
        for way in range(2):
            far = around(v if kind == 0 else beside, 2)
            kv_copy(far, kv_xx.at[way, kind], mate, slice(way, way + 1)).wait_recv()
    remote(kv.at[:, :, core], kv.at[:, :, core], kvm_s, kvm_r, vocab=mate).start()
    ring_next(2, 0)
    ring_start(2)
    ring_next(1, 3)

    @pl.loop(1, VOC)
    def _(d):
        p = lax.rem(v + d, VOC)
        remote(
            grad_pad.at[pl.ds(first_rows(p), 32)], slice_recv.at[v], slice_s, slice_r, vocab=p
        ).start()

    slice_recv[v] = grad_pad[pl.ds(first_rows(v), 32), :]

    wait_recv(query_recv.at[pl.ds(0, SEQ - 1)], q_r)
    pairs = query_recv[...].astype(F32).reshape(16, 2, 16, 128)
    even, odd = pairs[:, 0], pairs[:, 1]
    query_rows[0:128, :] = first_halves(even[:, 0:8], odd[:, 0:8]).reshape(128, 128).astype(BF16)
    query_rows[128:256, :] = second_halves(even[:, 0:8], odd[:, 0:8]).reshape(128, 128).astype(BF16)
    query_rows[256:384, :] = first_halves(even[:, 8:16], odd[:, 8:16]).reshape(128, 128).astype(BF16)

    wait_recv(kv.at[:, :, 1 - core], kvm_r)

    start = offset[0]
    r = lax.rem(lax.broadcasted_iota(jnp.int32, (1, STACK), 1), ROWS)
    q_place = (lax.rem(r // 4, 4) * 8 + r // 16) * TOK + 4 * v + lax.rem(r, 4)
    r = lax.broadcasted_iota(jnp.int32, (256, 1), 0)
    k_base = (lax.rem(r // 4, 4) * 8 + lax.rem(r // 16, 8)) * TOK + 4 * (r // ROWS) + lax.rem(r, 4)
    q_before = q_place < start

    def score_part(m, top):
        keys = slice(256 * m, 256 * m + 256)
        k_place = k_base + 8 * m
        seen = (k_place <= q_place) & ((k_place >= start) | q_before)
        x = dot_nt(kv[0, m].reshape(256, HEAD), query_rows[...]) * SCALE
        x = jnp.where(seen, x, MASKED)
        scores[keys, :] = x
        return jnp.maximum(top, jnp.max(x, axis=0, keepdims=True))

    def exp_part(m, top, total):
        keys = slice(256 * m, 256 * m + 256)
        x = jnp.exp(scores[keys, :] - top)
        scores[keys, :] = x
        return total + jnp.sum(x, axis=0, keepdims=True)

    def prob_part(m, share):
        keys = slice(256 * m, 256 * m + 256)
        x = scores[keys, :] * share
        scores[keys, :] = x
        probs_low[keys, :] = x.astype(BF16)

    state = {"top": jnp.full((1, STACK), MASKED, F32), "total": jnp.zeros((1, STACK), F32)}

    def piece(n):
        if n < 8:
            state["top"] = score_part(n, state["top"])
        elif n < 16:
            state["total"] = exp_part(n - 8, state["top"], state["total"])
        else:
            if n == 16:
                state["share"] = 1.0 / state["total"]
            prob_part(n - 16, state["share"])

    events = [(2, 1), (3, 0), (1, 2), (2, 3), (3, 1), (2, 2), (3, 3), (3, 2), (4, 0)]
    for n in range(24):
        piece(n)
        if n % 2 == 0 and n // 2 < len(events):
            ring_next(*events[n // 2])
        if n == 4:
            proj_next(0)
        if n == 12:
            proj_next(1)

    wait_recv(slice_recv.at[pl.ds(0, VOC - 1)], slice_r)
    pairs = slice_recv[...].astype(F32).reshape(8, 2, 32, 128)
    for b in range(4):
        even, odd = pairs[:, 0, 8 * b : 8 * b + 8], pairs[:, 1, 8 * b : 8 * b + 8]
        slice_tiles[2 * b] = first_halves(even, odd).reshape(TOK, 128)
        slice_tiles[2 * b + 1] = second_halves(even, odd).reshape(TOK, 128)
    skip = (5 * v) // 2 - first_rows(v) // 4
    lanes = lax.broadcasted_iota(jnp.int32, (TOK, 128), 1) < 64
    t = [slice_tiles[skip + i] for i in range(3)]
    turned = [pltpu.roll(x, 64, 1) for x in t]
    hidden_out[:, 0:128] = jnp.where(
        core == 0, t[0], jnp.where(lanes, turned[0], turned[1])
    ).astype(BF16)
    hidden_out[:, 128:256] = jnp.where(
        core == 0, t[1], jnp.where(lanes, turned[1], turned[2])
    ).astype(BF16)
    hidden_out[:, 256:320] = jnp.where(core == 0, t[2], turned[2])[:, 0:64].astype(BF16)
    stores[1].start()

    def act_block(b):
        def act_step(j, carry):
            x = blocks[b, :, pl.ds(pl.multiple_of(j * 16, 16), 16), :].astype(F32)
            rows = pl.ds(pl.multiple_of(b * 16, 16), 16)
            for n in range(4):
                part = x[:, 8 * (n // 2) : 8 * (n // 2) + 8]
                join = first_halves if n % 2 == 0 else second_halves
                cols = pl.ds(pl.multiple_of(j * 512 + 128 * n, 128), 128)
                acts[rows, cols] = jnp.concatenate(
                    [join(part[0], part[1]), join(part[2], part[3])], axis=0
                ).astype(BF16)
            return carry

        lax.fori_loop(0, 10, act_step, 0)

    for d in (0, 1, 2, 3, 5, 6, 7):
        act_block(lax.rem(y + d, 8))

    for kind in range(2):
        far = around(v if kind == 0 else beside, 2)
        for way in range(2):
            proj_copy(proj_rows(far, 160 * way, 160), proj_xx.at[way, kind], mate).wait_recv()
        proj_copy(proj_rows(far), proj_m, mate).start()

    for e in (1, 3, 2):
        ring_next(4, e)
    act_block(lax.rem(y + 4, 8))
    wait_recv(proj.at[pl.ds(0, 2560)], proj_m)

    def og_step(j, acc):
        cols = pl.ds(pl.multiple_of(j * 1024, 1024), 1024)
        return acc + jnp.dot(acts[:, cols], proj[cols, :], preferred_element_type=F32)

    out = lax.fori_loop(0, 5, og_step, jnp.zeros((ROWS, STACK), F32)).astype(BF16)
    out_grad = jnp.concatenate([out[:, 0:128], out[:, 128:256], out[:, 256:384]], axis=0)

    def dkvm_copy(n, m):
        return remote(dkv_give.at[n, m], dkv_mate.at[n, m], dkvm_s, dkvm_r.at[n, m], vocab=mate)

    def share(n, m, part):
        first, second = part[0:128], part[128:256]
        dkv_own[n, m] = jnp.where(core == 0, first, second)
        dkv_give[n, m] = jnp.where(core == 0, second, first).astype(BF16)
        dkvm_copy(n, m).start()

    def pass_on(n, m):
        dkvm_copy(n, m).wait_recv()
        dkv_sum[n, m] = (dkv_own[n, m] + dkv_mate[n, m].astype(F32)).astype(BF16)

    def dkv_copy(n, m):
        return remote(
            dkv_sum.at[n, m], dkv_recv.at[n, chip], dkv_s, dkv_r.at[n], vocab=2 * m + core
        )

    def send_on(n, m):
        pass_on(n, m)
        dkv_copy(n, m).start()

    def value_pass(d, carry):
        m = lax.rem(chip + d, 8)
        keys = pl.ds(pl.multiple_of(m * 256, 256), 256)
        share(1, m, jnp.dot(probs_low[keys, :], out_grad, preferred_element_type=F32))

        @pl.when(d > 4)
        def _():
            send_on(1, lax.rem(chip + d + 4, 8))

        return carry

    lax.fori_loop(1, 9, value_pass, 0)

    delta = jnp.zeros((1, STACK), F32)
    for m in range(4):
        keys = slice(512 * m, 512 * m + 512)
        x = dot_nt(kv[1, 2 * m : 2 * m + 2].reshape(512, HEAD), out_grad)
        prob_grad[keys, :] = x
        delta = delta + jnp.sum(probs_low[keys, :].astype(F32) * x, axis=0, keepdims=True)

    def key_pass(d, carry):
        m = lax.rem(chip + d, 8)
        keys = pl.ds(pl.multiple_of(m * 256, 256), 256)

        @pl.when(d < 4)
        def _():
            send_on(1, lax.rem(chip + d + 4, 8))

        ds_low = (scores[keys, :] * (prob_grad[keys, :] - delta)).astype(BF16)
        score_grad[keys, :] = ds_low
        share(0, m, jnp.dot(ds_low, query_rows[...], preferred_element_type=F32) * SCALE)

        @pl.when(d > 3)
        def _():
            send_on(0, lax.rem(chip + d + 5, 8))

        return carry

    lax.fori_loop(1, 9, key_pass, 0)
    for d in (6, 7):
        send_on(0, lax.rem(chip + d, 8))

    dq = dot_tn(score_grad[...], kv[0].reshape(KEYS, HEAD)) * SCALE
    t0, t1, t2 = [dq[128 * j : 128 * j + 128].reshape(16, 8, 128) for j in range(3)]
    dq_send[:, 0] = jnp.concatenate([first_halves(t0, t1), t2], axis=1).astype(BF16)
    dq_send[:, 1] = jnp.concatenate([second_halves(t0, t1), turn(t2)], axis=1).astype(BF16)

    @pl.loop(1, SEQ)
    def _(d):
        p = lax.rem(s + d, SEQ)
        at = lax.rem(p, 8) * 4 + p // 8
        remote(dq_send.at[at // 2, lax.rem(at, 2)], dq_recv.at[s], dq_s, dq_r, seq=p).start()

    dq_recv[s] = dq_send[slot // 2, lax.rem(slot, 2)]

    for n in range(2):
        pass_on(n, chip)
        dkv_recv[n, chip] = dkv_sum[n, chip]
    wait_recv(dkv_recv.at[1, pl.ds(0, 7)], dkv_r.at[1])
    values_sum = jnp.sum(dkv_recv[1].astype(F32), axis=0).reshape(16, 8, 128)
    wait_recv(dkv_recv.at[0, pl.ds(0, 7)], dkv_r.at[0])
    keys_sum = jnp.sum(dkv_recv[0].astype(F32), axis=0).reshape(16, 8, 128)
    fold_send[:, 0] = first_halves(keys_sum, values_sum)
    fold_send[:, 1] = second_halves(keys_sum, values_sum)

    @pl.loop(1, SEQ)
    def _(d):
        p = lax.rem(s + d, SEQ)
        at = lax.rem(p, 8) * 4 + p // 8
        remote(fold_send.at[at // 2, lax.rem(at, 2)], fold_recv.at[s], fold_s, fold_r, seq=p).start()

    fold_recv[s] = fold_send[slot // 2, lax.rem(slot, 2)]

    wait_send(stat_recv.at[pl.ds(0, VOC - 1)], stat_s)
    for i in range(2):
        mate_copy(i).wait_send()
    wait_send(part_recv.at[pl.ds(0, 7)], part_s)
    wait_send(slice_recv.at[pl.ds(0, VOC - 1)], slice_s)
    wait_send(kv_recv.at[pl.ds(0, SEQ - 1)], kv1_s)
    wait_send(query_recv.at[pl.ds(0, SEQ - 1)], q_s)
    wait_send(kv.at[:, pl.ds(0, 7), 0], kv_s)
    wait_send(kv.at[:, :, core], kvm_s)
    wait_send(proj.at[pl.ds(0, 15 * 320)], proj_s)
    wait_send(blocks.at[0, pl.ds(0, 3)], z_s)
    wait_send(blocks.at[pl.ds(0, 7)], ring_s)
    wait_send(dkv_mate, dkvm_s)
    wait_send(dkv_recv.at[:, pl.ds(0, 7)], dkv_s)
    wait_send(dq_recv.at[pl.ds(0, SEQ - 1)], dq_s)

    wait_recv(dq_recv.at[pl.ds(0, SEQ - 1)], dq_r)
    for t in range(SEQ):
        x = dq_recv[t].astype(F32)
        for j in range(GROUP_HEADS):
            lane = (GROUP_HEADS * t + j) * HEAD
            query_out[:, lane : lane + HEAD] = x[4 * j : 4 * j + 4].astype(BF16)
    stores[2].start()

    wait_send(fold_recv.at[pl.ds(0, SEQ - 1)], fold_s)
    wait_recv(fold_recv.at[pl.ds(0, SEQ - 1)], fold_r)
    for k in range(8):
        x = jnp.sum(fold_recv[4 * k : 4 * k + 4], axis=0)
        kv_out[0, :, k * HEAD : k * HEAD + HEAD] = x[0:4].astype(BF16)
        kv_out[1, :, k * HEAD : k * HEAD + HEAD] = x[4:8].astype(BF16)
    stores[3].start()
    for copy in stores:
        copy.wait()


def scratch():
    v = pltpu.VMEM
    dma = pltpu.SemaphoreType.DMA
    buffers = [
        v((TOK, D), BF16), v((1, D), F32), v((256, D), BF16), v((1, TOK), jnp.int32),
        v((4, 12288), BF16), v((2, 4, 1024), BF16),
        v((1, TOK), F32), v((TOK, 320), BF16), v((4, 12288), BF16), v((2, 4, 1024), BF16),
        v((256, TOK), F32), v((8, 128), F32), v((VOC, 8, 128), F32),
        v((2, 8, 160, 128), BF16), v((8, 160, 128), BF16), v((8, 160, 128), BF16), v((8, 160, 128), BF16),
        v((160, 128), F32), v((160, 128), F32), v((176, 128), BF16),
        v((VOC, 32, 128), BF16), v((8, TOK, 128), F32),
        v((8, 4, 160, 128), BF16), v((ROWS, D), BF16), v((D, STACK), BF16),
        v((SEQ, 16, 128), F32), v((SEQ, 16, 128), BF16), v((SEQ, 16, 128), BF16), v((STACK, 128), BF16),
        v((8, 8, 128), F32), v((SEQ, 8, 128), F32), v((2, 8, 2, ROWS, 128), BF16),
        v((KEYS, STACK), F32), v((KEYS, STACK), BF16), v((KEYS, STACK), F32), v((KEYS, STACK), BF16),
        v((16, 2, 16, 128), BF16), v((SEQ, 16, 128), BF16),
        v((2, 8, ROWS, 128), F32), v((2, 8, ROWS, 128), BF16), v((2, 8, ROWS, 128), BF16),
        v((2, 8, ROWS, 128), BF16), v((2, 8, ROWS, 128), BF16),
        v((16, 2, 8, 128), F32), v((SEQ, 8, 128), F32),
    ]
    sizes = [
        (8,), (4,), None, None, (2,), (2,), None, (2,), None, None, None, (4,), None, (2, 4, 4),
        None, None, (2, 2), (2, 2), None, None, None, None, None, None, None, (2, 2), (2, 2), None, None,
        None, None, None, (2, 8), None, (2,), None, None,
    ]
    return buffers + [dma if n is None else dma(n) for n in sizes]


def store(*refs):
    sems = refs[12]
    for first, second in ((0, 8), (8, 4)):
        copies = [pltpu.make_async_copy(refs[first + i], refs[second + i], sems.at[i]) for i in range(4)]
        for copy in copies:
            copy.start()
        for copy in copies:
            copy.wait()


def shards(hidden, norm_gain, head_weight, targets, out_proj, query, saved_key_value, offset):
    hbm = pl.BlockSpec(memory_space=pltpu.HBM)
    outs = (
        jax.ShapeDtypeStruct((1, TOK), F32),
        jax.ShapeDtypeStruct((TOK, 320), BF16),
        jax.ShapeDtypeStruct(query.shape, BF16),
        jax.ShapeDtypeStruct(saved_key_value.shape, BF16),
    )
    results = pl.pallas_call(
        body,
        out_shape=outs,
        in_specs=[hbm] * 7 + [pl.BlockSpec(memory_space=pltpu.SMEM)],
        out_specs=(hbm,) * 4,
        scratch_shapes=scratch(),
        compiler_params=pltpu.CompilerParams(
            collective_id=0, has_side_effects=True, vmem_limit_bytes=VMEM_BYTES
        ),
    )(
        hidden, norm_gain.reshape(1, D), head_weight, targets.reshape(1, TOK), out_proj.T, query,
        saved_key_value, offset,
    )
    loss, hidden_grad, query_grad, kv_grad = pl.pallas_call(
        store,
        out_shape=outs,
        in_specs=[hbm] * 4,
        out_specs=(hbm,) * 4,
        scratch_shapes=[pltpu.VMEM(x.shape, x.dtype) for x in outs] + [pltpu.SemaphoreType.DMA((4,))],
        compiler_params=pltpu.CompilerParams(vmem_limit_bytes=VMEM_BYTES),
    )(*results)
    return loss.reshape(TOK), hidden_grad, query_grad, kv_grad


def solution(mesh):
    in_specs = (
        P("seq", None),
        P(),
        P("vocab", None),
        P("seq"),
        P("seq", "vocab"),
        P(("seq", "vocab"), None),
        P(None, ("seq", "vocab"), None),
        P(),
    )
    out_specs = (
        P("seq"),
        P("seq", "vocab"),
        P(("seq", "vocab"), None),
        P(None, ("seq", "vocab"), None),
    )
    return jax.shard_map(shards, mesh=mesh, in_specs=in_specs, out_specs=out_specs, check_vma=False)
```

```python
import jax
import jax.numpy as jnp
from jax import lax
from jax.experimental import pallas as pl
from jax.experimental.pallas import tpu as pltpu
from jax.sharding import PartitionSpec as P

D = 5120
HEAD = 128
SEQ = 32
VOC = 16
TOK = 64
GROUP_HEADS = 3
ROWS = 128
STACK = GROUP_HEADS * ROWS
KEYS = 2048
EPS = 1e-05
LOSS_SCALE = 32.0
MASKED = -1e30
VMEM_BYTES = 62 * 2**20
SCALE = HEAD ** (-0.5)
MESH = pl.DeviceIdType.MESH
F32 = jnp.float32
BF16 = jnp.bfloat16


def remote(src, dst, send_sem, recv_sem, **device):
    return pltpu.make_async_remote_copy(
        src_ref=src,
        dst_ref=dst,
        send_sem=send_sem,
        recv_sem=recv_sem,
        device_id=device,
        device_id_type=MESH,
    )


def low_rows(shape):
    return lax.broadcasted_iota(jnp.int32, shape, len(shape) - 2) < 4


def turn(x):
    return pltpu.roll(x, 4, len(x.shape) - 2)


def first_halves(a, b):
    return jnp.where(low_rows(a.shape), a, turn(b))


def second_halves(a, b):
    return jnp.where(low_rows(a.shape), turn(a), b)


def dot_nt(a, b):
    return lax.dot_general(a, b, (((1,), (1,)), ((), ())), preferred_element_type=F32)


def dot_tn(a, b):
    return lax.dot_general(a, b, (((0,), (0,)), ((), ())), preferred_element_type=F32)


def body(
    hidden_in, gain_in, weight_in, targets_in, proj_in, query_in, key_value_in, offset,
    loss_res, hidden_res, query_res, kv_res,
    hidden, gain, weight, targets, query, key_value, loss_out, hidden_out, query_out, kv_out,
    grad_rows, part_raw, stat_send, stat_recv, part_send, part_mate, part_sum, part_recv,
    blocks, proj, proj_ends, og_own, og_give, og_mate, og_sum, og_recv,
    query_wide, query_send, queryz_recv, query_recv, query_rows, kv_wide, kvz_send, kvz_recv, kvy_send, kvy_recv, kv,
    scores, probs_low, prob_grad, score_grad,
    dq_send, dqy_recv, dq_recv, dkv_own, dkv_give, dkv_mate, dkv_sum, dkv_recv, foldy_send, foldy_recv, foldz_send, foldz_recv,
    in_s, out_s, stat_s, stat_r, mate_s, mate_r, part_s, part_r, z_s, z_r, ring_s, ring_r,
    ogm_s, ogm_r, og_s, og_r, qz_s, qz_r, q_s, q_r, kvz_s, kvz_r, kvy_s, kvy_r, kv_s, kv_z, kv_x, kv_xx, kvm_r,
    dqy_s, dqy_r, dq_s, dq_r, dkvm_s, dkvm_r, dkv_s, dkv_r, foldy_s, foldy_r, foldz_s, foldz_r,
):
    s = lax.axis_index("seq")
    v = lax.axis_index("vocab")
    h, y = s // 8, lax.rem(s, 8)
    chip, core = v // 2, lax.rem(v, 2)
    mate = v + 1 - 2 * core
    beside = v + 2 - 4 * lax.rem(chip, 2)

    def around(block, steps):
        return lax.rem(block + 4 * steps, VOC)

    def wait_recv(ref, sem):
        remote(ref, ref, sem, sem, vocab=mate).wait_recv()

    def wait_send(ref, sem):
        remote(ref, ref, sem, sem, vocab=mate).wait_send()

    loads = [
        pltpu.make_async_copy(src, dst, in_s.at[i])
        for i, (src, dst) in enumerate(
            [
                (hidden_in, hidden), (gain_in, gain), (targets_in, targets),
                (weight_in.at[:, 0:2560], weight.at[:, 0:2560]),
                (weight_in.at[:, 2560:5120], weight.at[:, 2560:5120]),
                (query_in, query), (key_value_in, key_value), (proj_in, proj),
            ]
        )
    ]
    for load in loads:
        load.start()
    barrier = pltpu.get_barrier_semaphore()

    def z_peer(d):
        return lax.rem(h + d, 4)

    def y_peer(d):
        return lax.rem(y + d, 8)

    for d in (2, 1, 3):
        pl.semaphore_signal(
            barrier, inc=1, device_id={"seq": z_peer(d) * 8 + y}, device_id_type=MESH
        )
    for d in (4, 3, 5, 2, 6, 1, 7):
        pl.semaphore_signal(
            barrier, inc=1, device_id={"seq": h * 8 + y_peer(d)}, device_id_type=MESH
        )

    @pl.loop(1, VOC)
    def _(d):
        pl.semaphore_signal(
            barrier, inc=1, device_id={"vocab": lax.rem(v + d, VOC)}, device_id_type=MESH
        )

    stores = [
        pltpu.make_async_copy(src, dst, out_s.at[i])
        for i, (src, dst) in enumerate(
            [(loss_out, loss_res), (hidden_out, hidden_res), (query_out, query_res), (kv_out, kv_res)]
        )
    ]

    def square(j, acc):
        x = hidden[:, pl.ds(pl.multiple_of(j * 512, 512), 512)].astype(F32)
        x = x * x
        return acc + (x[:, :128] + x[:, 128:256]) + (x[:, 256:384] + x[:, 384:])

    loads[0].wait()
    squares = lax.fori_loop(0, 10, square, jnp.zeros((TOK, 128), F32))
    inv_rms = lax.rsqrt(jnp.sum(squares, axis=1, keepdims=True) / D + EPS)
    loads[1].wait()
    loads[3].wait()

    def logit_step(j, acc):
        cols = pl.ds(pl.multiple_of(j * 1280, 1280), 1280)
        normed = (hidden[:, cols].astype(F32) * inv_rms * gain[:, cols]).astype(BF16)
        return acc + dot_nt(weight[:, cols], normed)

    logits = lax.fori_loop(0, 2, logit_step, jnp.zeros((256, TOK), F32))
    loads[4].wait()
    logits = lax.fori_loop(2, 4, logit_step, logits)
    loads[2].wait()
    hit = (v * 256 + lax.broadcasted_iota(jnp.int32, (256, TOK), 0)) == targets[...]
    peak = jnp.max(logits, axis=0, keepdims=True)
    raised = jnp.exp(logits - peak)
    stat_send[...] = jnp.zeros((8, 128), F32)
    stat_send[0:1, 0:TOK] = peak
    stat_send[1:2, 0:TOK] = jnp.sum(raised, axis=0, keepdims=True)
    stat_send[2:3, 0:TOK] = jnp.sum(raised * (logits - peak), axis=0, keepdims=True)
    stat_send[3:4, 0:TOK] = jnp.sum(jnp.where(hit, logits, 0.0), axis=0, keepdims=True)
    stat_recv[v] = stat_send[...]
    grad_rows[:, 0:TOK] = raised.astype(BF16)
    grad_rows[:, TOK : 2 * TOK] = hit.astype(F32).astype(BF16)

    for load in loads[5:]:
        load.wait()
    query_wide[...] = jnp.zeros(query_wide.shape, F32)
    for t in range(SEQ):
        for j in range(GROUP_HEADS):
            lane = (GROUP_HEADS * t + j) * HEAD
            query_wide[t, 4 * j : 4 * j + 4, :] = query[:, lane : lane + HEAD].astype(F32)
    query_send[...] = query_wide[...].astype(BF16).reshape(query_send.shape)
    for k in range(8):
        kv_wide[k // 2, 8 * (k % 2) : 8 * (k % 2) + 4, :] = key_value[
            0, :, k * HEAD : k * HEAD + HEAD
        ].astype(F32)
        kv_wide[k // 2, 8 * (k % 2) + 4 : 8 * (k % 2) + 8, :] = key_value[
            1, :, k * HEAD : k * HEAD + HEAD
        ].astype(F32)
    kvz_send[...] = kv_wide[...].astype(BF16)

    pl.semaphore_wait(barrier, 3 + 7 + VOC - 1)

    @pl.loop(1, VOC)
    def _(d):
        remote(stat_send, stat_recv.at[v], stat_s, stat_r, vocab=lax.rem(v + d, VOC)).start()

    for d in (1, 3, 2):
        remote(
            kvz_send.at[z_peer(d)], kvz_recv.at[h], kvz_s, kvz_r, seq=z_peer(d) * 8 + y
        ).start()
    kvz_recv[h] = kvz_send[h]

    proj_ends[...] = jnp.zeros(proj_ends.shape, BF16)
    proj_ends[0, 0:64, :] = proj[256:320, :]
    proj_ends[1, 64:128, :] = proj[256:320, :]
    left = lax.broadcasted_iota(jnp.int32, (1, 128), 1) < 64

    def half_turn(x):
        return pltpu.roll(x, 64, 1)

    def shifted(a, b, c):
        a, b, c = half_turn(a), half_turn(b), half_turn(c)
        return jnp.where(left, a, b), jnp.where(left, b, c), c

    def packed(a, b, c):
        return jnp.concatenate([a, b, jnp.where(left, c[0:32], half_turn(c[32:64]))], axis=0)

    def own_columns(ref):
        first = 128 * ((5 * v) // 2)
        t = [
            ref[:, pl.ds(pl.multiple_of(first + 128 * i, 128), 128)].astype(F32) for i in range(3)
        ]
        t = [jnp.broadcast_to(x, (TOK, 128)) for x in t]
        return [jnp.where(core == 0, a, b) for a, b in zip(t, shifted(*t))]

    def raw_step(j, carry):
        cols = pl.ds(pl.multiple_of(j * 1280, 1280), 1280)
        part_raw[:, cols] = dot_tn(grad_rows[...], weight[:, cols])
        return carry

    lax.fori_loop(0, 4, raw_step, 0)
    wait_recv(stat_recv.at[pl.ds(0, VOC - 1)], stat_r)
    stats = stat_recv[...]
    peaks = stats[:, 0, 0:TOK]
    row_peak = jnp.max(peaks, axis=0, keepdims=True)
    factor = jnp.exp(peaks - row_peak)
    row_total = jnp.sum(stats[:, 1, 0:TOK] * factor, axis=0, keepdims=True)
    weighted = jnp.sum(
        factor * (stats[:, 2, 0:TOK] + stats[:, 1, 0:TOK] * (peaks - row_peak)),
        axis=0, keepdims=True,
    )
    target_logit = jnp.sum(stats[:, 3, 0:TOK], axis=0, keepdims=True)
    loss_out[...] = jnp.log(row_total) + row_peak - target_logit
    stores[0].start()
    tilt = weighted / row_total + (row_peak - target_logit)
    eye = lax.broadcasted_iota(jnp.int32, (TOK, TOK), 0) == lax.broadcasted_iota(
        jnp.int32, (TOK, TOK), 1
    )

    def column(row):
        return jnp.sum(
            jnp.where(eye, jnp.broadcast_to(row, (TOK, TOK)), 0.0), axis=1, keepdims=True
        )

    tilt = inv_rms * inv_rms * column(tilt) * (LOSS_SCALE / D)
    grad_scale = column(LOSS_SCALE * jnp.exp(peak - row_peak) / row_total)

    wait_recv(kvz_recv.at[pl.ds(0, 3)], kvz_r)
    both = kvz_recv[...].astype(F32).reshape(4, 2, 8, 128)
    for i in range(2):
        kvy_send[i] = both[:, i].reshape(32, 128).astype(BF16)
    for d in (4, 3, 5, 2, 6, 1, 7):
        remote(
            kvy_send.at[y_peer(d) // 4], kvy_recv.at[y], kvy_s, kvy_r, seq=h * 8 + y_peer(d)
        ).start()
    kvy_recv[y] = kvy_send[y // 4]
    for d in (2, 1, 3):
        remote(
            query_send.at[z_peer(d)], queryz_recv.at[h], qz_s, qz_r, seq=z_peer(d) * 8 + y
        ).start()
    queryz_recv[h] = query_send[h]

    def part_chip(j):
        return 2 * lax.rem(chip // 2 + 1 + j // 2, 4) + lax.rem(j, 2)

    def part_step(j, carry):
        cols = pl.ds(pl.multiple_of(part_chip(2 * j) * 640, 1280), 1280)
        out = grad_scale * part_raw[0:TOK, cols] - LOSS_SCALE * part_raw[TOK : 2 * TOK, cols]
        t = [out[:, 128 * i : 128 * i + 128] for i in range(10)]
        for i in range(2):
            u = t[5 * i : 5 * i + 5]
            part_send[0, 2 * j + i] = packed(u[0], u[1], u[2]).astype(BF16)
            part_send[1, 2 * j + i] = packed(*shifted(u[2], u[3], u[4])).astype(BF16)
        return carry

    def mate_copy(i):
        half = pl.ds(4 * i, 4)
        return remote(
            part_send.at[1 - core, half], part_mate.at[half], mate_s.at[i], mate_r.at[i], vocab=mate
        )

    for i in range(2):
        lax.fori_loop(2 * i, 2 * i + 2, part_step, 0)
        mate_copy(i).start()

    for i in range(2):
        mate_copy(i).wait_recv()
        for j in range(4 * i, 4 * i + 4):
            part_sum[j] = (part_send[core, j].astype(F32) + part_mate[j].astype(F32)).astype(BF16)

            @pl.when(part_chip(j) != chip)
            def _():
                remote(
                    part_sum.at[j], part_recv.at[chip], part_s, part_r,
                    vocab=2 * part_chip(j) + core,
                ).start()

    part_recv[chip] = part_sum[6 + lax.rem(chip, 2)]

    wait_recv(kvy_recv.at[pl.ds(0, 7)], kvy_r)
    pairs = kvy_recv[...].astype(F32).reshape(16, 2, 8, 128)
    kv[0, chip, core] = first_halves(pairs[:, 0], pairs[:, 1]).reshape(ROWS, 128).astype(BF16)
    kv[1, chip, core] = second_halves(pairs[:, 0], pairs[:, 1]).reshape(ROWS, 128).astype(BF16)

    def kv_copy(block, sem, to, kinds=slice(0, 2)):
        at = kv.at[kinds, block // 2, lax.rem(block, 2)]
        return remote(at, at, kv_s, sem, vocab=to)

    kv_copy(v, kv_z, beside).start()
    for way in range(2):
        kv_copy(v, kv_x.at[way, 0], around(v, 1 + 2 * way)).start()
    kv_copy(v, kvm_r, mate).start()

    wait_recv(queryz_recv.at[pl.ds(0, 3)], qz_r)
    for d in (4, 3, 5, 2, 6, 1, 7):
        remote(
            queryz_recv.at[:, y_peer(d)], query_recv.at[y], q_s, q_r, seq=h * 8 + y_peer(d)
        ).start()
    query_recv[y] = queryz_recv[:, y]

    gains, rows = own_columns(gain), own_columns(hidden)
    wait_recv(part_recv.at[pl.ds(0, 7)], part_r)
    total = jnp.sum(part_recv[...].astype(F32), axis=0)
    ends = total[128:160]
    totals = [total[0:64], total[64:128], jnp.concatenate([ends, half_turn(ends)], axis=0)]
    grads = [inv_rms * g * t - x * tilt for g, t, x in zip(gains, totals, rows)]
    blocks[y, h] = packed(*grads).astype(BF16)

    def z_copy(d, target, origin):
        at = blocks.at[y, origin]
        return remote(at, at, z_s, z_r.at[d], seq=target * 8 + y)

    for d in (1, 3, 2):
        z_copy(d, lax.rem(h + d, 4), h).start()

    def ring_copy(way, k, e, block):
        to = lax.rem(y + 1 + 6 * way, 8)
        at = blocks.at[block, lax.rem(h + e, 4)]
        return remote(at, at, ring_s, ring_r.at[way, k, e], seq=h * 8 + to)

    def sent(way, k):
        return lax.rem(y + (8 - k if way == 0 else k), 8)

    def got(way, k):
        return lax.rem(y + (7 - k if way == 0 else k + 1), 8)

    def goes(way, k, e):
        return k < 3 or (e < 2) == (way == 0)

    for way in range(2):
        ring_copy(way, 0, 0, y).start()

    hidden_out[:, 0:128] = grads[0].astype(BF16)
    hidden_out[:, 128:256] = grads[1].astype(BF16)
    hidden_out[:, 256:320] = grads[2][:, 0:64].astype(BF16)
    stores[1].start()

    def kv_next(kind):
        block = v if kind == 0 else beside
        for way in range(2):
            here = around(block, 3 - 2 * way)
            kv_copy(here, kv_x.at[way, kind], mate).wait_recv()
            kv_copy(here, kv_xx.at[way, kind], around(v, 1 + 2 * way), slice(way, way + 1)).start()
            kv_copy(here, kvm_r, mate).start()

    def kv_last(kind):
        far = around(v if kind == 0 else beside, 2)
        for way in range(2):
            kv_copy(far, kv_xx.at[way, kind], mate, slice(way, way + 1)).wait_recv()
        kv_copy(far, kvm_r, mate).start()

    def ring_start(e):
        z_copy(4 - e, h, lax.rem(h + e, 4)).wait_recv()
        for way in range(2):
            ring_copy(way, 0, e, y).start()

    def ring_next(k, e):
        for way in range(2):
            if goes(way, k - 1, e):
                ring_copy(way, k - 1, e, got(way, k - 1)).wait_recv()
            if k < 4 and goes(way, k, e):
                ring_copy(way, k, e, sent(way, k)).start()

    kv_copy(beside, kv_z, mate).wait_recv()
    for way in range(2):
        kv_copy(beside, kv_x.at[way, 1], around(v, 1 + 2 * way)).start()
    kv_copy(beside, kvm_r, mate).start()
    kv_next(0)
    ring_next(1, 0)
    ring_start(1)
    ring_start(3)
    kv_next(1)
    ring_next(2, 0)
    ring_start(2)
    kv_last(0)

    def og_copy(j, b):
        return remote(og_give.at[b], og_mate.at[b], ogm_s, ogm_r.at[j], vocab=mate)

    def og_block(j, b):
        x = blocks[b]
        out = jnp.dot(x[:, 0:64].reshape(256, 128), proj[0:128, :], preferred_element_type=F32)
        out += jnp.dot(x[:, 64:128].reshape(256, 128), proj[128:256, :], preferred_element_type=F32)
        ends = x[:, 128:160].reshape(128, 128)
        ends = [
            jnp.dot(ends, proj_ends[i], preferred_element_type=F32).reshape(4, 32, STACK)
            for i in range(2)
        ]
        out = out.reshape(4, 64, STACK) + jnp.concatenate(ends, axis=1)
        out = [out[i].reshape(8, 8, STACK) for i in range(4)]
        even = jnp.concatenate([first_halves(out[0], out[1]), first_halves(out[2], out[3])], axis=1)
        odd = jnp.concatenate([second_halves(out[0], out[1]), second_halves(out[2], out[3])], axis=1)
        og_own[b] = jnp.where(core == 0, even, odd)
        og_give[b] = jnp.where(core == 0, odd, even).astype(BF16)
        og_copy(j, b).start()

    def og_pass(j, b):
        og_copy(j, b).wait_recv()
        og_sum[b] = (og_own[b] + og_mate[b].astype(F32)).astype(BF16)

        @pl.loop(1, 8)
        def _(d):
            m = lax.rem(chip + d, 8)
            remote(
                og_sum.at[b, m], og_recv.at[chip, b], og_s, og_r, vocab=2 * m + core
            ).start()

        og_recv[chip, b] = og_sum[b, chip]

    order = [lax.rem(y + d, 8) for d in (0, 7, 1, 6, 2, 5, 3, 4)]

    wait_recv(query_recv.at[pl.ds(0, 7)], q_r)
    pairs = query_recv[...].astype(F32).reshape(16, 2, 16, 128)
    even, odd = pairs[:, 0], pairs[:, 1]
    query_rows[0:128, :] = first_halves(even[:, 0:8], odd[:, 0:8]).reshape(128, 128).astype(BF16)
    query_rows[128:256, :] = second_halves(even[:, 0:8], odd[:, 0:8]).reshape(128, 128).astype(BF16)
    query_rows[256:384, :] = first_halves(even[:, 8:16], odd[:, 8:16]).reshape(128, 128).astype(BF16)

    start = offset[0]
    r = lax.rem(lax.broadcasted_iota(jnp.int32, (1, STACK), 1), ROWS)
    q_place = (lax.rem(r // 4, 4) * 8 + r // 16) * TOK + 4 * v + lax.rem(r, 4)
    r = lax.broadcasted_iota(jnp.int32, (256, 1), 0)
    k_base = (lax.rem(r // 4, 4) * 8 + lax.rem(r // 16, 8)) * TOK + 4 * (r // ROWS) + lax.rem(r, 4)
    q_before = q_place < start

    def score_part(m, top):
        keys = slice(256 * m, 256 * m + 256)
        k_place = k_base + 8 * m
        seen = (k_place <= q_place) & ((k_place >= start) | q_before)
        x = dot_nt(kv[0, m].reshape(256, HEAD), query_rows[...]) * SCALE
        x = jnp.where(seen, x, MASKED)
        scores[keys, :] = x
        return jnp.maximum(top, jnp.max(x, axis=0, keepdims=True))

    def exp_part(m, top, total):
        keys = slice(256 * m, 256 * m + 256)
        x = jnp.exp(scores[keys, :] - top)
        scores[keys, :] = x
        return total + jnp.sum(x, axis=0, keepdims=True)

    def prob_part(m, share):
        keys = slice(256 * m, 256 * m + 256)
        x = scores[keys, :] * share
        scores[keys, :] = x
        probs_low[keys, :] = x.astype(BF16)

    state = {"top": jnp.full((1, STACK), MASKED, F32), "total": jnp.zeros((1, STACK), F32)}

    def piece(n):
        if n < 8:
            state["top"] = score_part(n, state["top"])
        elif n < 16:
            state["total"] = exp_part(n - 8, state["top"], state["total"])
        else:
            if n == 16:
                state["share"] = 1.0 / state["total"]
            prob_part(n - 16, state["share"])

    def pieces(first, last):
        for n in range(first, last):
            piece(n)

    og_block(0, order[0])
    ring_next(1, 1)
    ring_next(1, 3)
    kv_last(1)
    ring_next(3, 0)
    ring_next(1, 2)
    og_block(1, order[1])
    og_block(2, order[2])
    ring_next(2, 1)
    og_pass(0, order[0])
    ring_next(2, 3)
    wait_recv(kv.at[:, :, 1 - core], kvm_r)
    pieces(0, 3)
    ring_next(4, 0)
    ring_next(2, 2)
    og_block(3, order[3])
    og_pass(1, order[1])
    ring_next(3, 1)
    og_block(4, order[4])
    og_pass(2, order[2])
    ring_next(3, 3)
    pieces(3, 7)
    ring_next(3, 2)
    og_block(5, order[5])
    og_pass(3, order[3])
    og_block(6, order[6])
    og_pass(4, order[4])
    ring_next(4, 1)
    ring_next(4, 3)
    pieces(7, 10)
    og_pass(5, order[5])
    ring_next(4, 2)
    og_block(7, order[7])
    og_pass(6, order[6])
    pieces(10, 18)
    og_pass(7, order[7])
    pieces(18, 24)
    wait_recv(og_recv.at[pl.ds(0, 7)], og_r)
    out = jnp.sum(og_recv[...].astype(F32), axis=0).reshape(ROWS, STACK).astype(BF16)
    out_grad = jnp.concatenate([out[:, 0:128], out[:, 128:256], out[:, 256:384]], axis=0)

    def group(j):
        return lax.rem(chip // 2 + 1 + j, 4)

    def group_keys(j):
        return pl.ds(pl.multiple_of(group(j) * 512, 512), 512)

    def dkvm_copy(n, j):
        return remote(dkv_give.at[n, j], dkv_mate.at[n, j], dkvm_s, dkvm_r.at[n, j], vocab=mate)

    def share(n, j, part):
        part = part.reshape(2, 2, ROWS, HEAD)
        first, second = part[:, 0], part[:, 1]
        dkv_own[n, j] = jnp.where(core == 0, first, second)
        dkv_give[n, j] = jnp.where(core == 0, second, first).astype(BF16)
        dkvm_copy(n, j).start()

    def send_on(n, j):
        dkvm_copy(n, j).wait_recv()
        dkv_sum[n, j] = (dkv_own[n, j] + dkv_mate[n, j].astype(F32)).astype(BF16)
        for i in range(2):
            m = 2 * group(j) + i

            @pl.when(m != chip)
            def _():
                remote(
                    dkv_sum.at[n, j, i], dkv_recv.at[n, chip], dkv_s, dkv_r.at[n], vocab=2 * m + core
                ).start()

    def value_pass(j):
        share(1, j, jnp.dot(probs_low[group_keys(j), :], out_grad, preferred_element_type=F32))

    def key_pass(j):
        keys = group_keys(j)
        ds_low = (scores[keys, :] * (prob_grad[keys, :] - delta)).astype(BF16)
        score_grad[keys, :] = ds_low
        share(0, j, jnp.dot(ds_low, query_rows[...], preferred_element_type=F32) * SCALE)

    value_pass(0)
    value_pass(1)
    value_pass(2)
    send_on(1, 0)
    value_pass(3)
    send_on(1, 1)

    delta = jnp.zeros((1, STACK), F32)
    for m in range(4):
        keys = slice(512 * m, 512 * m + 512)
        x = dot_nt(kv[1, 2 * m : 2 * m + 2].reshape(512, HEAD), out_grad)
        prob_grad[keys, :] = x
        delta = delta + jnp.sum(probs_low[keys, :].astype(F32) * x, axis=0, keepdims=True)

    send_on(1, 2)
    send_on(1, 3)
    key_pass(0)
    key_pass(1)
    key_pass(2)
    send_on(0, 0)
    key_pass(3)
    send_on(0, 1)
    send_on(0, 2)

    dq = dot_tn(score_grad[...], kv[0].reshape(KEYS, HEAD)) * SCALE
    send_on(0, 3)
    t0, t1, t2 = [dq[128 * j : 128 * j + 128].reshape(16, 8, 128) for j in range(3)]
    t0 = jnp.concatenate([first_halves(t0, t1), t2, second_halves(t0, t1), turn(t2)], axis=1)
    dq_send[...] = t0.astype(BF16).reshape(dq_send.shape)

    for d in (4, 3, 5, 2, 6, 1, 7):
        remote(
            dq_send.at[y_peer(d)], dqy_recv.at[y], dqy_s, dqy_r, seq=h * 8 + y_peer(d)
        ).start()
    dqy_recv[y] = dq_send[y]

    for n in range(2):
        dkv_recv[n, chip] = dkv_sum[n, 3, lax.rem(chip, 2)]
    wait_recv(dkv_recv.at[1, pl.ds(0, 7)], dkv_r.at[1])
    values_sum = jnp.sum(dkv_recv[1].astype(F32), axis=0).reshape(16, 8, 128)
    wait_recv(dkv_recv.at[0, pl.ds(0, 7)], dkv_r.at[0])
    keys_sum = jnp.sum(dkv_recv[0].astype(F32), axis=0).reshape(16, 8, 128)
    parts = jnp.stack(
        [first_halves(keys_sum, values_sum), second_halves(keys_sum, values_sum)], axis=1
    )
    foldy_send[...] = parts.reshape(8, 32, 128).astype(BF16)
    for d in (4, 3, 5, 2, 6, 1, 7):
        remote(
            foldy_send.at[y_peer(d)], foldy_recv.at[y], foldy_s, foldy_r, seq=h * 8 + y_peer(d)
        ).start()
    foldy_recv[y] = foldy_send[y]

    wait_recv(dqy_recv.at[pl.ds(0, 7)], dqy_r)
    for d in (2, 1, 3):
        remote(
            dqy_recv.at[:, z_peer(d)], dq_recv.at[h], dq_s, dq_r, seq=z_peer(d) * 8 + y
        ).start()
    dq_recv[h] = dqy_recv[:, h]

    wait_send(stat_recv.at[pl.ds(0, VOC - 1)], stat_s)
    for i in range(2):
        mate_copy(i).wait_send()
    wait_send(part_recv.at[pl.ds(0, 7)], part_s)
    wait_send(og_mate, ogm_s)
    wait_send(og_recv.at[pl.ds(0, 7)], og_s)
    wait_send(kvz_recv.at[pl.ds(0, 3)], kvz_s)
    wait_send(kvy_recv.at[pl.ds(0, 7)], kvy_s)
    wait_send(queryz_recv.at[pl.ds(0, 3)], qz_s)
    wait_send(query_recv.at[pl.ds(0, 7)], q_s)
    wait_send(score_grad.at[pl.ds(0, 1280)], kv_s)
    wait_send(blocks.at[0, pl.ds(0, 3)], z_s)
    wait_send(blocks.at[pl.ds(0, 7)], ring_s)
    wait_send(dkv_mate, dkvm_s)
    wait_send(dkv_recv.at[:, pl.ds(0, 7)], dkv_s)
    wait_send(dqy_recv.at[pl.ds(0, 7)], dqy_s)

    def dq_out():
        wait_recv(dq_recv.at[pl.ds(0, 3)], dq_r)
        for t in range(SEQ):
            x = dq_recv[t // 8, t % 8].astype(F32)
            for j in range(GROUP_HEADS):
                lane = (GROUP_HEADS * t + j) * HEAD
                query_out[:, lane : lane + HEAD] = x[4 * j : 4 * j + 4].astype(BF16)
        stores[2].start()

    wait_recv(foldy_recv.at[pl.ds(0, 7)], foldy_r)
    sums = []
    for i in range(2):
        head_sum = jnp.sum(foldy_recv[4 * i : 4 * i + 4].astype(F32), axis=0)
        sums.append(head_sum.reshape(4, 8, 128))
    foldz_send[...] = jnp.concatenate(sums, axis=1).astype(BF16)
    for d in (2, 1, 3):
        remote(
            foldz_send.at[z_peer(d)], foldz_recv.at[h], foldz_s, foldz_r, seq=z_peer(d) * 8 + y
        ).start()
    foldz_recv[h] = foldz_send[h]
    dq_out()
    wait_send(dq_recv.at[pl.ds(0, 3)], dq_s)
    wait_send(foldy_recv.at[pl.ds(0, 7)], foldy_s)
    wait_send(foldz_recv.at[pl.ds(0, 3)], foldz_s)
    wait_recv(foldz_recv.at[pl.ds(0, 3)], foldz_r)
    for k in range(8):
        x = foldz_recv[k // 2].astype(F32)[8 * (k % 2) : 8 * (k % 2) + 8]
        kv_out[0, :, k * HEAD : k * HEAD + HEAD] = x[0:4].astype(BF16)
        kv_out[1, :, k * HEAD : k * HEAD + HEAD] = x[4:8].astype(BF16)
    stores[3].start()
    for copy in stores:
        copy.wait()


def scratch():
    v = pltpu.VMEM
    dma = pltpu.SemaphoreType.DMA
    buffers = [
        v((TOK, D), BF16), v((1, D), F32), v((256, D), BF16), v((1, TOK), jnp.int32),
        v((4, 12288), BF16), v((2, 4, 1024), BF16),
        v((1, TOK), F32), v((TOK, 320), BF16), v((4, 12288), BF16), v((2, 4, 1024), BF16),
        v((256, 2 * TOK), BF16), v((2 * TOK, D), F32), v((8, 128), F32), v((VOC, 8, 128), F32),
        v((2, 8, 160, 128), BF16), v((8, 160, 128), BF16), v((8, 160, 128), BF16), v((8, 160, 128), BF16),
        v((8, 4, 160, 128), BF16), v((320, STACK), BF16), v((2, 128, STACK), BF16),
        v((8, 8, 16, STACK), F32), v((8, 8, 16, STACK), BF16), v((8, 8, 16, STACK), BF16),
        v((8, 8, 16, STACK), BF16), v((8, 8, 16, STACK), BF16),
        v((SEQ, 16, 128), F32), v((4, 8, 16, 128), BF16), v((4, 8, 16, 128), BF16), v((8, 4, 16, 128), BF16),
        v((STACK, 128), BF16),
        v((4, 16, 128), F32), v((4, 16, 128), BF16), v((4, 16, 128), BF16),
        v((2, 32, 128), BF16), v((8, 32, 128), BF16), v((2, 8, 2, ROWS, 128), BF16),
        v((KEYS, STACK), F32), v((KEYS, STACK), BF16), v((KEYS, STACK), F32), v((KEYS, STACK), BF16),
        v((8, 4, 16, 128), BF16), v((8, 4, 16, 128), BF16), v((4, 8, 16, 128), BF16),
        v((2, 4, 2, ROWS, 128), F32), v((2, 4, 2, ROWS, 128), BF16), v((2, 4, 2, ROWS, 128), BF16),
        v((2, 4, 2, ROWS, 128), BF16), v((2, 8, ROWS, 128), BF16),
        v((8, 32, 128), BF16), v((8, 32, 128), BF16), v((4, 16, 128), BF16), v((4, 16, 128), BF16),
    ]
    sizes = [
        (8,), (4,), None, None, (2,), (2,), None, None, None, (4,), None, (2, 4, 4),
        None, (8,), None, None, None, None, None, None, None, None, None, None,
        None, None, (2, 2), (2, 2), None,
        None, None, None, None, None, (2, 4), None, (2,), None, None, None, None,
    ]
    return buffers + [dma if n is None else dma(n) for n in sizes]


def store(*refs):
    sems = refs[12]
    for first, second in ((0, 8), (8, 4)):
        copies = [pltpu.make_async_copy(refs[first + i], refs[second + i], sems.at[i]) for i in range(4)]
        for copy in copies:
            copy.start()
        for copy in copies:
            copy.wait()


def shards(hidden, norm_gain, head_weight, targets, out_proj, query, saved_key_value, offset):
    hbm = pl.BlockSpec(memory_space=pltpu.HBM)
    outs = (
        jax.ShapeDtypeStruct((1, TOK), F32),
        jax.ShapeDtypeStruct((TOK, 320), BF16),
        jax.ShapeDtypeStruct(query.shape, BF16),
        jax.ShapeDtypeStruct(saved_key_value.shape, BF16),
    )
    results = pl.pallas_call(
        body,
        out_shape=outs,
        in_specs=[hbm] * 7 + [pl.BlockSpec(memory_space=pltpu.SMEM)],
        out_specs=(hbm,) * 4,
        scratch_shapes=scratch(),
        compiler_params=pltpu.CompilerParams(
            collective_id=0, has_side_effects=True, vmem_limit_bytes=VMEM_BYTES
        ),
    )(
        hidden, norm_gain.reshape(1, D), head_weight, targets.reshape(1, TOK), out_proj.T, query,
        saved_key_value, offset,
    )
    loss, hidden_grad, query_grad, kv_grad = pl.pallas_call(
        store,
        out_shape=outs,
        in_specs=[hbm] * 4,
        out_specs=(hbm,) * 4,
        scratch_shapes=[pltpu.VMEM(x.shape, x.dtype) for x in outs] + [pltpu.SemaphoreType.DMA((4,))],
        compiler_params=pltpu.CompilerParams(vmem_limit_bytes=VMEM_BYTES),
    )(*results)
    return loss.reshape(TOK), hidden_grad, query_grad, kv_grad


def solution(mesh):
    in_specs = (
        P("seq", None),
        P(),
        P("vocab", None),
        P("seq"),
        P("seq", "vocab"),
        P(("seq", "vocab"), None),
        P(None, ("seq", "vocab"), None),
        P(),
    )
    out_specs = (
        P("seq"),
        P("seq", "vocab"),
        P(("seq", "vocab"), None),
        P(None, ("seq", "vocab"), None),
    )
    return jax.shard_map(shards, mesh=mesh, in_specs=in_specs, out_specs=out_specs, check_vma=False)
```

```python
import jax
import jax.numpy as jnp
from jax import lax
from jax.experimental import pallas as pl
from jax.experimental.pallas import tpu as pltpu
from jax.sharding import PartitionSpec as P

D = 5120
HEAD = 128
SEQ = 32
VOC = 16
TOK = 64
GROUP_HEADS = 3
ROWS = 128
STACK = GROUP_HEADS * ROWS
KEYS = 2048
EPS = 1e-05
LOSS_SCALE = 32.0
MASKED = -1e30
VMEM_BYTES = 62 * 2**20
SCALE = HEAD ** (-0.5)
MESH = pl.DeviceIdType.MESH
F32 = jnp.float32
BF16 = jnp.bfloat16


def remote(src, dst, send_sem, recv_sem, **device):
    return pltpu.make_async_remote_copy(
        src_ref=src,
        dst_ref=dst,
        send_sem=send_sem,
        recv_sem=recv_sem,
        device_id=device,
        device_id_type=MESH,
    )


def low_rows(shape):
    return lax.broadcasted_iota(jnp.int32, shape, len(shape) - 2) < 4


def turn(x):
    return pltpu.roll(x, 4, len(x.shape) - 2)


def first_halves(a, b):
    return jnp.where(low_rows(a.shape), a, turn(b))


def second_halves(a, b):
    return jnp.where(low_rows(a.shape), turn(a), b)


def dot_nt(a, b):
    return lax.dot_general(a, b, (((1,), (1,)), ((), ())), preferred_element_type=F32)


def dot_tn(a, b):
    return lax.dot_general(a, b, (((0,), (0,)), ((), ())), preferred_element_type=F32)


def body(
    hidden_in, gain_in, weight_in, targets_in, proj_in, query_in, key_value_in, offset,
    loss_res, hidden_res, query_res, kv_res,
    hidden, gain, weight, targets, query, key_value, loss_out, hidden_out, query_out, kv_out,
    grad_rows, part_raw, stat_send, stat_recv, part_send, part_mate, part_sum, part_recv,
    blocks, acts, projs, og_own, og_give, og_mate, og_sum, og_recv, ogy_send, ogy_recv,
    query_wide, query_send, queryy_recv, query_recv, query_rows, kv_wide, kvz_send, kvz_recv, kvy_send, kvy_recv, kv,
    scores, probs_low, prob_grad, score_grad,
    dq_send, dqy_recv, dq_recv, dkv_own, dkv_give, dkv_mate, dkv_sum, dkv_recv, foldy_send, foldy_recv, foldz_send, foldz_recv,
    in_s, out_s, stat_s, stat_r, mate_s, mate_r, part_s, part_r, z_s, z_r, proj_s, proj_r,
    ogm_s, ogm_r, og_s, og_r, ogy_s, ogy_r, qy_s, qy_r, q_s, q_r, kvz_s, kvz_r, kvy_s, kvy_r, kv_s, kv_z, kv_x, kv_xx, kvm_r,
    dqy_s, dqy_r, dq_s, dq_r, dkvm_s, dkvm_r, dkv_s, dkv_r, foldy_s, foldy_r, foldz_s, foldz_r,
):
    s = lax.axis_index("seq")
    v = lax.axis_index("vocab")
    h, y = s // 8, lax.rem(s, 8)
    chip, core = v // 2, lax.rem(v, 2)
    mate = v + 1 - 2 * core
    beside = v + 2 - 4 * lax.rem(chip, 2)

    def around(block, steps):
        return lax.rem(block + 4 * steps, VOC)

    def wait_recv(ref, sem):
        remote(ref, ref, sem, sem, vocab=mate).wait_recv()

    def wait_send(ref, sem):
        remote(ref, ref, sem, sem, vocab=mate).wait_send()

    loads = [
        pltpu.make_async_copy(src, dst, in_s.at[i])
        for i, (src, dst) in enumerate(
            [
                (hidden_in, hidden), (gain_in, gain), (targets_in, targets),
                (weight_in.at[:, 0:2560], weight.at[:, 0:2560]),
                (weight_in.at[:, 2560:5120], weight.at[:, 2560:5120]),
                (query_in, query), (key_value_in, key_value), (proj_in, projs.at[y, 0:320]),
            ]
        )
    ]
    for load in loads:
        load.start()
    barrier = pltpu.get_barrier_semaphore()

    def z_peer(d):
        return lax.rem(h + d, 4)

    def y_peer(d):
        return lax.rem(y + d, 8)

    for d in (2, 1, 3):
        pl.semaphore_signal(
            barrier, inc=1, device_id={"seq": z_peer(d) * 8 + y}, device_id_type=MESH
        )
    for d in (4, 3, 5, 2, 6, 1, 7):
        pl.semaphore_signal(
            barrier, inc=1, device_id={"seq": h * 8 + y_peer(d)}, device_id_type=MESH
        )

    @pl.loop(1, VOC)
    def _(d):
        pl.semaphore_signal(
            barrier, inc=1, device_id={"vocab": lax.rem(v + d, VOC)}, device_id_type=MESH
        )

    stores = [
        pltpu.make_async_copy(src, dst, out_s.at[i])
        for i, (src, dst) in enumerate(
            [(loss_out, loss_res), (hidden_out, hidden_res), (query_out, query_res), (kv_out, kv_res)]
        )
    ]

    def square(j, acc):
        x = hidden[:, pl.ds(pl.multiple_of(j * 512, 512), 512)].astype(F32)
        x = x * x
        return acc + (x[:, :128] + x[:, 128:256]) + (x[:, 256:384] + x[:, 384:])

    loads[0].wait()
    squares = lax.fori_loop(0, 10, square, jnp.zeros((TOK, 128), F32))
    inv_rms = lax.rsqrt(jnp.sum(squares, axis=1, keepdims=True) / D + EPS)
    loads[1].wait()
    loads[3].wait()

    def logit_step(j, acc):
        cols = pl.ds(pl.multiple_of(j * 1280, 1280), 1280)
        normed = (hidden[:, cols].astype(F32) * inv_rms * gain[:, cols]).astype(BF16)
        return acc + dot_nt(weight[:, cols], normed)

    logits = lax.fori_loop(0, 2, logit_step, jnp.zeros((256, TOK), F32))
    loads[4].wait()
    logits = lax.fori_loop(2, 4, logit_step, logits)
    loads[2].wait()
    hit = (v * 256 + lax.broadcasted_iota(jnp.int32, (256, TOK), 0)) == targets[...]
    peak = jnp.max(logits, axis=0, keepdims=True)
    raised = jnp.exp(logits - peak)
    stat_send[...] = jnp.zeros((8, 128), F32)
    stat_send[0:1, 0:TOK] = peak
    stat_send[1:2, 0:TOK] = jnp.sum(raised, axis=0, keepdims=True)
    stat_send[2:3, 0:TOK] = jnp.sum(raised * (logits - peak), axis=0, keepdims=True)
    stat_send[3:4, 0:TOK] = jnp.sum(jnp.where(hit, logits, 0.0), axis=0, keepdims=True)
    stat_recv[v] = stat_send[...]
    grad_rows[:, 0:TOK] = raised.astype(BF16)
    grad_rows[:, TOK : 2 * TOK] = hit.astype(F32).astype(BF16)

    for load in loads[5:]:
        load.wait()
    query_wide[...] = jnp.zeros(query_wide.shape, F32)
    for t in range(SEQ):
        for j in range(GROUP_HEADS):
            lane = (GROUP_HEADS * t + j) * HEAD
            query_wide[t % 8 * 4 + t // 8, 4 * j : 4 * j + 4, :] = query[:, lane : lane + HEAD].astype(F32)
    query_send[...] = query_wide[...].astype(BF16).reshape(query_send.shape)
    for k in range(8):
        kv_wide[k // 2, 8 * (k % 2) : 8 * (k % 2) + 4, :] = key_value[
            0, :, k * HEAD : k * HEAD + HEAD
        ].astype(F32)
        kv_wide[k // 2, 8 * (k % 2) + 4 : 8 * (k % 2) + 8, :] = key_value[
            1, :, k * HEAD : k * HEAD + HEAD
        ].astype(F32)
    kvz_send[...] = kv_wide[...].astype(BF16)

    pl.semaphore_wait(barrier, 3 + 7 + VOC - 1)

    @pl.loop(1, VOC)
    def _(d):
        remote(stat_send, stat_recv.at[v], stat_s, stat_r, vocab=lax.rem(v + d, VOC)).start()

    for d in (1, 3, 2):
        remote(
            kvz_send.at[z_peer(d)], kvz_recv.at[h], kvz_s, kvz_r, seq=z_peer(d) * 8 + y
        ).start()
    kvz_recv[h] = kvz_send[h]

    def proj_copy(way, k, f, block):
        at = projs.at[block, 160 * f : 160 * f + 160]
        to = lax.rem(y + 1 + 6 * way, 8)
        return remote(at, at, proj_s, proj_r.at[way, k, f], seq=h * 8 + to)

    def sent(way, k):
        return lax.rem(y + (8 - k if way == 0 else k), 8)

    def got(way, k):
        return lax.rem(y + (7 - k if way == 0 else k + 1), 8)

    def goes(way, k, f):
        return k < 3 or f == way

    def proj_next(k, f):
        for way in range(2):
            if k > 0 and goes(way, k - 1, f):
                proj_copy(way, k - 1, f, got(way, k - 1)).wait_recv()
            if k < 4 and goes(way, k, f):
                proj_copy(way, k, f, sent(way, k)).start()

    proj_next(0, 0)
    proj_next(0, 1)

    left = lax.broadcasted_iota(jnp.int32, (1, 128), 1) < 64

    def half_turn(x):
        return pltpu.roll(x, 64, 1)

    def shifted(a, b, c):
        a, b, c = half_turn(a), half_turn(b), half_turn(c)
        return jnp.where(left, a, b), jnp.where(left, b, c), c

    def packed(a, b, c):
        return jnp.concatenate([a, b, jnp.where(left, c[0:32], half_turn(c[32:64]))], axis=0)

    def own_columns(ref):
        first = 128 * ((5 * v) // 2)
        t = [
            ref[:, pl.ds(pl.multiple_of(first + 128 * i, 128), 128)].astype(F32) for i in range(3)
        ]
        t = [jnp.broadcast_to(x, (TOK, 128)) for x in t]
        return [jnp.where(core == 0, a, b) for a, b in zip(t, shifted(*t))]

    def raw_step(j, carry):
        cols = pl.ds(pl.multiple_of(j * 1280, 1280), 1280)
        part_raw[:, cols] = dot_tn(grad_rows[...], weight[:, cols])
        return carry

    lax.fori_loop(0, 4, raw_step, 0)
    wait_recv(stat_recv.at[pl.ds(0, VOC - 1)], stat_r)
    stats = stat_recv[...]
    peaks = stats[:, 0, 0:TOK]
    row_peak = jnp.max(peaks, axis=0, keepdims=True)
    factor = jnp.exp(peaks - row_peak)
    row_total = jnp.sum(stats[:, 1, 0:TOK] * factor, axis=0, keepdims=True)
    weighted = jnp.sum(
        factor * (stats[:, 2, 0:TOK] + stats[:, 1, 0:TOK] * (peaks - row_peak)),
        axis=0, keepdims=True,
    )
    target_logit = jnp.sum(stats[:, 3, 0:TOK], axis=0, keepdims=True)
    loss_out[...] = jnp.log(row_total) + row_peak - target_logit
    stores[0].start()
    tilt = weighted / row_total + (row_peak - target_logit)
    eye = lax.broadcasted_iota(jnp.int32, (TOK, TOK), 0) == lax.broadcasted_iota(
        jnp.int32, (TOK, TOK), 1
    )

    def column(row):
        return jnp.sum(
            jnp.where(eye, jnp.broadcast_to(row, (TOK, TOK)), 0.0), axis=1, keepdims=True
        )

    tilt = inv_rms * inv_rms * column(tilt) * (LOSS_SCALE / D)
    grad_scale = column(LOSS_SCALE * jnp.exp(peak - row_peak) / row_total)

    wait_recv(kvz_recv.at[pl.ds(0, 3)], kvz_r)
    both = kvz_recv[...].astype(F32).reshape(4, 2, 8, 128)
    for i in range(2):
        kvy_send[i] = both[:, i].reshape(32, 128).astype(BF16)
    for d in (4, 3, 5, 2, 6, 1, 7):
        remote(
            kvy_send.at[y_peer(d) // 4], kvy_recv.at[y], kvy_s, kvy_r, seq=h * 8 + y_peer(d)
        ).start()
    kvy_recv[y] = kvy_send[y // 4]
    for d in (4, 3, 5, 2, 6, 1, 7):
        remote(
            query_send.at[y_peer(d)], queryy_recv.at[y], qy_s, qy_r, seq=h * 8 + y_peer(d)
        ).start()
    queryy_recv[y] = query_send[y]
    def part_chip(j):
        return 2 * lax.rem(chip // 2 + 1 + j // 2, 4) + lax.rem(j, 2)

    def part_step(j, carry):
        cols = pl.ds(pl.multiple_of(part_chip(2 * j) * 640, 1280), 1280)
        out = grad_scale * part_raw[0:TOK, cols] - LOSS_SCALE * part_raw[TOK : 2 * TOK, cols]
        t = [out[:, 128 * i : 128 * i + 128] for i in range(10)]
        for i in range(2):
            u = t[5 * i : 5 * i + 5]
            part_send[0, 2 * j + i] = packed(u[0], u[1], u[2]).astype(BF16)
            part_send[1, 2 * j + i] = packed(*shifted(u[2], u[3], u[4])).astype(BF16)
        return carry

    def mate_copy(i):
        half = pl.ds(4 * i, 4)
        return remote(
            part_send.at[1 - core, half], part_mate.at[half], mate_s.at[i], mate_r.at[i], vocab=mate
        )

    for i in range(2):
        lax.fori_loop(2 * i, 2 * i + 2, part_step, 0)
        mate_copy(i).start()

    portions = [pl.ds(0, 64), pl.ds(64, 96)]

    def part_copy(j, f):
        @pl.when(part_chip(j) != chip)
        def _():
            remote(
                part_sum.at[j, portions[f]], part_recv.at[chip, portions[f]], part_s, part_r.at[f],
                vocab=2 * part_chip(j) + core,
            ).start()

    for i in range(2):
        mate_copy(i).wait_recv()
        for j in range(4 * i, 4 * i + 4):
            part_sum[j] = (part_send[core, j].astype(F32) + part_mate[j].astype(F32)).astype(BF16)

            part_copy(j, 0)

    for j in range(8):
        part_copy(j, 1)
    part_recv[chip] = part_sum[6 + lax.rem(chip, 2)]

    proj_next(1, 0)
    proj_next(1, 1)

    wait_recv(kvy_recv.at[pl.ds(0, 7)], kvy_r)
    pairs = kvy_recv[...].astype(F32).reshape(16, 2, 8, 128)
    kv[0, chip, core] = first_halves(pairs[:, 0], pairs[:, 1]).reshape(ROWS, 128).astype(BF16)
    kv[1, chip, core] = second_halves(pairs[:, 0], pairs[:, 1]).reshape(ROWS, 128).astype(BF16)

    def kv_copy(block, sem, to, kinds=slice(0, 2)):
        at = kv.at[kinds, block // 2, lax.rem(block, 2)]
        return remote(at, at, kv_s, sem, vocab=to)

    kv_copy(v, kv_z, beside).start()
    for way in range(2):
        kv_copy(v, kv_x.at[way, 0], around(v, 1 + 2 * way)).start()
    kv_copy(v, kvm_r, mate).start()


    gains, rows = own_columns(gain), own_columns(hidden)

    def grad(i, total):
        return inv_rms * gains[i] * total - rows[i] * tilt

    def z_copy(f, d, target, origin):
        at = blocks.at[origin, portions[f]]
        return remote(at, at, z_s, z_r.at[f, d], seq=target * 8 + y)

    def kv_next(kind):
        block = v if kind == 0 else beside
        for way in range(2):
            here = around(block, 3 - 2 * way)
            kv_copy(here, kv_x.at[way, kind], mate).wait_recv()
            kv_copy(here, kv_xx.at[way, kind], around(v, 1 + 2 * way), slice(way, way + 1)).start()
            kv_copy(here, kvm_r, mate).start()

    def kv_last(kind):
        far = around(v if kind == 0 else beside, 2)
        for way in range(2):
            kv_copy(far, kv_xx.at[way, kind], mate, slice(way, way + 1)).wait_recv()
        kv_copy(far, kvm_r, mate).start()

    def send_block(f):
        for d in (2, 1, 3):
            z_copy(f, d, lax.rem(h + d, 4), h).start()

    wait_recv(part_recv.at[pl.ds(0, 7), portions[0]], part_r.at[0])
    first_grad = grad(0, jnp.sum(part_recv[:, 0:64].astype(F32), axis=0))
    blocks[h, 0:64, :] = first_grad.astype(BF16)
    send_block(0)
    hidden_out[:, 0:128] = first_grad.astype(BF16)
    wait_recv(part_recv.at[pl.ds(0, 7), portions[1]], part_r.at[1])
    total = jnp.sum(part_recv[:, 64:160].astype(F32), axis=0)
    ends = total[64:96]
    second_grad = grad(1, total[0:64])
    third_grad = grad(2, jnp.concatenate([ends, half_turn(ends)], axis=0))
    blocks[h, 64:160, :] = jnp.concatenate(
        [second_grad, jnp.where(left, third_grad[0:32], half_turn(third_grad[32:64]))], axis=0
    ).astype(BF16)
    send_block(1)
    hidden_out[:, 128:256] = second_grad.astype(BF16)
    hidden_out[:, 256:320] = third_grad[:, 0:64].astype(BF16)
    stores[1].start()

    proj_next(2, 0)
    kv_copy(beside, kv_z, mate).wait_recv()
    for way in range(2):
        kv_copy(beside, kv_x.at[way, 1], around(v, 1 + 2 * way)).start()
    kv_copy(beside, kvm_r, mate).start()
    kv_next(0)
    proj_next(2, 1)
    for f in range(2):
        for d in (1, 3, 2):
            z_copy(f, d, h, lax.rem(h + 4 - d, 4)).wait_recv()
    x = blocks[...]
    ends = x[:, 128:160]
    keep = lax.broadcasted_iota(jnp.int32, ends.shape, 2) < 64
    zero = jnp.zeros_like(ends)
    ends = jnp.concatenate([jnp.where(keep, ends, zero), jnp.where(keep, zero, ends)], axis=1)
    acts[:, 0:128] = x[:, 0:64].reshape(256, 128)
    acts[:, 128:256] = x[:, 64:128].reshape(256, 128)
    acts[:, 256:384] = ends.reshape(256, 128)
    kv_next(1)
    wait_recv(queryy_recv.at[pl.ds(0, 7)], qy_r)
    for d in (2, 1, 3):
        remote(
            queryy_recv.at[:, z_peer(d)], query_recv.at[h], q_s, q_r, seq=z_peer(d) * 8 + y
        ).start()
    query_recv[h] = queryy_recv[:, h]

    def og_copy(j, b):
        return remote(og_give.at[b], og_mate.at[b], ogm_s, ogm_r.at[j], vocab=mate)

    def og_block(j, b):
        projs[b, 320:384, :] = projs[b, 256:320, :]
        out = jnp.dot(acts[...], projs[b], preferred_element_type=F32).reshape(4, 64, STACK)
        out = [out[i].reshape(8, 8, STACK) for i in range(4)]
        even = jnp.concatenate([first_halves(out[0], out[1]), first_halves(out[2], out[3])], axis=1)
        odd = jnp.concatenate([second_halves(out[0], out[1]), second_halves(out[2], out[3])], axis=1)
        og_own[b] = jnp.where(core == 0, even, odd)
        og_give[b] = jnp.where(core == 0, odd, even).astype(BF16)
        og_copy(j, b).start()

    def og_pass(j, b):
        og_copy(j, b).wait_recv()
        og_sum[b] = (og_own[b] + og_mate[b].astype(F32)).astype(BF16)

        @pl.loop(1, 8)
        def _(d):
            m = lax.rem(chip + d, 8)
            remote(
                og_sum.at[b, m], og_recv.at[chip, b], og_s, og_r.at[j], vocab=2 * m + core
            ).start()

        og_recv[chip, b] = og_sum[b, chip]

    def og_done(j, b):
        wait_recv(og_recv.at[pl.ds(0, 7), b], og_r.at[j])
        total = jnp.sum(og_recv[:, b].astype(F32), axis=0).astype(BF16)
        if j == 0:
            ogy_recv[y] = total
        else:
            ogy_send[b] = total
            remote(ogy_send.at[b], ogy_recv.at[y], ogy_s, ogy_r, seq=h * 8 + b).start()

    order = [lax.rem(y + d, 8) for d in (0, 7, 1, 6, 2, 5, 3, 4)]

    def query_step():
        wait_recv(query_recv.at[pl.ds(0, 3)], q_r)
        x = query_recv[...].astype(F32)
        for j in range(GROUP_HEADS):
            part = x[:, :, 8 * (j // 2) : 8 * (j // 2) + 8]
            join = first_halves if j % 2 == 0 else second_halves
            part = jnp.concatenate([join(part[0], part[1]), join(part[2], part[3])], axis=1)
            query_rows[ROWS * j : ROWS * j + ROWS, :] = part.reshape(ROWS, HEAD).astype(BF16)

    start = offset[0]
    r = lax.rem(lax.broadcasted_iota(jnp.int32, (1, STACK), 1), ROWS)
    q_place = (lax.rem(r // 4, 4) * 8 + r // 16) * TOK + 4 * v + lax.rem(r, 4)
    r = lax.broadcasted_iota(jnp.int32, (256, 1), 0)
    k_base = (lax.rem(r // 4, 4) * 8 + lax.rem(r // 16, 8)) * TOK + 4 * (r // ROWS) + lax.rem(r, 4)
    q_before = q_place < start

    def score_part(m, top):
        keys = slice(256 * m, 256 * m + 256)
        k_place = k_base + 8 * m
        seen = (k_place <= q_place) & ((k_place >= start) | q_before)
        x = dot_nt(kv[0, m].reshape(256, HEAD), query_rows[...]) * SCALE
        x = jnp.where(seen, x, MASKED)
        scores[keys, :] = x
        return jnp.maximum(top, jnp.max(x, axis=0, keepdims=True))

    def exp_part(m, top, total):
        keys = slice(256 * m, 256 * m + 256)
        x = jnp.exp(scores[keys, :] - top)
        scores[keys, :] = x
        return total + jnp.sum(x, axis=0, keepdims=True)

    def prob_part(m, share):
        keys = slice(256 * m, 256 * m + 256)
        x = scores[keys, :] * share
        scores[keys, :] = x
        probs_low[keys, :] = x.astype(BF16)

    state = {"top": jnp.full((1, STACK), MASKED, F32), "total": jnp.zeros((1, STACK), F32)}

    def piece(n):
        if n < 8:
            state["top"] = score_part(n, state["top"])
        elif n < 16:
            state["total"] = exp_part(n - 8, state["top"], state["total"])
        else:
            if n == 16:
                state["share"] = 1.0 / state["total"]
            prob_part(n - 16, state["share"])

    def pieces(first, last):
        for n in range(first, last):
            piece(n)

    def pieces(first, last):
        for n in range(first, last):
            piece(n)

    og_block(0, order[0])
    og_block(1, order[1])
    og_block(2, order[2])
    proj_next(3, 0)
    og_pass(0, order[0])
    og_pass(1, order[1])
    og_pass(2, order[2])
    kv_last(0)
    proj_next(3, 1)
    og_block(3, order[3])
    og_block(4, order[4])
    kv_last(1)
    og_block(5, order[5])
    og_pass(3, order[3])
    og_block(6, order[6])
    og_pass(4, order[4])
    wait_recv(kv.at[:, :, 1 - core], kvm_r)
    query_step()
    pieces(0, 4)
    og_pass(5, order[5])
    proj_next(4, 0)
    proj_next(4, 1)
    og_block(7, order[7])
    og_pass(6, order[6])
    pieces(4, 8)
    og_done(0, order[0])
    og_done(1, order[1])
    og_pass(7, order[7])
    og_done(2, order[2])
    pieces(8, 11)
    og_done(3, order[3])
    pieces(11, 14)
    og_done(4, order[4])
    pieces(14, 16)
    og_done(5, order[5])
    pieces(16, 18)
    og_done(6, order[6])
    og_done(7, order[7])
    pieces(18, 24)
    wait_recv(ogy_recv.at[pl.ds(0, 7)], ogy_r)
    out = ogy_recv[...].reshape(ROWS, STACK)
    out_grad = jnp.concatenate([out[:, 0:128], out[:, 128:256], out[:, 256:384]], axis=0)

    def group(j):
        return lax.rem(chip // 2 + 1 + j, 4)

    def group_keys(j):
        return pl.ds(pl.multiple_of(group(j) * 512, 512), 512)

    def dkvm_copy(n, j):
        return remote(dkv_give.at[n, j], dkv_mate.at[n, j], dkvm_s, dkvm_r.at[n, j], vocab=mate)

    def share(n, j, part):
        part = part.reshape(2, 2, ROWS, HEAD)
        first, second = part[:, 0], part[:, 1]
        dkv_own[n, j] = jnp.where(core == 0, first, second)
        dkv_give[n, j] = jnp.where(core == 0, second, first).astype(BF16)
        dkvm_copy(n, j).start()

    def send_on(n, j):
        dkvm_copy(n, j).wait_recv()
        dkv_sum[n, j] = (dkv_own[n, j] + dkv_mate[n, j].astype(F32)).astype(BF16)
        for i in range(2):
            m = 2 * group(j) + i

            @pl.when(m != chip)
            def _():
                remote(
                    dkv_sum.at[n, j, i], dkv_recv.at[n, chip], dkv_s, dkv_r.at[n], vocab=2 * m + core
                ).start()

    def value_pass(j):
        share(1, j, jnp.dot(probs_low[group_keys(j), :], out_grad, preferred_element_type=F32))

    def key_pass(j):
        keys = group_keys(j)
        ds_low = (scores[keys, :] * (prob_grad[keys, :] - delta)).astype(BF16)
        score_grad[keys, :] = ds_low
        share(0, j, jnp.dot(ds_low, query_rows[...], preferred_element_type=F32) * SCALE)

    value_pass(0)
    value_pass(1)
    value_pass(2)
    send_on(1, 0)
    value_pass(3)
    send_on(1, 1)

    delta = jnp.zeros((1, STACK), F32)
    for m in range(4):
        keys = slice(512 * m, 512 * m + 512)
        x = dot_nt(kv[1, 2 * m : 2 * m + 2].reshape(512, HEAD), out_grad)
        prob_grad[keys, :] = x
        delta = delta + jnp.sum(probs_low[keys, :].astype(F32) * x, axis=0, keepdims=True)

    send_on(1, 2)
    send_on(1, 3)
    key_pass(0)
    key_pass(1)
    key_pass(2)
    send_on(0, 0)
    key_pass(3)
    send_on(0, 1)
    send_on(0, 2)

    dq = dot_tn(score_grad[...], kv[0].reshape(KEYS, HEAD)) * SCALE
    send_on(0, 3)
    t0, t1, t2 = [dq[128 * j : 128 * j + 128].reshape(16, 8, 128) for j in range(3)]
    t0 = jnp.concatenate([first_halves(t0, t1), t2, second_halves(t0, t1), turn(t2)], axis=1)
    dq_send[...] = t0.astype(BF16).reshape(dq_send.shape)

    for d in (4, 3, 5, 2, 6, 1, 7):
        remote(
            dq_send.at[y_peer(d)], dqy_recv.at[y], dqy_s, dqy_r, seq=h * 8 + y_peer(d)
        ).start()
    dqy_recv[y] = dq_send[y]

    for n in range(2):
        dkv_recv[n, chip] = dkv_sum[n, 3, lax.rem(chip, 2)]
    wait_recv(dkv_recv.at[1, pl.ds(0, 7)], dkv_r.at[1])
    values_sum = jnp.sum(dkv_recv[1].astype(F32), axis=0).reshape(16, 8, 128)
    wait_recv(dkv_recv.at[0, pl.ds(0, 7)], dkv_r.at[0])
    keys_sum = jnp.sum(dkv_recv[0].astype(F32), axis=0).reshape(16, 8, 128)
    parts = jnp.stack(
        [first_halves(keys_sum, values_sum), second_halves(keys_sum, values_sum)], axis=1
    )
    foldy_send[...] = parts.reshape(8, 32, 128).astype(BF16)
    for d in (4, 3, 5, 2, 6, 1, 7):
        remote(
            foldy_send.at[y_peer(d)], foldy_recv.at[y], foldy_s, foldy_r, seq=h * 8 + y_peer(d)
        ).start()
    foldy_recv[y] = foldy_send[y]

    wait_recv(dqy_recv.at[pl.ds(0, 7)], dqy_r)
    for d in (2, 1, 3):
        remote(
            dqy_recv.at[:, z_peer(d)], dq_recv.at[h], dq_s, dq_r, seq=z_peer(d) * 8 + y
        ).start()
    dq_recv[h] = dqy_recv[:, h]

    wait_send(stat_recv.at[pl.ds(0, VOC - 1)], stat_s)
    for i in range(2):
        mate_copy(i).wait_send()
    wait_send(part_recv.at[pl.ds(0, 7)], part_s)
    wait_send(og_mate, ogm_s)
    wait_send(og_recv.at[pl.ds(0, 7)], og_s)
    wait_send(ogy_recv.at[pl.ds(0, 7)], ogy_s)
    wait_send(kvz_recv.at[pl.ds(0, 3)], kvz_s)
    wait_send(kvy_recv.at[pl.ds(0, 7)], kvy_s)
    wait_send(queryy_recv.at[pl.ds(0, 7)], qy_s)
    wait_send(query_recv.at[pl.ds(0, 3)], q_s)
    wait_send(score_grad.at[pl.ds(0, 1280)], kv_s)
    wait_send(blocks.at[pl.ds(0, 3)], z_s)
    wait_send(projs.at[pl.ds(0, 7), 0:320], proj_s)
    wait_send(dkv_mate, dkvm_s)
    wait_send(dkv_recv.at[:, pl.ds(0, 7)], dkv_s)
    wait_send(dqy_recv.at[pl.ds(0, 7)], dqy_s)

    def dq_out():
        wait_recv(dq_recv.at[pl.ds(0, 3)], dq_r)
        for t in range(SEQ):
            x = dq_recv[t // 8, t % 8].astype(F32)
            for j in range(GROUP_HEADS):
                lane = (GROUP_HEADS * t + j) * HEAD
                query_out[:, lane : lane + HEAD] = x[4 * j : 4 * j + 4].astype(BF16)
        stores[2].start()

    wait_recv(foldy_recv.at[pl.ds(0, 7)], foldy_r)
    sums = []
    for i in range(2):
        head_sum = jnp.sum(foldy_recv[4 * i : 4 * i + 4].astype(F32), axis=0)
        sums.append(head_sum.reshape(4, 8, 128))
    foldz_send[...] = jnp.concatenate(sums, axis=1).astype(BF16)
    for d in (2, 1, 3):
        remote(
            foldz_send.at[z_peer(d)], foldz_recv.at[h], foldz_s, foldz_r, seq=z_peer(d) * 8 + y
        ).start()
    foldz_recv[h] = foldz_send[h]
    dq_out()
    wait_send(dq_recv.at[pl.ds(0, 3)], dq_s)
    wait_send(foldy_recv.at[pl.ds(0, 7)], foldy_s)
    wait_send(foldz_recv.at[pl.ds(0, 3)], foldz_s)
    wait_recv(foldz_recv.at[pl.ds(0, 3)], foldz_r)
    for k in range(8):
        x = foldz_recv[k // 2].astype(F32)[8 * (k % 2) : 8 * (k % 2) + 8]
        kv_out[0, :, k * HEAD : k * HEAD + HEAD] = x[0:4].astype(BF16)
        kv_out[1, :, k * HEAD : k * HEAD + HEAD] = x[4:8].astype(BF16)
    stores[3].start()
    for copy in stores:
        copy.wait()


def scratch():
    v = pltpu.VMEM
    dma = pltpu.SemaphoreType.DMA
    buffers = [
        v((TOK, D), BF16), v((1, D), F32), v((256, D), BF16), v((1, TOK), jnp.int32),
        v((4, 12288), BF16), v((2, 4, 1024), BF16),
        v((1, TOK), F32), v((TOK, 320), BF16), v((4, 12288), BF16), v((2, 4, 1024), BF16),
        v((256, 2 * TOK), BF16), v((2 * TOK, D), F32), v((8, 128), F32), v((VOC, 8, 128), F32),
        v((2, 8, 160, 128), BF16), v((8, 160, 128), BF16), v((8, 160, 128), BF16), v((8, 160, 128), BF16),
        v((4, 160, 128), BF16), v((256, 384), BF16), v((8, 384, STACK), BF16),
        v((8, 8, 16, STACK), F32), v((8, 8, 16, STACK), BF16), v((8, 8, 16, STACK), BF16),
        v((8, 8, 16, STACK), BF16), v((8, 8, 16, STACK), BF16),
        v((8, 16, STACK), BF16), v((8, 16, STACK), BF16),
        v((SEQ, 16, 128), F32), v((8, 4, 16, 128), BF16), v((8, 4, 16, 128), BF16), v((4, 8, 16, 128), BF16),
        v((STACK, 128), BF16),
        v((4, 16, 128), F32), v((4, 16, 128), BF16), v((4, 16, 128), BF16),
        v((2, 32, 128), BF16), v((8, 32, 128), BF16), v((2, 8, 2, ROWS, 128), BF16),
        v((KEYS, STACK), F32), v((KEYS, STACK), BF16), v((KEYS, STACK), F32), v((KEYS, STACK), BF16),
        v((8, 4, 16, 128), BF16), v((8, 4, 16, 128), BF16), v((4, 8, 16, 128), BF16),
        v((2, 4, 2, ROWS, 128), F32), v((2, 4, 2, ROWS, 128), BF16), v((2, 4, 2, ROWS, 128), BF16),
        v((2, 4, 2, ROWS, 128), BF16), v((2, 8, ROWS, 128), BF16),
        v((8, 32, 128), BF16), v((8, 32, 128), BF16), v((4, 16, 128), BF16), v((4, 16, 128), BF16),
    ]
    sizes = [
        (8,), (4,), None, None, (2,), (2,), None, (2,), None, (2, 4), None, (2, 4, 2),
        None, (8,), None, (8,), None, None, None, None, None, None, None, None, None, None,
        None, None, (2, 2), (2, 2), None,
        None, None, None, None, None, (2, 4), None, (2,), None, None, None, None,
    ]
    return buffers + [dma if n is None else dma(n) for n in sizes]


def store(*refs):
    sems = refs[12]
    ins = [pltpu.make_async_copy(refs[i], refs[8 + i], sems.at[i]) for i in range(4)]
    outs = [pltpu.make_async_copy(refs[8 + i], refs[4 + i], sems.at[4 + i]) for i in range(4)]
    for copy in ins:
        copy.start()
    for first, second in zip(ins, outs):
        first.wait()
        second.start()
    for copy in outs:
        copy.wait()


def shards(hidden, norm_gain, head_weight, targets, out_proj, query, saved_key_value, offset):
    hbm = pl.BlockSpec(memory_space=pltpu.HBM)
    outs = (
        jax.ShapeDtypeStruct((1, TOK), F32),
        jax.ShapeDtypeStruct((TOK, 320), BF16),
        jax.ShapeDtypeStruct(query.shape, BF16),
        jax.ShapeDtypeStruct(saved_key_value.shape, BF16),
    )
    results = pl.pallas_call(
        body,
        out_shape=outs,
        in_specs=[hbm] * 7 + [pl.BlockSpec(memory_space=pltpu.SMEM)],
        out_specs=(hbm,) * 4,
        scratch_shapes=scratch(),
        compiler_params=pltpu.CompilerParams(
            collective_id=0, has_side_effects=True, vmem_limit_bytes=VMEM_BYTES
        ),
    )(
        hidden, norm_gain.reshape(1, D), head_weight, targets.reshape(1, TOK), out_proj.T, query,
        saved_key_value, offset,
    )
    loss, hidden_grad, query_grad, kv_grad = pl.pallas_call(
        store,
        out_shape=outs,
        in_specs=[hbm] * 4,
        out_specs=(hbm,) * 4,
        scratch_shapes=[pltpu.VMEM(x.shape, x.dtype) for x in outs] + [pltpu.SemaphoreType.DMA((8,))],
        compiler_params=pltpu.CompilerParams(vmem_limit_bytes=VMEM_BYTES),
    )(*results)
    return loss.reshape(TOK), hidden_grad, query_grad, kv_grad


def solution(mesh):
    in_specs = (
        P("seq", None),
        P(),
        P("vocab", None),
        P("seq"),
        P("seq", "vocab"),
        P(("seq", "vocab"), None),
        P(None, ("seq", "vocab"), None),
        P(),
    )
    out_specs = (
        P("seq"),
        P("seq", "vocab"),
        P(("seq", "vocab"), None),
        P(None, ("seq", "vocab"), None),
    )
    return jax.shard_map(shards, mesh=mesh, in_specs=in_specs, out_specs=out_specs, check_vma=False)
```

```python
import jax
import jax.numpy as jnp
from jax import lax
from jax.experimental import pallas as pl
from jax.experimental.pallas import tpu as pltpu
from jax.sharding import PartitionSpec as P

D = 5120
HEAD = 128
SEQ = 32
VOC = 16
TOK = 64
GROUP_HEADS = 3
ROWS = 128
STACK = GROUP_HEADS * ROWS
KEYS = 2048
EPS = 1e-05
LOSS_SCALE = 32.0
MASKED = -1e30
VMEM_BYTES = 62 * 2**20
SCALE = HEAD ** (-0.5)
MESH = pl.DeviceIdType.MESH
F32 = jnp.float32
BF16 = jnp.bfloat16


def remote(src, dst, send_sem, recv_sem, **device):
    return pltpu.make_async_remote_copy(
        src_ref=src,
        dst_ref=dst,
        send_sem=send_sem,
        recv_sem=recv_sem,
        device_id=device,
        device_id_type=MESH,
    )


def low_rows(shape):
    return lax.broadcasted_iota(jnp.int32, shape, len(shape) - 2) < 4


def turn(x):
    return pltpu.roll(x, 4, len(x.shape) - 2)


def first_halves(a, b):
    return jnp.where(low_rows(a.shape), a, turn(b))


def second_halves(a, b):
    return jnp.where(low_rows(a.shape), turn(a), b)


def dot_nt(a, b):
    return lax.dot_general(a, b, (((1,), (1,)), ((), ())), preferred_element_type=F32)


def dot_tn(a, b):
    return lax.dot_general(a, b, (((0,), (0,)), ((), ())), preferred_element_type=F32)


def body(
    hidden_in, gain_in, weight_in, targets_in, proj_in, query, key_value, offset,
    loss_res, hidden_res, query_out, kv_out,
    hidden, gain, weight, targets, loss_out, hidden_out,
    grad_rows, part_raw, stat_send, stat_recv, part_send, part_mate, part_sum, part_recv,
    blocks, acts, projs, og_own, og_give, og_mate, og_sum, og_recv, ogy_send, ogy_recv,
    query_wide, query_send, queryy_recv, query_recv, query_rows, kv_wide, kvz_send, kvz_recv, kvy_send, kvy_recv, kv,
    scores, probs_low, prob_grad, score_grad,
    dq_send, dqy_recv, dq_recv, dkv_own, dkv_give, dkv_mate, dkv_sum, dkv_recv, foldy_send, foldy_recv, foldz_send, foldz_recv,
    in_s, out_s, stat_s, stat_r, mate_s, mate_r, part_s, part_r, z_s, z_r, proj_s, proj_r,
    ogm_s, ogm_r, og_s, og_r, ogy_s, ogy_r, qy_s, qy_r, q_s, q_r, kvz_s, kvz_r, kvy_s, kvy_r, kv_s, kv_z, kv_x, kv_xx, kvm_r,
    dqy_s, dqy_r, dq_s, dq_r, dkvm_s, dkvm_r, dkv_s, dkv_r, foldy_s, foldy_r, foldz_s, foldz_r,
):
    s = lax.axis_index("seq")
    v = lax.axis_index("vocab")
    h, y = s // 8, lax.rem(s, 8)
    chip, core = v // 2, lax.rem(v, 2)
    mate = v + 1 - 2 * core
    beside = v + 2 - 4 * lax.rem(chip, 2)

    def around(block, steps):
        return lax.rem(block + 4 * steps, VOC)

    def wait_recv(ref, sem):
        remote(ref, ref, sem, sem, vocab=mate).wait_recv()

    def wait_send(ref, sem):
        remote(ref, ref, sem, sem, vocab=mate).wait_send()

    loads = [
        pltpu.make_async_copy(src, dst, in_s.at[i])
        for i, (src, dst) in enumerate(
            [
                (hidden_in, hidden), (gain_in, gain), (targets_in, targets),
                (weight_in.at[:, 0:2560], weight.at[:, 0:2560]),
                (weight_in.at[:, 2560:5120], weight.at[:, 2560:5120]),
                (proj_in, projs.at[y, 0:320]),
            ]
        )
    ]
    for load in loads:
        load.start()
    barrier = pltpu.get_barrier_semaphore()

    def z_peer(d):
        return lax.rem(h + d, 4)

    def y_peer(d):
        return lax.rem(y + d, 8)

    for d in (2, 1, 3):
        pl.semaphore_signal(
            barrier, inc=1, device_id={"seq": z_peer(d) * 8 + y}, device_id_type=MESH
        )
    for d in (4, 3, 5, 2, 6, 1, 7):
        pl.semaphore_signal(
            barrier, inc=1, device_id={"seq": h * 8 + y_peer(d)}, device_id_type=MESH
        )

    @pl.loop(1, VOC)
    def _(d):
        pl.semaphore_signal(
            barrier, inc=1, device_id={"vocab": lax.rem(v + d, VOC)}, device_id_type=MESH
        )

    stores = [
        pltpu.make_async_copy(src, dst, out_s.at[i])
        for i, (src, dst) in enumerate(
            [(loss_out, loss_res), (hidden_out, hidden_res)]
        )
    ]

    def square(j, acc):
        x = hidden[:, pl.ds(pl.multiple_of(j * 512, 512), 512)].astype(F32)
        x = x * x
        return acc + (x[:, :128] + x[:, 128:256]) + (x[:, 256:384] + x[:, 384:])

    loads[0].wait()
    squares = lax.fori_loop(0, 10, square, jnp.zeros((TOK, 128), F32))
    inv_rms = lax.rsqrt(jnp.sum(squares, axis=1, keepdims=True) / D + EPS)
    loads[1].wait()
    loads[3].wait()

    def logit_step(j, acc):
        cols = pl.ds(pl.multiple_of(j * 1280, 1280), 1280)
        normed = (hidden[:, cols].astype(F32) * inv_rms * gain[:, cols]).astype(BF16)
        return acc + dot_nt(weight[:, cols], normed)

    logits = lax.fori_loop(0, 2, logit_step, jnp.zeros((256, TOK), F32))
    loads[4].wait()
    logits = lax.fori_loop(2, 4, logit_step, logits)
    loads[2].wait()
    hit = (v * 256 + lax.broadcasted_iota(jnp.int32, (256, TOK), 0)) == targets[...]
    peak = jnp.max(logits, axis=0, keepdims=True)
    raised = jnp.exp(logits - peak)
    stat_send[...] = jnp.zeros((8, 128), F32)
    stat_send[0:1, 0:TOK] = peak
    stat_send[1:2, 0:TOK] = jnp.sum(raised, axis=0, keepdims=True)
    stat_send[2:3, 0:TOK] = jnp.sum(raised * (logits - peak), axis=0, keepdims=True)
    stat_send[3:4, 0:TOK] = jnp.sum(jnp.where(hit, logits, 0.0), axis=0, keepdims=True)
    stat_recv[v] = stat_send[...]
    grad_rows[:, 0:TOK] = raised.astype(BF16)
    grad_rows[:, TOK : 2 * TOK] = hit.astype(F32).astype(BF16)

    for load in loads[5:]:
        load.wait()
    query_wide[...] = jnp.zeros(query_wide.shape, F32)
    for t in range(SEQ):
        for j in range(GROUP_HEADS):
            lane = (GROUP_HEADS * t + j) * HEAD
            query_wide[t % 8 * 4 + t // 8, 4 * j : 4 * j + 4, :] = query[:, lane : lane + HEAD].astype(F32)
    query_send[...] = query_wide[...].astype(BF16).reshape(query_send.shape)
    for k in range(8):
        kv_wide[k // 2, 8 * (k % 2) : 8 * (k % 2) + 4, :] = key_value[
            0, :, k * HEAD : k * HEAD + HEAD
        ].astype(F32)
        kv_wide[k // 2, 8 * (k % 2) + 4 : 8 * (k % 2) + 8, :] = key_value[
            1, :, k * HEAD : k * HEAD + HEAD
        ].astype(F32)
    kvz_send[...] = kv_wide[...].astype(BF16)

    pl.semaphore_wait(barrier, 3 + 7 + VOC - 1)

    @pl.loop(1, VOC)
    def _(d):
        remote(stat_send, stat_recv.at[v], stat_s, stat_r, vocab=lax.rem(v + d, VOC)).start()

    for d in (1, 3, 2):
        remote(
            kvz_send.at[z_peer(d)], kvz_recv.at[h], kvz_s, kvz_r, seq=z_peer(d) * 8 + y
        ).start()
    kvz_recv[h] = kvz_send[h]

    def proj_copy(way, k, f, block):
        at = projs.at[block, 160 * f : 160 * f + 160]
        to = lax.rem(y + 1 + 6 * way, 8)
        return remote(at, at, proj_s, proj_r.at[way, k, f], seq=h * 8 + to)

    def sent(way, k):
        return lax.rem(y + (8 - k if way == 0 else k), 8)

    def got(way, k):
        return lax.rem(y + (7 - k if way == 0 else k + 1), 8)

    def goes(way, k, f):
        return k < 3 or f == way

    def proj_next(k, f):
        for way in range(2):
            if k > 0 and goes(way, k - 1, f):
                proj_copy(way, k - 1, f, got(way, k - 1)).wait_recv()
            if k < 4 and goes(way, k, f):
                proj_copy(way, k, f, sent(way, k)).start()

    proj_next(0, 0)
    proj_next(0, 1)

    left = lax.broadcasted_iota(jnp.int32, (1, 128), 1) < 64

    def half_turn(x):
        return pltpu.roll(x, 64, 1)

    def shifted(a, b, c):
        a, b, c = half_turn(a), half_turn(b), half_turn(c)
        return jnp.where(left, a, b), jnp.where(left, b, c), c

    def packed(a, b, c):
        return jnp.concatenate([a, b, jnp.where(left, c[0:32], half_turn(c[32:64]))], axis=0)

    def own_columns(ref):
        first = 128 * ((5 * v) // 2)
        t = [
            ref[:, pl.ds(pl.multiple_of(first + 128 * i, 128), 128)].astype(F32) for i in range(3)
        ]
        t = [jnp.broadcast_to(x, (TOK, 128)) for x in t]
        return [jnp.where(core == 0, a, b) for a, b in zip(t, shifted(*t))]

    def raw_step(j, carry):
        cols = pl.ds(pl.multiple_of(j * 1280, 1280), 1280)
        part_raw[:, cols] = dot_tn(grad_rows[...], weight[:, cols])
        return carry

    lax.fori_loop(0, 4, raw_step, 0)
    wait_recv(stat_recv.at[pl.ds(0, VOC - 1)], stat_r)
    stats = stat_recv[...]
    peaks = stats[:, 0, 0:TOK]
    row_peak = jnp.max(peaks, axis=0, keepdims=True)
    factor = jnp.exp(peaks - row_peak)
    row_total = jnp.sum(stats[:, 1, 0:TOK] * factor, axis=0, keepdims=True)
    weighted = jnp.sum(
        factor * (stats[:, 2, 0:TOK] + stats[:, 1, 0:TOK] * (peaks - row_peak)),
        axis=0, keepdims=True,
    )
    target_logit = jnp.sum(stats[:, 3, 0:TOK], axis=0, keepdims=True)
    loss_out[...] = jnp.log(row_total) + row_peak - target_logit
    stores[0].start()
    tilt = weighted / row_total + (row_peak - target_logit)
    eye = lax.broadcasted_iota(jnp.int32, (TOK, TOK), 0) == lax.broadcasted_iota(
        jnp.int32, (TOK, TOK), 1
    )

    def column(row):
        return jnp.sum(
            jnp.where(eye, jnp.broadcast_to(row, (TOK, TOK)), 0.0), axis=1, keepdims=True
        )

    tilt = inv_rms * inv_rms * column(tilt) * (LOSS_SCALE / D)
    grad_scale = column(LOSS_SCALE * jnp.exp(peak - row_peak) / row_total)

    wait_recv(kvz_recv.at[pl.ds(0, 3)], kvz_r)
    both = kvz_recv[...].astype(F32).reshape(4, 2, 8, 128)
    for i in range(2):
        kvy_send[i] = both[:, i].reshape(32, 128).astype(BF16)
    for d in (4, 3, 5, 2, 6, 1, 7):
        remote(
            kvy_send.at[y_peer(d) // 4], kvy_recv.at[y], kvy_s, kvy_r, seq=h * 8 + y_peer(d)
        ).start()
    kvy_recv[y] = kvy_send[y // 4]
    for d in (4, 3, 5, 2, 6, 1, 7):
        remote(
            query_send.at[y_peer(d)], queryy_recv.at[y], qy_s, qy_r, seq=h * 8 + y_peer(d)
        ).start()
    queryy_recv[y] = query_send[y]
    def part_chip(j):
        return 2 * lax.rem(chip // 2 + 1 + j // 2, 4) + lax.rem(j, 2)

    def part_step(j, carry):
        cols = pl.ds(pl.multiple_of(part_chip(2 * j) * 640, 1280), 1280)
        out = grad_scale * part_raw[0:TOK, cols] - LOSS_SCALE * part_raw[TOK : 2 * TOK, cols]
        t = [out[:, 128 * i : 128 * i + 128] for i in range(10)]
        for i in range(2):
            u = t[5 * i : 5 * i + 5]
            part_send[0, 2 * j + i] = packed(u[0], u[1], u[2]).astype(BF16)
            part_send[1, 2 * j + i] = packed(*shifted(u[2], u[3], u[4])).astype(BF16)
        return carry

    def mate_copy(i):
        half = pl.ds(4 * i, 4)
        return remote(
            part_send.at[1 - core, half], part_mate.at[half], mate_s.at[i], mate_r.at[i], vocab=mate
        )

    for i in range(2):
        lax.fori_loop(2 * i, 2 * i + 2, part_step, 0)
        mate_copy(i).start()

    portions = [pl.ds(0, 64), pl.ds(64, 96)]

    def part_copy(j, f):
        @pl.when(part_chip(j) != chip)
        def _():
            remote(
                part_sum.at[j, portions[f]], part_recv.at[chip, portions[f]], part_s, part_r.at[f],
                vocab=2 * part_chip(j) + core,
            ).start()

    for i in range(2):
        mate_copy(i).wait_recv()
        for j in range(4 * i, 4 * i + 4):
            part_sum[j] = (part_send[core, j].astype(F32) + part_mate[j].astype(F32)).astype(BF16)

            part_copy(j, 0)

    for j in range(8):
        part_copy(j, 1)
    part_recv[chip] = part_sum[6 + lax.rem(chip, 2)]

    proj_next(1, 0)
    proj_next(1, 1)

    wait_recv(kvy_recv.at[pl.ds(0, 7)], kvy_r)
    pairs = kvy_recv[...].astype(F32).reshape(16, 2, 8, 128)
    kv[0, chip, core] = first_halves(pairs[:, 0], pairs[:, 1]).reshape(ROWS, 128).astype(BF16)
    kv[1, chip, core] = second_halves(pairs[:, 0], pairs[:, 1]).reshape(ROWS, 128).astype(BF16)

    def kv_copy(block, sem, to, kinds=slice(0, 2)):
        at = kv.at[kinds, block // 2, lax.rem(block, 2)]
        return remote(at, at, kv_s, sem, vocab=to)

    kv_copy(v, kv_z, beside).start()
    for way in range(2):
        kv_copy(v, kv_x.at[way, 0], around(v, 1 + 2 * way)).start()
    kv_copy(v, kvm_r, mate).start()


    gains, rows = own_columns(gain), own_columns(hidden)

    def grad(i, total):
        return inv_rms * gains[i] * total - rows[i] * tilt

    def z_copy(f, d, target, origin):
        at = blocks.at[origin, portions[f]]
        return remote(at, at, z_s, z_r.at[f, d], seq=target * 8 + y)

    def kv_next(kind):
        block = v if kind == 0 else beside
        for way in range(2):
            here = around(block, 3 - 2 * way)
            kv_copy(here, kv_x.at[way, kind], mate).wait_recv()
            kv_copy(here, kv_xx.at[way, kind], around(v, 1 + 2 * way), slice(way, way + 1)).start()
            kv_copy(here, kvm_r, mate).start()

    def kv_last(kind):
        far = around(v if kind == 0 else beside, 2)
        for way in range(2):
            kv_copy(far, kv_xx.at[way, kind], mate, slice(way, way + 1)).wait_recv()
        kv_copy(far, kvm_r, mate).start()

    def send_block(f):
        for d in (2, 1, 3):
            z_copy(f, d, lax.rem(h + d, 4), h).start()

    wait_recv(part_recv.at[pl.ds(0, 7), portions[0]], part_r.at[0])
    first_grad = grad(0, jnp.sum(part_recv[:, 0:64].astype(F32), axis=0))
    blocks[h, 0:64, :] = first_grad.astype(BF16)
    send_block(0)
    hidden_out[:, 0:128] = first_grad.astype(BF16)
    wait_recv(part_recv.at[pl.ds(0, 7), portions[1]], part_r.at[1])
    total = jnp.sum(part_recv[:, 64:160].astype(F32), axis=0)
    ends = total[64:96]
    second_grad = grad(1, total[0:64])
    third_grad = grad(2, jnp.concatenate([ends, half_turn(ends)], axis=0))
    blocks[h, 64:160, :] = jnp.concatenate(
        [second_grad, jnp.where(left, third_grad[0:32], half_turn(third_grad[32:64]))], axis=0
    ).astype(BF16)
    send_block(1)
    hidden_out[:, 128:256] = second_grad.astype(BF16)
    hidden_out[:, 256:320] = third_grad[:, 0:64].astype(BF16)
    stores[1].start()

    proj_next(2, 0)
    kv_copy(beside, kv_z, mate).wait_recv()
    for way in range(2):
        kv_copy(beside, kv_x.at[way, 1], around(v, 1 + 2 * way)).start()
    kv_copy(beside, kvm_r, mate).start()
    kv_next(0)
    proj_next(2, 1)
    for f in range(2):
        for d in (1, 3, 2):
            z_copy(f, d, h, lax.rem(h + 4 - d, 4)).wait_recv()
    x = blocks[...]
    ends = x[:, 128:160]
    keep = lax.broadcasted_iota(jnp.int32, ends.shape, 2) < 64
    zero = jnp.zeros_like(ends)
    ends = jnp.concatenate([jnp.where(keep, ends, zero), jnp.where(keep, zero, ends)], axis=1)
    acts[:, 0:128] = x[:, 0:64].reshape(256, 128)
    acts[:, 128:256] = x[:, 64:128].reshape(256, 128)
    acts[:, 256:384] = ends.reshape(256, 128)
    kv_next(1)
    wait_recv(queryy_recv.at[pl.ds(0, 7)], qy_r)
    for d in (2, 1, 3):
        remote(
            queryy_recv.at[:, z_peer(d)], query_recv.at[h], q_s, q_r, seq=z_peer(d) * 8 + y
        ).start()
    query_recv[h] = queryy_recv[:, h]

    def og_copy(j, b):
        return remote(og_give.at[b], og_mate.at[b], ogm_s, ogm_r.at[j], vocab=mate)

    def og_block(j, b):
        projs[b, 320:384, :] = projs[b, 256:320, :]
        out = jnp.dot(acts[...], projs[b], preferred_element_type=F32).reshape(4, 64, STACK)
        out = [out[i].reshape(8, 8, STACK) for i in range(4)]
        even = jnp.concatenate([first_halves(out[0], out[1]), first_halves(out[2], out[3])], axis=1)
        odd = jnp.concatenate([second_halves(out[0], out[1]), second_halves(out[2], out[3])], axis=1)
        og_own[b] = jnp.where(core == 0, even, odd)
        og_give[b] = jnp.where(core == 0, odd, even).astype(BF16)
        og_copy(j, b).start()

    def og_pass(j, b):
        og_copy(j, b).wait_recv()
        og_sum[b] = (og_own[b] + og_mate[b].astype(F32)).astype(BF16)

        @pl.loop(1, 8)
        def _(d):
            m = lax.rem(chip + d, 8)
            remote(
                og_sum.at[b, m], og_recv.at[chip, b], og_s, og_r.at[j], vocab=2 * m + core
            ).start()

        og_recv[chip, b] = og_sum[b, chip]

    def og_done(j, b):
        wait_recv(og_recv.at[pl.ds(0, 7), b], og_r.at[j])
        total = jnp.sum(og_recv[:, b].astype(F32), axis=0).astype(BF16)
        if j == 0:
            ogy_recv[y] = total
        else:
            ogy_send[b] = total
            remote(ogy_send.at[b], ogy_recv.at[y], ogy_s, ogy_r, seq=h * 8 + b).start()

    order = [lax.rem(y + d, 8) for d in (0, 7, 1, 6, 2, 5, 3, 4)]

    def query_step():
        wait_recv(query_recv.at[pl.ds(0, 3)], q_r)
        x = query_recv[...].astype(F32)
        for j in range(GROUP_HEADS):
            part = x[:, :, 8 * (j // 2) : 8 * (j // 2) + 8]
            join = first_halves if j % 2 == 0 else second_halves
            part = jnp.concatenate([join(part[0], part[1]), join(part[2], part[3])], axis=1)
            query_rows[ROWS * j : ROWS * j + ROWS, :] = part.reshape(ROWS, HEAD).astype(BF16)

    start = offset[0]
    r = lax.rem(lax.broadcasted_iota(jnp.int32, (1, STACK), 1), ROWS)
    q_place = (lax.rem(r // 4, 4) * 8 + r // 16) * TOK + 4 * v + lax.rem(r, 4)
    r = lax.broadcasted_iota(jnp.int32, (256, 1), 0)
    k_base = (lax.rem(r // 4, 4) * 8 + lax.rem(r // 16, 8)) * TOK + 4 * (r // ROWS) + lax.rem(r, 4)
    q_before = q_place < start

    def score_part(m, top):
        keys = slice(256 * m, 256 * m + 256)
        k_place = k_base + 8 * m
        seen = (k_place <= q_place) & ((k_place >= start) | q_before)
        x = dot_nt(kv[0, m].reshape(256, HEAD), query_rows[...]) * SCALE
        x = jnp.where(seen, x, MASKED)
        scores[keys, :] = x
        return jnp.maximum(top, jnp.max(x, axis=0, keepdims=True))

    def exp_part(m, top, total):
        keys = slice(256 * m, 256 * m + 256)
        x = jnp.exp(scores[keys, :] - top)
        scores[keys, :] = x
        return total + jnp.sum(x, axis=0, keepdims=True)

    def prob_part(m, share):
        keys = slice(256 * m, 256 * m + 256)
        x = scores[keys, :] * share
        scores[keys, :] = x
        probs_low[keys, :] = x.astype(BF16)

    state = {"top": jnp.full((1, STACK), MASKED, F32), "total": jnp.zeros((1, STACK), F32)}

    def piece(n):
        if n < 8:
            state["top"] = score_part(n, state["top"])
        elif n < 16:
            state["total"] = exp_part(n - 8, state["top"], state["total"])
        else:
            if n == 16:
                state["share"] = 1.0 / state["total"]
            prob_part(n - 16, state["share"])

    def pieces(first, last):
        for n in range(first, last):
            piece(n)

    def pieces(first, last):
        for n in range(first, last):
            piece(n)

    og_block(0, order[0])
    og_block(1, order[1])
    og_block(2, order[2])
    proj_next(3, 0)
    og_pass(0, order[0])
    og_pass(1, order[1])
    og_pass(2, order[2])
    kv_last(0)
    proj_next(3, 1)
    og_block(3, order[3])
    og_block(4, order[4])
    kv_last(1)
    og_block(5, order[5])
    og_pass(3, order[3])
    og_block(6, order[6])
    og_pass(4, order[4])
    wait_recv(kv.at[:, :, 1 - core], kvm_r)
    query_step()
    pieces(0, 4)
    og_pass(5, order[5])
    proj_next(4, 0)
    proj_next(4, 1)
    og_block(7, order[7])
    og_pass(6, order[6])
    pieces(4, 8)
    og_done(0, order[0])
    og_done(1, order[1])
    og_pass(7, order[7])
    og_done(2, order[2])
    pieces(8, 11)
    og_done(3, order[3])
    pieces(11, 14)
    og_done(4, order[4])
    pieces(14, 16)
    og_done(5, order[5])
    pieces(16, 18)
    og_done(6, order[6])
    og_done(7, order[7])
    pieces(18, 24)
    wait_recv(ogy_recv.at[pl.ds(0, 7)], ogy_r)
    out = ogy_recv[...].reshape(ROWS, STACK)
    out_grad = jnp.concatenate([out[:, 0:128], out[:, 128:256], out[:, 256:384]], axis=0)

    def group(j):
        return lax.rem(chip // 2 + 1 + j, 4)

    def group_keys(j):
        return pl.ds(pl.multiple_of(group(j) * 512, 512), 512)

    def dkvm_copy(n, j):
        return remote(dkv_give.at[n, j], dkv_mate.at[n, j], dkvm_s, dkvm_r.at[n, j], vocab=mate)

    def share(n, j, part):
        part = part.reshape(2, 2, ROWS, HEAD)
        first, second = part[:, 0], part[:, 1]
        dkv_own[n, j] = jnp.where(core == 0, first, second)
        dkv_give[n, j] = jnp.where(core == 0, second, first).astype(BF16)
        dkvm_copy(n, j).start()

    def send_on(n, j):
        dkvm_copy(n, j).wait_recv()
        dkv_sum[n, j] = (dkv_own[n, j] + dkv_mate[n, j].astype(F32)).astype(BF16)
        for i in range(2):
            m = 2 * group(j) + i

            @pl.when(m != chip)
            def _():
                remote(
                    dkv_sum.at[n, j, i], dkv_recv.at[n, chip], dkv_s, dkv_r.at[n], vocab=2 * m + core
                ).start()

    def value_pass(j):
        share(1, j, jnp.dot(probs_low[group_keys(j), :], out_grad, preferred_element_type=F32))

    def key_pass(j):
        keys = group_keys(j)
        ds_low = (scores[keys, :] * (prob_grad[keys, :] - delta)).astype(BF16)
        score_grad[keys, :] = ds_low
        share(0, j, jnp.dot(ds_low, query_rows[...], preferred_element_type=F32) * SCALE)

    value_pass(0)
    value_pass(1)
    value_pass(2)
    send_on(1, 0)
    value_pass(3)
    send_on(1, 1)

    delta = jnp.zeros((1, STACK), F32)
    for m in range(4):
        keys = slice(512 * m, 512 * m + 512)
        x = dot_nt(kv[1, 2 * m : 2 * m + 2].reshape(512, HEAD), out_grad)
        prob_grad[keys, :] = x
        delta = delta + jnp.sum(probs_low[keys, :].astype(F32) * x, axis=0, keepdims=True)

    send_on(1, 2)
    send_on(1, 3)
    key_pass(0)
    key_pass(1)
    key_pass(2)
    send_on(0, 0)
    key_pass(3)
    send_on(0, 1)
    send_on(0, 2)

    dq = dot_tn(score_grad[...], kv[0].reshape(KEYS, HEAD)) * SCALE
    send_on(0, 3)
    t0, t1, t2 = [dq[128 * j : 128 * j + 128].reshape(16, 8, 128) for j in range(3)]
    t0 = jnp.concatenate([first_halves(t0, t1), t2, second_halves(t0, t1), turn(t2)], axis=1)
    dq_send[...] = t0.astype(BF16).reshape(dq_send.shape)

    for d in (4, 3, 5, 2, 6, 1, 7):
        remote(
            dq_send.at[y_peer(d)], dqy_recv.at[y], dqy_s, dqy_r, seq=h * 8 + y_peer(d)
        ).start()
    dqy_recv[y] = dq_send[y]

    for n in range(2):
        dkv_recv[n, chip] = dkv_sum[n, 3, lax.rem(chip, 2)]
    wait_recv(dkv_recv.at[1, pl.ds(0, 7)], dkv_r.at[1])
    values_sum = jnp.sum(dkv_recv[1].astype(F32), axis=0).reshape(16, 8, 128)
    wait_recv(dkv_recv.at[0, pl.ds(0, 7)], dkv_r.at[0])
    keys_sum = jnp.sum(dkv_recv[0].astype(F32), axis=0).reshape(16, 8, 128)
    parts = jnp.stack(
        [first_halves(keys_sum, values_sum), second_halves(keys_sum, values_sum)], axis=1
    )
    foldy_send[...] = parts.reshape(8, 32, 128).astype(BF16)
    for d in (4, 3, 5, 2, 6, 1, 7):
        remote(
            foldy_send.at[y_peer(d)], foldy_recv.at[y], foldy_s, foldy_r, seq=h * 8 + y_peer(d)
        ).start()
    foldy_recv[y] = foldy_send[y]

    wait_recv(dqy_recv.at[pl.ds(0, 7)], dqy_r)
    for d in (2, 1, 3):
        remote(
            dqy_recv.at[:, z_peer(d)], dq_recv.at[h], dq_s, dq_r, seq=z_peer(d) * 8 + y
        ).start()
    dq_recv[h] = dqy_recv[:, h]

    wait_send(stat_recv.at[pl.ds(0, VOC - 1)], stat_s)
    for i in range(2):
        mate_copy(i).wait_send()
    wait_send(part_recv.at[pl.ds(0, 7)], part_s)
    wait_send(og_mate, ogm_s)
    wait_send(og_recv.at[pl.ds(0, 7)], og_s)
    wait_send(ogy_recv.at[pl.ds(0, 7)], ogy_s)
    wait_send(kvz_recv.at[pl.ds(0, 3)], kvz_s)
    wait_send(kvy_recv.at[pl.ds(0, 7)], kvy_s)
    wait_send(queryy_recv.at[pl.ds(0, 7)], qy_s)
    wait_send(query_recv.at[pl.ds(0, 3)], q_s)
    wait_send(score_grad.at[pl.ds(0, 1280)], kv_s)
    wait_send(blocks.at[pl.ds(0, 3)], z_s)
    wait_send(projs.at[pl.ds(0, 7), 0:320], proj_s)
    wait_send(dkv_mate, dkvm_s)
    wait_send(dkv_recv.at[:, pl.ds(0, 7)], dkv_s)
    wait_send(dqy_recv.at[pl.ds(0, 7)], dqy_s)

    def dq_out():
        wait_recv(dq_recv.at[pl.ds(0, 3)], dq_r)
        for t in range(SEQ):
            x = dq_recv[t // 8, t % 8].astype(F32)
            for j in range(GROUP_HEADS):
                lane = (GROUP_HEADS * t + j) * HEAD
                query_out[:, lane : lane + HEAD] = x[4 * j : 4 * j + 4].astype(BF16)

    wait_recv(foldy_recv.at[pl.ds(0, 7)], foldy_r)
    sums = []
    for i in range(2):
        head_sum = jnp.sum(foldy_recv[4 * i : 4 * i + 4].astype(F32), axis=0)
        sums.append(head_sum.reshape(4, 8, 128))
    foldz_send[...] = jnp.concatenate(sums, axis=1).astype(BF16)
    for d in (2, 1, 3):
        remote(
            foldz_send.at[z_peer(d)], foldz_recv.at[h], foldz_s, foldz_r, seq=z_peer(d) * 8 + y
        ).start()
    foldz_recv[h] = foldz_send[h]
    dq_out()
    wait_send(dq_recv.at[pl.ds(0, 3)], dq_s)
    wait_send(foldy_recv.at[pl.ds(0, 7)], foldy_s)
    wait_send(foldz_recv.at[pl.ds(0, 3)], foldz_s)
    wait_recv(foldz_recv.at[pl.ds(0, 3)], foldz_r)
    for k in range(8):
        x = foldz_recv[k // 2].astype(F32)[8 * (k % 2) : 8 * (k % 2) + 8]
        kv_out[0, :, k * HEAD : k * HEAD + HEAD] = x[0:4].astype(BF16)
        kv_out[1, :, k * HEAD : k * HEAD + HEAD] = x[4:8].astype(BF16)
    for copy in stores:
        copy.wait()


def scratch():
    v = pltpu.VMEM
    dma = pltpu.SemaphoreType.DMA
    buffers = [
        v((TOK, D), BF16), v((1, D), F32), v((256, D), BF16), v((1, TOK), jnp.int32),
        v((1, TOK), F32), v((TOK, 320), BF16),
        v((256, 2 * TOK), BF16), v((2 * TOK, D), F32), v((8, 128), F32), v((VOC, 8, 128), F32),
        v((2, 8, 160, 128), BF16), v((8, 160, 128), BF16), v((8, 160, 128), BF16), v((8, 160, 128), BF16),
        v((4, 160, 128), BF16), v((256, 384), BF16), v((8, 384, STACK), BF16),
        v((8, 8, 16, STACK), F32), v((8, 8, 16, STACK), BF16), v((8, 8, 16, STACK), BF16),
        v((8, 8, 16, STACK), BF16), v((8, 8, 16, STACK), BF16),
        v((8, 16, STACK), BF16), v((8, 16, STACK), BF16),
        v((SEQ, 16, 128), F32), v((8, 4, 16, 128), BF16), v((8, 4, 16, 128), BF16), v((4, 8, 16, 128), BF16),
        v((STACK, 128), BF16),
        v((4, 16, 128), F32), v((4, 16, 128), BF16), v((4, 16, 128), BF16),
        v((2, 32, 128), BF16), v((8, 32, 128), BF16), v((2, 8, 2, ROWS, 128), BF16),
        v((KEYS, STACK), F32), v((KEYS, STACK), BF16), v((KEYS, STACK), F32), v((KEYS, STACK), BF16),
        v((8, 4, 16, 128), BF16), v((8, 4, 16, 128), BF16), v((4, 8, 16, 128), BF16),
        v((2, 4, 2, ROWS, 128), F32), v((2, 4, 2, ROWS, 128), BF16), v((2, 4, 2, ROWS, 128), BF16),
        v((2, 4, 2, ROWS, 128), BF16), v((2, 8, ROWS, 128), BF16),
        v((8, 32, 128), BF16), v((8, 32, 128), BF16), v((4, 16, 128), BF16), v((4, 16, 128), BF16),
    ]
    sizes = [
        (6,), (2,), None, None, (2,), (2,), None, (2,), None, (2, 4), None, (2, 4, 2),
        None, (8,), None, (8,), None, None, None, None, None, None, None, None, None, None,
        None, None, (2, 2), (2, 2), None,
        None, None, None, None, None, (2, 4), None, (2,), None, None, None, None,
    ]
    return buffers + [dma if n is None else dma(n) for n in sizes]


def store(*refs):
    for src, dst in zip(refs[:4], refs[4:]):
        dst[...] = src[...]


def shards(hidden, norm_gain, head_weight, targets, out_proj, query, saved_key_value, offset):
    vmem = pl.BlockSpec(memory_space=pltpu.VMEM)
    hbm = pl.BlockSpec(memory_space=pltpu.HBM)
    outs = (
        jax.ShapeDtypeStruct((1, TOK), F32),
        jax.ShapeDtypeStruct((TOK, 320), BF16),
        jax.ShapeDtypeStruct(query.shape, BF16),
        jax.ShapeDtypeStruct(saved_key_value.shape, BF16),
    )
    results = pl.pallas_call(
        body,
        out_shape=outs,
        in_specs=[hbm] * 5 + [vmem] * 2 + [pl.BlockSpec(memory_space=pltpu.SMEM)],
        out_specs=(hbm, hbm, vmem, vmem),
        scratch_shapes=scratch(),
        compiler_params=pltpu.CompilerParams(
            collective_id=0, has_side_effects=True, vmem_limit_bytes=VMEM_BYTES
        ),
    )(
        hidden, norm_gain.reshape(1, D), head_weight, targets.reshape(1, TOK), out_proj.T, query,
        saved_key_value, offset,
    )
    loss, hidden_grad, query_grad, kv_grad = pl.pallas_call(
        store,
        out_shape=outs,
        in_specs=[vmem] * 4,
        out_specs=(vmem,) * 4,
        compiler_params=pltpu.CompilerParams(vmem_limit_bytes=VMEM_BYTES),
    )(*results)
    return loss.reshape(TOK), hidden_grad, query_grad, kv_grad


def solution(mesh):
    in_specs = (
        P("seq", None),
        P(),
        P("vocab", None),
        P("seq"),
        P("seq", "vocab"),
        P(("seq", "vocab"), None),
        P(None, ("seq", "vocab"), None),
        P(),
    )
    out_specs = (
        P("seq"),
        P("seq", "vocab"),
        P(("seq", "vocab"), None),
        P(None, ("seq", "vocab"), None),
    )
    return jax.shard_map(shards, mesh=mesh, in_specs=in_specs, out_specs=out_specs, check_vma=False)
```

```python
import jax
import jax.numpy as jnp
from jax import lax
from jax.experimental import pallas as pl
from jax.experimental.pallas import tpu as pltpu
from jax.sharding import PartitionSpec as P

D = 5120
HEAD = 128
SEQ = 32
VOC = 16
TOK = 64
GROUP_HEADS = 3
ROWS = 128
STACK = GROUP_HEADS * ROWS
KEYS = 2048
EPS = 1e-05
LOSS_SCALE = 32.0
MASKED = -1e30
VMEM_BYTES = 62 * 2**20
SCALE = HEAD ** (-0.5)
MESH = pl.DeviceIdType.MESH
F32 = jnp.float32
BF16 = jnp.bfloat16


def remote(src, dst, send_sem, recv_sem, **device):
    return pltpu.make_async_remote_copy(
        src_ref=src,
        dst_ref=dst,
        send_sem=send_sem,
        recv_sem=recv_sem,
        device_id=device,
        device_id_type=MESH,
    )


def low_rows(shape):
    return lax.broadcasted_iota(jnp.int32, shape, len(shape) - 2) < 4


def turn(x):
    return pltpu.roll(x, 4, len(x.shape) - 2)


def first_halves(a, b):
    return jnp.where(low_rows(a.shape), a, turn(b))


def second_halves(a, b):
    return jnp.where(low_rows(a.shape), turn(a), b)


def dot_nt(a, b):
    return lax.dot_general(a, b, (((1,), (1,)), ((), ())), preferred_element_type=F32)


def dot_tn(a, b):
    return lax.dot_general(a, b, (((0,), (0,)), ((), ())), preferred_element_type=F32)


def body(
    hidden_in, gain_in, weight_in, targets_in, proj_in, query_in, key_value_in, offset,
    loss_res, hidden_res, query_res, kv_res,
    hidden, gain, weight, targets, query, key_value, loss_out, hidden_out, query_out, kv_out,
    grad_rows, part_raw, stat_send, stat_recv, part_send, part_mate, part_sum, part_recv,
    blocks, acts, projs, og_own, og_give, og_mate, og_sum, og_recv, ogy_send, ogy_recv,
    query_wide, query_send, queryy_recv, query_recv, query_rows, kv_wide, kvz_send, kvz_recv, kvy_send, kvy_recv, kv,
    scores, probs_low, prob_grad, score_grad,
    dq_send, dqy_recv, dq_recv, dkv_own, dkv_give, dkv_mate, dkv_sum, dkv_recv, foldy_send, foldy_recv, foldz_send, foldz_recv,
    in_s, out_s, stat_s, stat_r, mate_s, mate_r, part_s, part_r, z_s, z_r, proj_s, proj_r,
    ogm_s, ogm_r, og_s, og_r, ogy_s, ogy_r, qy_s, qy_r, q_s, q_r, kvz_s, kvz_r, kvy_s, kvy_r, kv_s, kv_z, kv_x, kv_xx, kvm_r,
    dqy_s, dqy_r, dq_s, dq_r, dkvm_s, dkvm_r, dkv_s, dkv_r, foldy_s, foldy_r, foldz_s, foldz_r,
):
    s = lax.axis_index("seq")
    v = lax.axis_index("vocab")
    h, y = s // 8, lax.rem(s, 8)
    chip, core = v // 2, lax.rem(v, 2)
    mate = v + 1 - 2 * core
    beside = v + 2 - 4 * lax.rem(chip, 2)

    def around(block, steps):
        return lax.rem(block + 4 * steps, VOC)

    def wait_recv(ref, sem):
        remote(ref, ref, sem, sem, vocab=mate).wait_recv()

    def wait_send(ref, sem):
        remote(ref, ref, sem, sem, vocab=mate).wait_send()

    loads = [
        pltpu.make_async_copy(src, dst, in_s.at[i])
        for i, (src, dst) in enumerate(
            [
                (hidden_in, hidden), (gain_in, gain), (targets_in, targets),
                (weight_in.at[:, 0:2560], weight.at[:, 0:2560]),
                (weight_in.at[:, 2560:5120], weight.at[:, 2560:5120]),
                (query_in, query), (key_value_in, key_value), (proj_in, projs.at[y, 0:320]),
            ]
        )
    ]
    for load in loads:
        load.start()
    barrier = pltpu.get_barrier_semaphore()

    def z_peer(d):
        return lax.rem(h + d, 4)

    def y_peer(d):
        return lax.rem(y + d, 8)

    for d in (2, 1, 3):
        pl.semaphore_signal(
            barrier, inc=1, device_id={"seq": z_peer(d) * 8 + y}, device_id_type=MESH
        )
    for d in (4, 3, 5, 2, 6, 1, 7):
        pl.semaphore_signal(
            barrier, inc=1, device_id={"seq": h * 8 + y_peer(d)}, device_id_type=MESH
        )

    @pl.loop(1, VOC)
    def _(d):
        pl.semaphore_signal(
            barrier, inc=1, device_id={"vocab": lax.rem(v + d, VOC)}, device_id_type=MESH
        )

    stores = [
        pltpu.make_async_copy(src, dst, out_s.at[i])
        for i, (src, dst) in enumerate(
            [(loss_out, loss_res), (hidden_out, hidden_res), (query_out, query_res), (kv_out, kv_res)]
        )
    ]

    def square(j, acc):
        x = hidden[:, pl.ds(pl.multiple_of(j * 512, 512), 512)].astype(F32)
        x = x * x
        return acc + (x[:, :128] + x[:, 128:256]) + (x[:, 256:384] + x[:, 384:])

    loads[0].wait()
    squares = lax.fori_loop(0, 10, square, jnp.zeros((TOK, 128), F32))
    inv_rms = lax.rsqrt(jnp.sum(squares, axis=1, keepdims=True) / D + EPS)
    loads[1].wait()
    loads[3].wait()

    def logit_step(j, acc):
        cols = pl.ds(pl.multiple_of(j * 1280, 1280), 1280)
        normed = (hidden[:, cols].astype(F32) * inv_rms * gain[:, cols]).astype(BF16)
        return acc + dot_nt(weight[:, cols], normed)

    logits = lax.fori_loop(0, 2, logit_step, jnp.zeros((256, TOK), F32))
    loads[4].wait()
    logits = lax.fori_loop(2, 4, logit_step, logits)
    loads[2].wait()
    hit = (v * 256 + lax.broadcasted_iota(jnp.int32, (256, TOK), 0)) == targets[...]
    peak = jnp.max(logits, axis=0, keepdims=True)
    raised = jnp.exp(logits - peak)
    stat_send[...] = jnp.zeros((8, 128), F32)
    stat_send[0:1, 0:TOK] = peak
    stat_send[1:2, 0:TOK] = jnp.sum(raised, axis=0, keepdims=True)
    stat_send[2:3, 0:TOK] = jnp.sum(raised * (logits - peak), axis=0, keepdims=True)
    stat_send[3:4, 0:TOK] = jnp.sum(jnp.where(hit, logits, 0.0), axis=0, keepdims=True)
    stat_recv[v] = stat_send[...]
    grad_rows[:, 0:TOK] = raised.astype(BF16)
    grad_rows[:, TOK : 2 * TOK] = hit.astype(F32).astype(BF16)

    for load in loads[5:]:
        load.wait()
    query_wide[...] = jnp.zeros(query_wide.shape, F32)
    for t in range(SEQ):
        for j in range(GROUP_HEADS):
            lane = (GROUP_HEADS * t + j) * HEAD
            query_wide[t % 8 * 4 + t // 8, 4 * j : 4 * j + 4, :] = query[:, lane : lane + HEAD].astype(F32)
    query_send[...] = query_wide[...].astype(BF16).reshape(query_send.shape)
    for k in range(8):
        kv_wide[k // 2, 8 * (k % 2) : 8 * (k % 2) + 4, :] = key_value[
            0, :, k * HEAD : k * HEAD + HEAD
        ].astype(F32)
        kv_wide[k // 2, 8 * (k % 2) + 4 : 8 * (k % 2) + 8, :] = key_value[
            1, :, k * HEAD : k * HEAD + HEAD
        ].astype(F32)
    kvz_send[...] = kv_wide[...].astype(BF16)

    pl.semaphore_wait(barrier, 3 + 7 + VOC - 1)

    @pl.loop(1, VOC)
    def _(d):
        remote(stat_send, stat_recv.at[v], stat_s, stat_r, vocab=lax.rem(v + d, VOC)).start()

    for d in (1, 3, 2):
        remote(
            kvz_send.at[z_peer(d)], kvz_recv.at[h], kvz_s, kvz_r, seq=z_peer(d) * 8 + y
        ).start()
    kvz_recv[h] = kvz_send[h]

    def proj_copy(way, k, f, block):
        at = projs.at[block, 160 * f : 160 * f + 160]
        to = lax.rem(y + 1 + 6 * way, 8)
        return remote(at, at, proj_s, proj_r.at[way, k, f], seq=h * 8 + to)

    def sent(way, k):
        return lax.rem(y + (8 - k if way == 0 else k), 8)

    def got(way, k):
        return lax.rem(y + (7 - k if way == 0 else k + 1), 8)

    def goes(way, k, f):
        return k < 3 or f == way

    def proj_next(k, f):
        for way in range(2):
            if k > 0 and goes(way, k - 1, f):
                proj_copy(way, k - 1, f, got(way, k - 1)).wait_recv()
            if k < 4 and goes(way, k, f):
                proj_copy(way, k, f, sent(way, k)).start()

    proj_next(0, 0)
    proj_next(0, 1)

    left = lax.broadcasted_iota(jnp.int32, (1, 128), 1) < 64

    def half_turn(x):
        return pltpu.roll(x, 64, 1)

    def shifted(a, b, c):
        a, b, c = half_turn(a), half_turn(b), half_turn(c)
        return jnp.where(left, a, b), jnp.where(left, b, c), c

    def packed(a, b, c):
        return jnp.concatenate([a, b, jnp.where(left, c[0:32], half_turn(c[32:64]))], axis=0)

    def own_columns(ref):
        first = 128 * ((5 * v) // 2)
        t = [
            ref[:, pl.ds(pl.multiple_of(first + 128 * i, 128), 128)].astype(F32) for i in range(3)
        ]
        t = [jnp.broadcast_to(x, (TOK, 128)) for x in t]
        return [jnp.where(core == 0, a, b) for a, b in zip(t, shifted(*t))]

    def raw_step(j, carry):
        cols = pl.ds(pl.multiple_of(j * 1280, 1280), 1280)
        part_raw[:, cols] = dot_tn(grad_rows[...], weight[:, cols])
        return carry

    lax.fori_loop(0, 4, raw_step, 0)
    wait_recv(stat_recv.at[pl.ds(0, VOC - 1)], stat_r)
    stats = stat_recv[...]
    peaks = stats[:, 0, 0:TOK]
    row_peak = jnp.max(peaks, axis=0, keepdims=True)
    factor = jnp.exp(peaks - row_peak)
    row_total = jnp.sum(stats[:, 1, 0:TOK] * factor, axis=0, keepdims=True)
    weighted = jnp.sum(
        factor * (stats[:, 2, 0:TOK] + stats[:, 1, 0:TOK] * (peaks - row_peak)),
        axis=0, keepdims=True,
    )
    target_logit = jnp.sum(stats[:, 3, 0:TOK], axis=0, keepdims=True)
    loss_out[...] = jnp.log(row_total) + row_peak - target_logit
    stores[0].start()
    tilt = weighted / row_total + (row_peak - target_logit)
    eye = lax.broadcasted_iota(jnp.int32, (TOK, TOK), 0) == lax.broadcasted_iota(
        jnp.int32, (TOK, TOK), 1
    )

    def column(row):
        return jnp.sum(
            jnp.where(eye, jnp.broadcast_to(row, (TOK, TOK)), 0.0), axis=1, keepdims=True
        )

    tilt = inv_rms * inv_rms * column(tilt) * (LOSS_SCALE / D)
    grad_scale = column(LOSS_SCALE * jnp.exp(peak - row_peak) / row_total)

    wait_recv(kvz_recv.at[pl.ds(0, 3)], kvz_r)
    both = kvz_recv[...].astype(F32).reshape(4, 2, 8, 128)
    for i in range(2):
        kvy_send[i] = both[:, i].reshape(32, 128).astype(BF16)
    for d in (4, 3, 5, 2, 6, 1, 7):
        remote(
            kvy_send.at[y_peer(d) // 4], kvy_recv.at[y], kvy_s, kvy_r, seq=h * 8 + y_peer(d)
        ).start()
    kvy_recv[y] = kvy_send[y // 4]
    for d in (4, 3, 5, 2, 6, 1, 7):
        remote(
            query_send.at[y_peer(d)], queryy_recv.at[y], qy_s, qy_r, seq=h * 8 + y_peer(d)
        ).start()
    queryy_recv[y] = query_send[y]
    def part_chip(j):
        return 2 * lax.rem(chip // 2 + 1 + j // 2, 4) + lax.rem(j, 2)

    def part_step(j, carry):
        cols = pl.ds(pl.multiple_of(part_chip(2 * j) * 640, 1280), 1280)
        out = grad_scale * part_raw[0:TOK, cols] - LOSS_SCALE * part_raw[TOK : 2 * TOK, cols]
        t = [out[:, 128 * i : 128 * i + 128] for i in range(10)]
        for i in range(2):
            u = t[5 * i : 5 * i + 5]
            part_send[0, 2 * j + i] = packed(u[0], u[1], u[2]).astype(BF16)
            part_send[1, 2 * j + i] = packed(*shifted(u[2], u[3], u[4])).astype(BF16)
        return carry

    def mate_copy(i):
        half = pl.ds(4 * i, 4)
        return remote(
            part_send.at[1 - core, half], part_mate.at[half], mate_s.at[i], mate_r.at[i], vocab=mate
        )

    for i in range(2):
        lax.fori_loop(2 * i, 2 * i + 2, part_step, 0)
        mate_copy(i).start()

    portions = [pl.ds(0, 64), pl.ds(64, 96)]

    def part_copy(j, f):
        @pl.when(part_chip(j) != chip)
        def _():
            remote(
                part_sum.at[j, portions[f]], part_recv.at[chip, portions[f]], part_s, part_r.at[f],
                vocab=2 * part_chip(j) + core,
            ).start()

    for i in range(2):
        mate_copy(i).wait_recv()
        for j in range(4 * i, 4 * i + 4):
            part_sum[j] = (part_send[core, j].astype(F32) + part_mate[j].astype(F32)).astype(BF16)

            part_copy(j, 0)

    for j in range(8):
        part_copy(j, 1)
    part_recv[chip] = part_sum[6 + lax.rem(chip, 2)]

    proj_next(1, 0)
    proj_next(1, 1)

    wait_recv(kvy_recv.at[pl.ds(0, 7)], kvy_r)
    pairs = kvy_recv[...].astype(F32).reshape(16, 2, 8, 128)
    kv[0, chip, core] = first_halves(pairs[:, 0], pairs[:, 1]).reshape(ROWS, 128).astype(BF16)
    kv[1, chip, core] = second_halves(pairs[:, 0], pairs[:, 1]).reshape(ROWS, 128).astype(BF16)

    def kv_copy(block, sem, to, kinds=slice(0, 2)):
        at = kv.at[kinds, block // 2, lax.rem(block, 2)]
        return remote(at, at, kv_s, sem, vocab=to)

    kv_copy(v, kv_z, beside).start()
    for way in range(2):
        kv_copy(v, kv_x.at[way, 0], around(v, 1 + 2 * way)).start()
    kv_copy(v, kvm_r, mate).start()


    gains, rows = own_columns(gain), own_columns(hidden)

    def grad(i, total):
        return inv_rms * gains[i] * total - rows[i] * tilt

    def z_copy(f, d, target, origin):
        at = blocks.at[origin, portions[f]]
        return remote(at, at, z_s, z_r.at[f, d], seq=target * 8 + y)

    def kv_next(kind):
        block = v if kind == 0 else beside
        for way in range(2):
            here = around(block, 3 - 2 * way)
            kv_copy(here, kv_x.at[way, kind], mate).wait_recv()
            kv_copy(here, kv_xx.at[way, kind], around(v, 1 + 2 * way), slice(way, way + 1)).start()
            kv_copy(here, kvm_r, mate).start()

    def kv_last(kind):
        far = around(v if kind == 0 else beside, 2)
        for way in range(2):
            kv_copy(far, kv_xx.at[way, kind], mate, slice(way, way + 1)).wait_recv()
        kv_copy(far, kvm_r, mate).start()

    def send_block(f):
        for d in (2, 1, 3):
            z_copy(f, d, lax.rem(h + d, 4), h).start()

    wait_recv(part_recv.at[pl.ds(0, 7), portions[0]], part_r.at[0])
    first_grad = grad(0, jnp.sum(part_recv[:, 0:64].astype(F32), axis=0))
    blocks[h, 0:64, :] = first_grad.astype(BF16)
    send_block(0)
    hidden_out[:, 0:128] = first_grad.astype(BF16)
    wait_recv(part_recv.at[pl.ds(0, 7), portions[1]], part_r.at[1])
    total = jnp.sum(part_recv[:, 64:160].astype(F32), axis=0)
    ends = total[64:96]
    second_grad = grad(1, total[0:64])
    third_grad = grad(2, jnp.concatenate([ends, half_turn(ends)], axis=0))
    blocks[h, 64:160, :] = jnp.concatenate(
        [second_grad, jnp.where(left, third_grad[0:32], half_turn(third_grad[32:64]))], axis=0
    ).astype(BF16)
    send_block(1)
    hidden_out[:, 128:256] = second_grad.astype(BF16)
    hidden_out[:, 256:320] = third_grad[:, 0:64].astype(BF16)
    stores[1].start()

    proj_next(2, 0)
    kv_copy(beside, kv_z, mate).wait_recv()
    for way in range(2):
        kv_copy(beside, kv_x.at[way, 1], around(v, 1 + 2 * way)).start()
    kv_copy(beside, kvm_r, mate).start()
    kv_next(0)
    proj_next(2, 1)
    for f in range(2):
        for d in (1, 3, 2):
            z_copy(f, d, h, lax.rem(h + 4 - d, 4)).wait_recv()
    x = blocks[...]
    ends = x[:, 128:160]
    keep = lax.broadcasted_iota(jnp.int32, ends.shape, 2) < 64
    zero = jnp.zeros_like(ends)
    ends = jnp.concatenate([jnp.where(keep, ends, zero), jnp.where(keep, zero, ends)], axis=1)
    acts[:, 0:128] = x[:, 0:64].reshape(256, 128)
    acts[:, 128:256] = x[:, 64:128].reshape(256, 128)
    acts[:, 256:384] = ends.reshape(256, 128)
    kv_next(1)
    wait_recv(queryy_recv.at[pl.ds(0, 7)], qy_r)
    for d in (2, 1, 3):
        remote(
            queryy_recv.at[:, z_peer(d)], query_recv.at[h], q_s, q_r, seq=z_peer(d) * 8 + y
        ).start()
    query_recv[h] = queryy_recv[:, h]

    def og_copy(j, b):
        return remote(og_give.at[b], og_mate.at[b], ogm_s, ogm_r.at[j], vocab=mate)

    def og_block(j, b):
        projs[b, 320:384, :] = projs[b, 256:320, :]
        out = jnp.dot(acts[...], projs[b], preferred_element_type=F32).reshape(4, 64, STACK)
        out = [out[i].reshape(8, 8, STACK) for i in range(4)]
        even = jnp.concatenate([first_halves(out[0], out[1]), first_halves(out[2], out[3])], axis=1)
        odd = jnp.concatenate([second_halves(out[0], out[1]), second_halves(out[2], out[3])], axis=1)
        og_own[b] = jnp.where(core == 0, even, odd)
        og_give[b] = jnp.where(core == 0, odd, even).astype(BF16)
        og_copy(j, b).start()

    def og_pass(j, b):
        og_copy(j, b).wait_recv()
        og_sum[b] = (og_own[b] + og_mate[b].astype(F32)).astype(BF16)

        for d in (4, 5, 3, 2, 6, 7, 1):
            m = lax.rem(chip + d, 8)
            remote(
                og_sum.at[b, m], og_recv.at[chip, b], og_s, og_r.at[j], vocab=2 * m + core
            ).start()

        og_recv[chip, b] = og_sum[b, chip]

    def og_done(j, b):
        wait_recv(og_recv.at[pl.ds(0, 7), b], og_r.at[j])
        total = jnp.sum(og_recv[:, b].astype(F32), axis=0).astype(BF16)
        if j == 0:
            ogy_recv[y] = total
        else:
            ogy_send[b] = total
            remote(ogy_send.at[b], ogy_recv.at[y], ogy_s, ogy_r, seq=h * 8 + b).start()

    order = [lax.rem(y + d, 8) for d in (0, 7, 1, 6, 2, 5, 3, 4)]

    def query_step():
        wait_recv(query_recv.at[pl.ds(0, 3)], q_r)
        x = query_recv[...].astype(F32)
        for j in range(GROUP_HEADS):
            part = x[:, :, 8 * (j // 2) : 8 * (j // 2) + 8]
            join = first_halves if j % 2 == 0 else second_halves
            part = jnp.concatenate([join(part[0], part[1]), join(part[2], part[3])], axis=1)
            query_rows[ROWS * j : ROWS * j + ROWS, :] = part.reshape(ROWS, HEAD).astype(BF16)

    start = offset[0]
    r = lax.rem(lax.broadcasted_iota(jnp.int32, (1, STACK), 1), ROWS)
    q_place = (lax.rem(r // 4, 4) * 8 + r // 16) * TOK + 4 * v + lax.rem(r, 4)
    r = lax.broadcasted_iota(jnp.int32, (256, 1), 0)
    k_base = (lax.rem(r // 4, 4) * 8 + lax.rem(r // 16, 8)) * TOK + 4 * (r // ROWS) + lax.rem(r, 4)
    q_before = q_place < start

    def score_part(m, top):
        keys = slice(256 * m, 256 * m + 256)
        k_place = k_base + 8 * m
        seen = (k_place <= q_place) & ((k_place >= start) | q_before)
        x = dot_nt(kv[0, m].reshape(256, HEAD), query_rows[...]) * SCALE
        x = jnp.where(seen, x, MASKED)
        scores[keys, :] = x
        return jnp.maximum(top, jnp.max(x, axis=0, keepdims=True))

    def exp_part(m, top, total):
        keys = slice(256 * m, 256 * m + 256)
        x = jnp.exp(scores[keys, :] - top)
        scores[keys, :] = x
        return total + jnp.sum(x, axis=0, keepdims=True)

    def prob_part(m, share):
        keys = slice(256 * m, 256 * m + 256)
        x = scores[keys, :] * share
        scores[keys, :] = x
        probs_low[keys, :] = x.astype(BF16)

    state = {"top": jnp.full((1, STACK), MASKED, F32), "total": jnp.zeros((1, STACK), F32)}

    def piece(n):
        if n < 8:
            state["top"] = score_part(n, state["top"])
        elif n < 16:
            state["total"] = exp_part(n - 8, state["top"], state["total"])
        else:
            if n == 16:
                state["share"] = 1.0 / state["total"]
            prob_part(n - 16, state["share"])

    def pieces(first, last):
        for n in range(first, last):
            piece(n)

    def pieces(first, last):
        for n in range(first, last):
            piece(n)

    og_block(0, order[0])
    og_block(1, order[1])
    og_block(2, order[2])
    proj_next(3, 0)
    og_pass(0, order[0])
    og_pass(1, order[1])
    og_pass(2, order[2])
    kv_last(0)
    proj_next(3, 1)
    og_block(3, order[3])
    og_block(4, order[4])
    kv_last(1)
    og_block(5, order[5])
    og_pass(3, order[3])
    og_block(6, order[6])
    og_pass(4, order[4])
    wait_recv(kv.at[:, :, 1 - core], kvm_r)
    query_step()
    pieces(0, 4)
    og_pass(5, order[5])
    proj_next(4, 0)
    proj_next(4, 1)
    og_block(7, order[7])
    og_pass(6, order[6])
    pieces(4, 8)
    og_done(0, order[0])
    og_done(1, order[1])
    og_pass(7, order[7])
    og_done(2, order[2])
    pieces(8, 11)
    og_done(3, order[3])
    pieces(11, 14)
    og_done(4, order[4])
    pieces(14, 16)
    og_done(5, order[5])
    pieces(16, 18)
    og_done(6, order[6])
    og_done(7, order[7])
    pieces(18, 24)
    wait_recv(ogy_recv.at[pl.ds(0, 7)], ogy_r)
    out = ogy_recv[...].reshape(ROWS, STACK)
    out_grad = jnp.concatenate([out[:, 0:128], out[:, 128:256], out[:, 256:384]], axis=0)

    def group(j):
        return lax.rem(chip // 2 + (2, 1, 3, 0)[j], 4)

    def group_keys(j):
        return pl.ds(pl.multiple_of(group(j) * 512, 512), 512)

    def dkvm_copy(n, j):
        return remote(dkv_give.at[n, j], dkv_mate.at[n, j], dkvm_s, dkvm_r.at[n, j], vocab=mate)

    def share(n, j, part):
        part = part.reshape(2, 2, ROWS, HEAD)
        first, second = part[:, 0], part[:, 1]
        dkv_own[n, j] = jnp.where(core == 0, first, second)
        dkv_give[n, j] = jnp.where(core == 0, second, first).astype(BF16)
        dkvm_copy(n, j).start()

    def send_on(n, j):
        dkvm_copy(n, j).wait_recv()
        dkv_sum[n, j] = (dkv_own[n, j] + dkv_mate[n, j].astype(F32)).astype(BF16)
        for i in range(2):
            m = 2 * group(j) + i

            @pl.when(m != chip)
            def _():
                remote(
                    dkv_sum.at[n, j, i], dkv_recv.at[n, chip], dkv_s, dkv_r.at[n], vocab=2 * m + core
                ).start()

    def value_pass(j):
        share(1, j, jnp.dot(probs_low[group_keys(j), :], out_grad, preferred_element_type=F32))

    def key_pass(j):
        keys = group_keys(j)
        ds_low = (scores[keys, :] * (prob_grad[keys, :] - delta)).astype(BF16)
        score_grad[keys, :] = ds_low
        share(0, j, jnp.dot(ds_low, query_rows[...], preferred_element_type=F32) * SCALE)

    value_pass(0)
    value_pass(1)
    value_pass(2)
    send_on(1, 0)
    value_pass(3)
    send_on(1, 1)

    delta = jnp.zeros((1, STACK), F32)
    for m in range(4):
        keys = slice(512 * m, 512 * m + 512)
        x = dot_nt(kv[1, 2 * m : 2 * m + 2].reshape(512, HEAD), out_grad)
        prob_grad[keys, :] = x
        delta = delta + jnp.sum(probs_low[keys, :].astype(F32) * x, axis=0, keepdims=True)

    send_on(1, 2)
    send_on(1, 3)
    key_pass(0)
    key_pass(1)
    key_pass(2)
    send_on(0, 0)
    key_pass(3)
    send_on(0, 1)
    send_on(0, 2)

    dq = dot_tn(score_grad[...], kv[0].reshape(KEYS, HEAD)) * SCALE
    send_on(0, 3)
    t0, t1, t2 = [dq[128 * j : 128 * j + 128].reshape(16, 8, 128) for j in range(3)]
    t0 = jnp.concatenate([first_halves(t0, t1), t2, second_halves(t0, t1), turn(t2)], axis=1)
    dq_send[...] = t0.astype(BF16).reshape(dq_send.shape)

    for d in (4, 3, 5, 2, 6, 1, 7):
        remote(
            dq_send.at[y_peer(d)], dqy_recv.at[y], dqy_s, dqy_r, seq=h * 8 + y_peer(d)
        ).start()
    dqy_recv[y] = dq_send[y]

    for n in range(2):
        dkv_recv[n, chip] = dkv_sum[n, 3, lax.rem(chip, 2)]
    wait_recv(dkv_recv.at[1, pl.ds(0, 7)], dkv_r.at[1])
    values_sum = jnp.sum(dkv_recv[1].astype(F32), axis=0).reshape(16, 8, 128)
    wait_recv(dkv_recv.at[0, pl.ds(0, 7)], dkv_r.at[0])
    keys_sum = jnp.sum(dkv_recv[0].astype(F32), axis=0).reshape(16, 8, 128)
    parts = jnp.stack(
        [first_halves(keys_sum, values_sum), second_halves(keys_sum, values_sum)], axis=1
    )
    foldy_send[...] = parts.reshape(8, 32, 128).astype(BF16)
    for d in (4, 3, 5, 2, 6, 1, 7):
        remote(
            foldy_send.at[y_peer(d)], foldy_recv.at[y], foldy_s, foldy_r, seq=h * 8 + y_peer(d)
        ).start()
    foldy_recv[y] = foldy_send[y]

    wait_recv(dqy_recv.at[pl.ds(0, 7)], dqy_r)
    for d in (2, 1, 3):
        remote(
            dqy_recv.at[:, z_peer(d)], dq_recv.at[h], dq_s, dq_r, seq=z_peer(d) * 8 + y
        ).start()
    dq_recv[h] = dqy_recv[:, h]

    wait_send(stat_recv.at[pl.ds(0, VOC - 1)], stat_s)
    for i in range(2):
        mate_copy(i).wait_send()
    wait_send(part_recv.at[pl.ds(0, 7)], part_s)
    wait_send(og_mate, ogm_s)
    wait_send(og_recv.at[pl.ds(0, 7)], og_s)
    wait_send(ogy_recv.at[pl.ds(0, 7)], ogy_s)
    wait_send(kvz_recv.at[pl.ds(0, 3)], kvz_s)
    wait_send(kvy_recv.at[pl.ds(0, 7)], kvy_s)
    wait_send(queryy_recv.at[pl.ds(0, 7)], qy_s)
    wait_send(query_recv.at[pl.ds(0, 3)], q_s)
    wait_send(score_grad.at[pl.ds(0, 1280)], kv_s)
    wait_send(blocks.at[pl.ds(0, 3)], z_s)
    wait_send(projs.at[pl.ds(0, 7), 0:320], proj_s)
    wait_send(dkv_mate, dkvm_s)
    wait_send(dkv_recv.at[:, pl.ds(0, 7)], dkv_s)
    wait_send(dqy_recv.at[pl.ds(0, 7)], dqy_s)

    def dq_out():
        wait_recv(dq_recv.at[pl.ds(0, 3)], dq_r)
        for t in range(SEQ):
            x = dq_recv[t // 8, t % 8].astype(F32)
            for j in range(GROUP_HEADS):
                lane = (GROUP_HEADS * t + j) * HEAD
                query_out[:, lane : lane + HEAD] = x[4 * j : 4 * j + 4].astype(BF16)
        stores[2].start()

    wait_recv(foldy_recv.at[pl.ds(0, 7)], foldy_r)
    sums = []
    for i in range(2):
        head_sum = jnp.sum(foldy_recv[4 * i : 4 * i + 4].astype(F32), axis=0)
        sums.append(head_sum.reshape(4, 8, 128))
    foldz_send[...] = jnp.concatenate(sums, axis=1).astype(BF16)
    for d in (2, 1, 3):
        remote(
            foldz_send.at[z_peer(d)], foldz_recv.at[h], foldz_s, foldz_r, seq=z_peer(d) * 8 + y
        ).start()
    foldz_recv[h] = foldz_send[h]
    dq_out()
    wait_send(dq_recv.at[pl.ds(0, 3)], dq_s)
    wait_send(foldy_recv.at[pl.ds(0, 7)], foldy_s)
    wait_send(foldz_recv.at[pl.ds(0, 3)], foldz_s)
    wait_recv(foldz_recv.at[pl.ds(0, 3)], foldz_r)
    for k in range(8):
        x = foldz_recv[k // 2].astype(F32)[8 * (k % 2) : 8 * (k % 2) + 8]
        kv_out[0, :, k * HEAD : k * HEAD + HEAD] = x[0:4].astype(BF16)
        kv_out[1, :, k * HEAD : k * HEAD + HEAD] = x[4:8].astype(BF16)
    stores[3].start()
    for copy in stores:
        copy.wait()


def scratch():
    v = pltpu.VMEM
    dma = pltpu.SemaphoreType.DMA
    buffers = [
        v((TOK, D), BF16), v((1, D), F32), v((256, D), BF16), v((1, TOK), jnp.int32),
        v((4, 12288), BF16), v((2, 4, 1024), BF16),
        v((1, TOK), F32), v((TOK, 320), BF16), v((4, 12288), BF16), v((2, 4, 1024), BF16),
        v((256, 2 * TOK), BF16), v((2 * TOK, D), F32), v((8, 128), F32), v((VOC, 8, 128), F32),
        v((2, 8, 160, 128), BF16), v((8, 160, 128), BF16), v((8, 160, 128), BF16), v((8, 160, 128), BF16),
        v((4, 160, 128), BF16), v((256, 384), BF16), v((8, 384, STACK), BF16),
        v((8, 8, 16, STACK), F32), v((8, 8, 16, STACK), BF16), v((8, 8, 16, STACK), BF16),
        v((8, 8, 16, STACK), BF16), v((8, 8, 16, STACK), BF16),
        v((8, 16, STACK), BF16), v((8, 16, STACK), BF16),
        v((SEQ, 16, 128), F32), v((8, 4, 16, 128), BF16), v((8, 4, 16, 128), BF16), v((4, 8, 16, 128), BF16),
        v((STACK, 128), BF16),
        v((4, 16, 128), F32), v((4, 16, 128), BF16), v((4, 16, 128), BF16),
        v((2, 32, 128), BF16), v((8, 32, 128), BF16), v((2, 8, 2, ROWS, 128), BF16),
        v((KEYS, STACK), F32), v((KEYS, STACK), BF16), v((KEYS, STACK), F32), v((KEYS, STACK), BF16),
        v((8, 4, 16, 128), BF16), v((8, 4, 16, 128), BF16), v((4, 8, 16, 128), BF16),
        v((2, 4, 2, ROWS, 128), F32), v((2, 4, 2, ROWS, 128), BF16), v((2, 4, 2, ROWS, 128), BF16),
        v((2, 4, 2, ROWS, 128), BF16), v((2, 8, ROWS, 128), BF16),
        v((8, 32, 128), BF16), v((8, 32, 128), BF16), v((4, 16, 128), BF16), v((4, 16, 128), BF16),
    ]
    sizes = [
        (8,), (4,), None, None, (2,), (2,), None, (2,), None, (2, 4), None, (2, 4, 2),
        None, (8,), None, (8,), None, None, None, None, None, None, None, None, None, None,
        None, None, (2, 2), (2, 2), None,
        None, None, None, None, None, (2, 4), None, (2,), None, None, None, None,
    ]
    return buffers + [dma if n is None else dma(n) for n in sizes]


def store(*refs):
    sems = refs[12]
    ins = [pltpu.make_async_copy(refs[i], refs[8 + i], sems.at[i]) for i in range(4)]
    outs = [pltpu.make_async_copy(refs[8 + i], refs[4 + i], sems.at[4 + i]) for i in range(4)]
    for copy in ins:
        copy.start()
    for first, second in zip(ins, outs):
        first.wait()
        second.start()
    for copy in outs:
        copy.wait()


def shards(hidden, norm_gain, head_weight, targets, out_proj, query, saved_key_value, offset):
    hbm = pl.BlockSpec(memory_space=pltpu.HBM)
    outs = (
        jax.ShapeDtypeStruct((1, TOK), F32),
        jax.ShapeDtypeStruct((TOK, 320), BF16),
        jax.ShapeDtypeStruct(query.shape, BF16),
        jax.ShapeDtypeStruct(saved_key_value.shape, BF16),
    )
    results = pl.pallas_call(
        body,
        out_shape=outs,
        in_specs=[hbm] * 7 + [pl.BlockSpec(memory_space=pltpu.SMEM)],
        out_specs=(hbm,) * 4,
        scratch_shapes=scratch(),
        compiler_params=pltpu.CompilerParams(
            collective_id=0, has_side_effects=True, vmem_limit_bytes=VMEM_BYTES
        ),
    )(
        hidden, norm_gain.reshape(1, D), head_weight, targets.reshape(1, TOK), out_proj.T, query,
        saved_key_value, offset,
    )
    loss, hidden_grad, query_grad, kv_grad = pl.pallas_call(
        store,
        out_shape=outs,
        in_specs=[hbm] * 4,
        out_specs=(hbm,) * 4,
        scratch_shapes=[pltpu.VMEM(x.shape, x.dtype) for x in outs] + [pltpu.SemaphoreType.DMA((8,))],
        compiler_params=pltpu.CompilerParams(vmem_limit_bytes=VMEM_BYTES),
    )(*results)
    return loss.reshape(TOK), hidden_grad, query_grad, kv_grad


def solution(mesh):
    in_specs = (
        P("seq", None),
        P(),
        P("vocab", None),
        P("seq"),
        P("seq", "vocab"),
        P(("seq", "vocab"), None),
        P(None, ("seq", "vocab"), None),
        P(),
    )
    out_specs = (
        P("seq"),
        P("seq", "vocab"),
        P(("seq", "vocab"), None),
        P(None, ("seq", "vocab"), None),
    )
    return jax.shard_map(shards, mesh=mesh, in_specs=in_specs, out_specs=out_specs, check_vma=False)
```
